512 devices in a mesh: elec: 16 (over x, y_hi), tm: 32 (over y_lo, z, core).
Axes of the slice: x: 4, y: 8 (y_hi: 4, y_lo: 2; y = y_hi * 2 + y_lo), z: 8, core: 2. Of those that a mesh axis runs over, the one named last changes fastest.
Arguments:
- signals: bfloat16 [4096, 12288], P('elec', 'tm'), may hold values from -6 to 6
- vectors: bfloat16 [128, 65536], P(None, 'elec'), may hold values from -0.0234375 to 0.0234375
Outputs:
- sources: bfloat16 [128, 12288], P(None, 'tm')
- unmixing: float32 [128, 65536], P(None, ('elec', 'tm'))
The draws below stay inside these ranges and needn't reach their ends.
All inputs are finite; a program needn't handle non-finite values.
Results may differ from the reference program's by a relative error of at most 0.004.
Values may be sent and summed in bfloat16 or wider, within the bound.
A program may use at most 64 MiB of HBM per device.

```python
import math
import jax
import jax.numpy as jnp
from jax import lax

ELECTRODES = 4096
LAGS = 16
VECTORS = 128
NS_STEPS = 6
EXT = 65536
SAMPLES = 12288


def steps_of(own_key, dims, shards, low, top_value):
    loudness = 1.0
    for dim, blocks in shards:
        steps = jax.random.uniform(jax.random.fold_in(jax.random.fold_in(own_key, 6), dim), (blocks,), jnp.float32, low / len(shards), top_value / len(shards))
        loudness = loudness * jnp.repeat(jnp.exp(steps), dims[dim] // blocks).reshape((-1,) + (1,) * (len(dims) - 1 - dim))
    return loudness


def bell_draw(rng, extent, scale, limit, cuts=(), kind=jnp.bfloat16):
    level = steps_of(rng, extent, cuts, -0.22, 0.18) if cuts else 1.0
    entries = jax.random.normal(rng, extent, jnp.float32) * scale * level
    return jnp.minimum(jnp.maximum(entries, -limit), limit).astype(kind)


def setup_inputs(seed: int = 0) -> dict:
    streams_of = jax.random.split(jax.random.key(seed), 3)
    signals = bell_draw(streams_of[0], (ELECTRODES, SAMPLES), 1.0, 6.0, ((0, 16), (1, 32)))
    vectors = bell_draw(streams_of[1], (VECTORS, EXT), EXT ** -0.5, 0.0234375, ((1, 16),))
    return dict(signals=signals, vectors=vectors)


START = 0.15

def reference(signals, vectors):
    padded = jnp.pad(signals, ((0, 0), (LAGS - 1, 0)))
    weights = vectors.reshape(VECTORS, ELECTRODES, LAGS)
    source_sums = jnp.zeros((VECTORS, SAMPLES), jnp.float32)
    for offset in range(LAGS):
        window = lax.slice_in_dim(padded, LAGS - 1 - offset, LAGS - 1 - offset + SAMPLES, axis=1)
        source_sums = source_sums + jnp.dot(weights[:, :, offset], window, preferred_element_type=jnp.float32)
    cubed = (source_sums * source_sums * source_sums).astype(jnp.bfloat16)
    deriv_mean = lax.optimization_barrier(jnp.sum(3.0 * source_sums * source_sums, axis=1)) / SAMPLES
    pieces = []
    for offset in range(LAGS):
        window = lax.slice_in_dim(padded, LAGS - 1 - offset, LAGS - 1 - offset + SAMPLES, axis=1)
        pieces.append(lax.dot_general(cubed, window, (((1,), (1,)), ((), ())), preferred_element_type=jnp.float32))
    gradient = jnp.stack(pieces, axis=2).reshape(VECTORS, EXT)
    updated = gradient / SAMPLES - deriv_mean[:, None] * vectors.astype(jnp.float32)
    squares = jnp.sum(updated * updated)
    current = updated * (START * math.sqrt(VECTORS) * lax.rsqrt(squares + 1e-06))
    for iteration in range(NS_STEPS):
        gram = lax.dot_general(current, current, (((1,), (1,)), ((), ())), precision=lax.Precision.HIGHEST, preferred_element_type=jnp.float32)
        current = 1.5 * current - 0.5 * jnp.dot(gram, current, precision=lax.Precision.HIGHEST)
    return (source_sums.astype(jnp.bfloat16), current)
```

```python
import functools
import itertools
import math

import jax
import jax.numpy as jnp
from jax import lax
from jax.experimental import pallas as pl
from jax.experimental.pallas import tpu as pltpu
from jax.sharding import PartitionSpec as P

LAGS = 16
NS_STEPS = 6
START = 0.15
MESH = pl.DeviceIdType.MESH
SIZE = dict(x=4, h=4, l=2, z=8, c=2)
F32, BF16 = jnp.float32, jnp.bfloat16
LANES = 128


def hops(move):
    x, y, z = move.get("x", 0), 2 * move.get("h", 0) + move.get("l", 0), move.get("z", 0)
    return min(x, 4 - x) + min(y, 8 - y) + min(z, 8 - z)


def moves(*names):
    every = itertools.product(*[range(SIZE[name]) for name in names])
    found = [dict(zip(names, move)) for move in every if any(move)]
    return sorted(found, key=lambda move: -hops(move))


ELEC, PART, RING = moves("x", "h"), moves("l", "c"), moves("z")


def place():
    elec, tm = lax.axis_index("elec"), lax.axis_index("tm")
    return dict(x=elec // 4, h=elec % 4, l=tm // 16, z=(tm // 2) % 8, c=tm % 2)


def moved(at, move):
    return {k: lax.rem(v + move.get(k, 0), SIZE[k]) for k, v in at.items()}


def elec_of(at):
    return at["x"] * 4 + at["h"]


def tm_of(at):
    return (at["l"] * 8 + at["z"]) * 2 + at["c"]


def part_of(at):
    return at["l"] * 2 + at["c"]


def device(at):
    return {"elec": elec_of(at), "tm": tm_of(at)}


def send(src, dst, sems, slot, at):
    copy = pltpu.make_async_remote_copy(
        src_ref=src,
        dst_ref=dst,
        send_sem=sems[0].at[slot],
        recv_sem=sems[1].at[slot],
        device_id=device(at),
        device_id_type=MESH,
    )
    copy.start()
    return copy


def halves(a):
    top = a.astype(BF16)
    return top, (a - top.astype(F32)).astype(BF16)


def dot(a, b, dims=(((1,), (0,)), ((), ()))):
    return lax.dot_general(a, b, dims, preferred_element_type=F32)


def fine_dot(a, b):
    (a1, a2), (b1, b2) = halves(a), halves(b)
    return dot(jnp.concatenate([a1, a1, a2], 1), jnp.concatenate([b1, b2, b1], 0))


def fine_gram(a):
    a1, a2 = halves(a)
    both = (((1,), (1,)), ((), ()))
    return dot(jnp.concatenate([a1, a1, a2], 1), jnp.concatenate([a1, a2, a1], 1), both)


def lagged(rows):
    turned = [
        pltpu.roll(jnp.broadcast_to(row, (LAGS, LANES)), 0, 1, stride=1, stride_axis=0) for row in rows
    ]
    lane = lax.broadcasted_iota(jnp.int32, (LAGS, LANES), 1)
    late = lax.broadcasted_iota(jnp.int32, (LAGS, LANES), 0)
    return [jnp.where(lane < late, a, b) for a, b in zip(turned, turned[1:])]


def kernel(
    sig, vec, sources, unmixing,
    tail, padded, ext, far_out, far_in, feat, partial, summed, sums, cubes, deriv_out, deriv_in,
    grad_out, grad_in, gram, gram_part, gram_ring, gram_ring_in, gram_elec, gram_elec_in, gram_all,
    tail_s, tail_r, far_s, far_r, rs_s, rs_r, ag_s, ag_r, cube_s, cube_r, deriv_s, deriv_r,
    grad_s, grad_r, g1_s, g1_r, g2_s, g2_r, g3_s, g3_r, g4_s, g4_r,
):
    at = place()
    elec, tm = elec_of(at), tm_of(at)
    length = sig.shape[1]
    tiles = length // LANES
    after, before = lax.rem(tm + 1, 32), lax.rem(tm + 31, 32)

    barrier = pltpu.get_barrier_semaphore()
    for move in ELEC + PART + RING:
        pl.semaphore_signal(barrier, inc=1, device_id=device(moved(at, move)), device_id_type=MESH)
    for other in (after, before):
        pl.semaphore_signal(barrier, inc=1, device_id={"elec": elec, "tm": other}, device_id_type=MESH)
    pl.semaphore_wait(barrier, len(ELEC) + len(PART) + len(RING) + 2)

    tail_copy = pltpu.make_async_remote_copy(
        src_ref=sig.at[:, pl.ds(length - LANES, LANES)],
        dst_ref=tail,
        send_sem=tail_s.at[0],
        recv_sem=tail_r.at[0],
        device_id={"elec": elec, "tm": after},
        device_id_type=MESH,
    )
    tail_copy.start()
    padded[:, LANES:] = sig[...].astype(F32)

    @pl.loop(0, 32)
    def _(block):
        rows = padded[pl.ds(block * 8, 8), LANES:]
        for r in range(8):
            pieces = lagged([rows[r : r + 1, k * LANES : (k + 1) * LANES] for k in range(tiles)])
            for k, piece in enumerate(pieces):
                ext[pl.ds((block * 8 + r) * LAGS, LAGS), (k + 1) * LANES : (k + 2) * LANES] = piece.astype(BF16)

    partial[:, LANES:] = dot(vec[...], ext[:, LANES:])

    tail_copy.wait()
    first = jnp.where(tm > 0, 1.0, 0.0)
    padded[:, :LANES] = tail[...].astype(F32) * first

    @pl.loop(0, 32)
    def _(block):
        rows = padded[pl.ds(block * 8, 8), : 2 * LANES]
        for r in range(8):
            (piece,) = lagged([rows[r : r + 1, :LANES], rows[r : r + 1, LANES:]])
            ext[pl.ds((block * 8 + r) * LAGS, LAGS), :LANES] = piece.astype(BF16)

    far_copies = []
    for i, move in enumerate(PART):
        to = moved(at, move)
        blocks = [pl.multiple_of((to["l"] * 16 + z * 2 + to["c"]) * 8, 8) for z in range(8)]
        far_out[i] = jnp.concatenate([padded[pl.ds(block, 8), :] for block in blocks], 0).astype(BF16)
        far_copies.append(send(far_out.at[i], far_in.at[i], (far_s, far_r), i, to))

    partial[:, :LANES] = dot(vec[...], ext[:, :LANES])

    rs_copies = []
    for i, move in enumerate(ELEC):
        to = moved(at, move)
        rows = pl.ds(pl.multiple_of(elec_of(to) * 8, 8), 8)
        rs_copies.append(send(partial.at[rows], summed.at[i], (rs_s, rs_r), i, to))

    for z in range(8):
        own = pl.multiple_of((at["l"] * 16 + z * 2 + at["c"]) * LANES, LANES)
        feat[z * LANES : (z + 1) * LANES, :length] = ext[pl.ds(own, LANES), :]
    for i, copy in enumerate(far_copies):
        copy.wait()

        @pl.loop(0, 4)
        def _(block):
            rows = far_in[i, pl.ds(block * 16, 16), :].astype(F32)
            for r in range(16):
                pieces = lagged([rows[r : r + 1, k * LANES : (k + 1) * LANES] for k in range(tiles + 1)])
                for k, piece in enumerate(pieces):
                    begin = (i + 1) * length + k * LANES
                    feat[pl.ds((block * 16 + r) * LAGS, LAGS), begin : begin + LANES] = piece.astype(BF16)

    mine = pl.ds(pl.multiple_of(elec * 8, 8), 8)
    total = partial[mine, :]
    for i, copy in enumerate(rs_copies):
        copy.wait()
        total = total + summed[i]
    sums[mine, :] = total
    ag_copies = [
        send(sums.at[mine], sums.at[mine], (ag_s, ag_r), i, moved(at, move)) for i, move in enumerate(ELEC)
    ]
    for copy in ag_copies:
        copy.wait()

    s = sums[...]
    sources[...] = s.astype(BF16)
    cubes[0] = (s * s * s).astype(BF16)
    square = 3.0 * s * s
    deriv = jnp.sum(square, axis=1, keepdims=True)
    deriv_out[...] = jnp.transpose(jnp.broadcast_to(deriv, (LANES, LANES)))[:8]
    cube_copies, deriv_copies = [], []
    for i, move in enumerate(PART):
        to = moved(at, move)
        cube_copies.append(send(cubes.at[0], cubes.at[i + 1], (cube_s, cube_r), i, to))
        deriv_copies.append(send(deriv_out, deriv_in.at[i], (deriv_s, deriv_r), i, to))
    for copy in cube_copies + deriv_copies:
        copy.wait()
    deriv_row = deriv_out[...]
    for i in range(len(PART)):
        deriv_row = deriv_row + deriv_in[i]
    deriv = jnp.transpose(jnp.broadcast_to(deriv_row[:1], (LANES, LANES)))

    cubed = jnp.concatenate([cubes[i] for i in range(len(PART) + 1)], 1)

    def block_of(z):
        rows = pl.ds(pl.multiple_of(z * LANES, LANES), LANES)
        columns = pl.ds(pl.multiple_of((at["l"] * 16 + z * 2 + at["c"]) * LANES, LANES), LANES)
        grad = dot(cubed, feat[rows, :], (((1,), (1,)), ((), ())))
        return grad - deriv * vec[:, columns].astype(F32)

    grad_copies = []
    for i, move in enumerate(RING):
        to = moved(at, move)
        grad_out[i] = block_of(to["z"]).astype(BF16)
        grad_copies.append(send(grad_out.at[i], grad_in.at[i], (grad_s, grad_r), i, to))
    updated = block_of(at["z"])
    for i, copy in enumerate(grad_copies):
        copy.wait()
        updated = updated + grad_in[i].astype(F32)
    updated = updated * (1.0 / (length * 32))

    gram[...] = fine_gram(updated)
    part = part_of(at)
    quarter = pl.ds(pl.multiple_of(part * 32, 32), 32)
    copies = []
    for i, move in enumerate(PART):
        to = moved(at, move)
        rows = pl.ds(pl.multiple_of(part_of(to) * 32, 32), 32)
        copies.append(send(gram.at[rows], gram_part.at[i], (g1_s, g1_r), i, to))
    total = gram[quarter, :]
    for i, copy in enumerate(copies):
        copy.wait()
        total = total + gram_part[i]
    gram_ring[...] = total.astype(BF16)
    copies = [
        send(gram_ring, gram_ring_in.at[i], (g2_s, g2_r), i, moved(at, move)) for i, move in enumerate(RING)
    ]
    total = gram_ring[...].astype(F32)
    for i, copy in enumerate(copies):
        copy.wait()
        total = total + gram_ring_in[i].astype(F32)
    gram_elec[...] = total.astype(BF16)
    copies = [
        send(gram_elec, gram_elec_in.at[i], (g3_s, g3_r), i, moved(at, move)) for i, move in enumerate(ELEC)
    ]
    total = gram_elec[...].astype(F32)
    for i, copy in enumerate(copies):
        copy.wait()
        total = total + gram_elec_in[i].astype(F32)
    gram_all[quarter, :] = total
    copies = [
        send(gram_all.at[quarter], gram_all.at[quarter], (g4_s, g4_r), i, moved(at, move))
        for i, move in enumerate(PART)
    ]
    for copy in copies:
        copy.wait()

    g = gram_all[...]
    row = lax.broadcasted_iota(jnp.int32, (LANES, LANES), 0)
    column = lax.broadcasted_iota(jnp.int32, (LANES, LANES), 1)
    unit = jnp.where(row == column, 1.0, 0.0)
    squares = jnp.sum(jnp.sum(g * unit, axis=1, keepdims=True), axis=0, keepdims=True)
    scale = START * math.sqrt(LANES) * lax.rsqrt(squares + 1e-06)
    g = g * scale * scale
    product = None
    for step in range(NS_STEPS):
        factor = 1.5 * unit - 0.5 * g
        product = factor if product is None else fine_dot(factor, product)
        if step < NS_STEPS - 1:
            g = fine_dot(fine_dot(factor, g), factor)
    unmixing[...] = fine_dot(product, updated * scale)


def sem_pairs(*counts):
    return [pltpu.SemaphoreType.DMA((count,)) for count in counts for _ in range(2)]


def shards(signals, vectors):
    channels, length = signals.shape
    count, columns = vectors.shape
    near, ring, part = len(ELEC), len(RING), len(PART)
    vmem = pl.BlockSpec(memory_space=pltpu.VMEM)
    return pl.pallas_call(
        kernel,
        out_shape=(
            jax.ShapeDtypeStruct((count, length), BF16),
            jax.ShapeDtypeStruct((count, LANES), F32),
        ),
        in_specs=[vmem, vmem],
        out_specs=(vmem, vmem),
        scratch_shapes=[
            pltpu.VMEM((channels, LANES), BF16),
            pltpu.VMEM((channels, LANES + length), F32),
            pltpu.VMEM((columns, length), BF16),
            pltpu.VMEM((part, 64, LANES + length), BF16),
            pltpu.VMEM((part, 64, LANES + length), BF16),
            pltpu.VMEM((8 * LANES, (part + 1) * length), BF16),
            pltpu.VMEM((count, length), F32),
            pltpu.VMEM((near, 8, length), F32),
            pltpu.VMEM((count, length), F32),
            pltpu.VMEM((part + 1, count, length), BF16),
            pltpu.VMEM((8, LANES), F32),
            pltpu.VMEM((part, 8, LANES), F32),
            pltpu.VMEM((ring, count, LANES), BF16),
            pltpu.VMEM((ring, count, LANES), BF16),
            pltpu.VMEM((LANES, LANES), F32),
            pltpu.VMEM((part, 32, LANES), F32),
            pltpu.VMEM((32, LANES), BF16),
            pltpu.VMEM((ring, 32, LANES), BF16),
            pltpu.VMEM((32, LANES), BF16),
            pltpu.VMEM((near, 32, LANES), BF16),
            pltpu.VMEM((LANES, LANES), F32),
            *sem_pairs(1, part, near, near, part, part, ring, part, ring, near, part),
        ],
        compiler_params=pltpu.CompilerParams(
            collective_id=0, has_side_effects=True, vmem_limit_bytes=40 * 2**20
        ),
        cost_estimate=pl.CostEstimate(flops=10**9, bytes_accessed=2 * 10**6, transcendentals=0),
        name="separate",
    )(signals, vectors)


def solution(mesh):
    return jax.shard_map(
        shards,
        mesh=mesh,
        in_specs=(P("elec", "tm"), P(None, "elec")),
        out_specs=(P(None, "tm"), P(None, ("elec", "tm"))),
        check_vma=False,
    )
```

```python
import functools
import itertools
import math

import jax
import jax.numpy as jnp
from jax import lax
from jax.experimental import pallas as pl
from jax.experimental.pallas import tpu as pltpu
from jax.sharding import PartitionSpec as P

LAGS = 16
NS_STEPS = 6
START = 0.15
MESH = pl.DeviceIdType.MESH
SIZE = dict(x=4, h=4, l=2, z=8, c=2)
F32, BF16 = jnp.float32, jnp.bfloat16
LANES = 128


def hops(move):
    x, y, z = move.get("x", 0), 2 * move.get("h", 0) + move.get("l", 0), move.get("z", 0)
    return min(x, 4 - x) + min(y, 8 - y) + min(z, 8 - z)


def moves(*names):
    every = itertools.product(*[range(SIZE[name]) for name in names])
    found = [dict(zip(names, move)) for move in every if any(move)]
    return sorted(found, key=lambda move: -hops(move))


ELEC, PLANE, RING = moves("x", "h"), moves("x", "h", "l"), moves("z")
PART = [dict(l=1), dict(c=1), dict(l=1, c=1)]


def place():
    elec, tm = lax.axis_index("elec"), lax.axis_index("tm")
    return dict(x=elec // 4, h=elec % 4, l=tm // 16, z=(tm // 2) % 8, c=tm % 2)


def moved(at, move):
    return {k: lax.rem(v + move.get(k, 0), SIZE[k]) for k, v in at.items()}


def elec_of(at):
    return at["x"] * 4 + at["h"]


def tm_of(at):
    return (at["l"] * 8 + at["z"]) * 2 + at["c"]


def part_of(at):
    return at["l"] * 2 + at["c"]


def device(at):
    return {"elec": elec_of(at), "tm": tm_of(at)}


def send(src, dst, sems, slot, at):
    copy = pltpu.make_async_remote_copy(
        src_ref=src,
        dst_ref=dst,
        send_sem=sems[0].at[slot],
        recv_sem=sems[1].at[slot],
        device_id=device(at),
        device_id_type=MESH,
    )
    copy.start()
    return copy


def halves(a):
    top = a.astype(BF16)
    return top, (a - top.astype(F32)).astype(BF16)


def dot(a, b, dims=(((1,), (0,)), ((), ()))):
    return lax.dot_general(a, b, dims, preferred_element_type=F32)


def fine_dot(a, b):
    (a1, a2), (b1, b2) = halves(a), halves(b)
    return dot(jnp.concatenate([a1, a1, a2], 1), jnp.concatenate([b1, b2, b1], 0))


def fine_gram(a):
    a1, a2 = halves(a)
    both = (((1,), (1,)), ((), ()))
    return dot(jnp.concatenate([a1, a1, a2], 1), jnp.concatenate([a1, a2, a1], 1), both)


def lagged(row):
    return pltpu.roll(jnp.broadcast_to(row, (LAGS, LANES)), 0, 1, stride=1, stride_axis=0)


def kernel(
    sig_hbm, vec_hbm, sources, unmixing,
    sig, vec, tail, padded, ext, far_out, far_in, feat, partial, summed, blocks, waves, cubes,
    grad_out, grad_in, gram, gram_part, gram_ring, gram_ring_in, gram_elec, gram_elec_in, gram_all,
    load, tail_s, tail_r, far_s, far_r, rs1_s, rs1_r, rs2_s, rs2_r, cube_s, cube_r, core_s, core_r, wave_s, wave_r,
    grad_s, grad_r, g1_s, g1_r, g2_s, g2_r, g3_s, g3_r, g4_s, g4_r,
):
    at = place()
    elec, tm = elec_of(at), tm_of(at)
    length = sig.shape[1]
    tiles = length // LANES
    after, before = lax.rem(tm + 1, 32), lax.rem(tm + 31, 32)

    loads = [
        pltpu.make_async_copy(sig_hbm, sig, load.at[0]),
        pltpu.make_async_copy(vec_hbm, vec, load.at[1]),
    ]
    for copy in loads:
        copy.start()
    barrier = pltpu.get_barrier_semaphore()
    for other in (after, before):
        pl.semaphore_signal(barrier, inc=1, device_id={"elec": elec, "tm": other}, device_id_type=MESH)
    greeted = PLANE + RING + PART[1:]
    for move in greeted:
        pl.semaphore_signal(barrier, inc=1, device_id=device(moved(at, move)), device_id_type=MESH)

    lane = lax.broadcasted_iota(jnp.int32, (LAGS, LANES), 1)
    late = lax.broadcasted_iota(jnp.int32, (LAGS, LANES), 0)
    spill = lane < late

    loads[0].wait()
    padded[:, LANES:] = sig[...].astype(F32)

    @pl.loop(0, 16)
    def _(block):
        rows = padded[pl.ds(block * 16, 16), LANES:]
        for r in range(16):
            to = pl.ds((block * 16 + r) * LAGS, LAGS)
            turned = [lagged(rows[r : r + 1, k * LANES : (k + 1) * LANES]) for k in range(tiles)]
            ext[to, :LANES] = turned[0].astype(BF16)
            for k in range(1, tiles):
                ext[to, k * LANES : (k + 1) * LANES] = jnp.where(spill, turned[k - 1], turned[k]).astype(BF16)

    pl.semaphore_wait(barrier, len(greeted) + 2)
    tail_copy = pltpu.make_async_remote_copy(
        src_ref=sig.at[:, pl.ds(length - LANES, LANES)],
        dst_ref=tail,
        send_sem=tail_s.at[0],
        recv_sem=tail_r.at[0],
        device_id={"elec": elec, "tm": after},
        device_id_type=MESH,
    )
    tail_copy.start()
    loads[1].wait()
    partial[:, LANES:] = dot(vec[...], ext[:, LANES:])
    rs_copies = []
    for i, move in enumerate(ELEC):
        to = moved(at, move)
        rows = pl.ds(pl.multiple_of(elec_of(to) * 8, 8), 8)
        rs_copies.append(
            send(partial.at[rows, pl.ds(LANES, length - LANES)], summed.at[i, :, pl.ds(LANES, length - LANES)], (rs1_s, rs1_r), i, to)
        )

    tail_copy.wait()
    first = jnp.where(tm > 0, 1.0, 0.0)
    padded[:, :LANES] = tail[...].astype(F32) * first

    @pl.loop(0, 8)
    def _(block):
        rows = padded[pl.ds(block * 32, 32), :LANES]
        for r in range(32):
            to = pl.ds((block * 32 + r) * LAGS, LAGS)
            ext[to, :LANES] = jnp.where(spill, lagged(rows[r : r + 1]), ext[to, :LANES].astype(F32)).astype(BF16)

    partial[:, :LANES] = dot(vec[...], ext[:, :LANES])
    for i, move in enumerate(ELEC):
        to = moved(at, move)
        rows = pl.ds(pl.multiple_of(elec_of(to) * 8, 8), 8)
        rs_copies.append(
            send(partial.at[rows, pl.ds(0, LANES)], summed.at[i, :, pl.ds(0, LANES)], (rs2_s, rs2_r), i, to)
        )

    far_copies = []
    for i, move in enumerate(PART):
        to = moved(at, move)
        starts = [pl.multiple_of((to["l"] * 16 + z * 2 + to["c"]) * 8, 8) for z in range(8)]
        far_out[i] = jnp.concatenate([padded[pl.ds(start, 8), :] for start in starts], 0).astype(BF16)
        far_copies.append(send(far_out.at[i], far_in.at[i], (far_s, far_r), i, to))
    for z in range(8):
        own = pl.multiple_of((at["l"] * 16 + z * 2 + at["c"]) * LANES, LANES)
        feat[z * LANES : (z + 1) * LANES, :length] = ext[pl.ds(own, LANES), :]

    mine = pl.ds(pl.multiple_of(elec * 8, 8), 8)
    total = partial[mine, :]
    for copy in rs_copies:
        copy.wait()
    for i in range(len(ELEC)):
        total = total + summed[i]

    def stacked(block, last):
        return jnp.concatenate([block[:, k * LANES : (k + 1) * LANES] for k in range(tiles)] + [last], 0).astype(BF16)

    deriv = jnp.sum(3.0 * total * total, axis=1, keepdims=True)
    high = deriv.astype(BF16).astype(F32)
    middle = (deriv - high).astype(BF16).astype(F32)
    low = deriv - high - middle
    lane = lax.broadcasted_iota(jnp.int32, (8, LANES), 1)
    pad = jnp.where(lane == 0, high, jnp.where(lane == 1, middle, jnp.where(lane == 2, low, 0.0)))
    blocks[0, elec] = stacked(total * total * total, pad)
    waves[elec] = stacked(total, jnp.zeros((8, LANES), F32))
    cube_copies = []
    for i, move in enumerate(PLANE):
        cube_copies.append(
            send(blocks.at[0, elec], blocks.at[move["l"], elec], (cube_s, cube_r), i, moved(at, move))
        )
    wave_copies = [
        send(waves.at[elec], waves.at[elec], (wave_s, wave_r), i, moved(at, move)) for i, move in enumerate(ELEC)
    ]

    for i, copy in enumerate(far_copies):
        copy.wait()

        @pl.loop(0, 4)
        def _(block):
            rows = far_in[i, pl.ds(block * 16, 16), :].astype(F32)
            for r in range(16):
                to = pl.ds((block * 16 + r) * LAGS, LAGS)
                turned = [lagged(rows[r : r + 1, k * LANES : (k + 1) * LANES]) for k in range(tiles + 1)]
                for k in range(tiles):
                    begin = (i + 1) * length + k * LANES
                    feat[to, begin : begin + LANES] = jnp.where(spill, turned[k], turned[k + 1]).astype(BF16)

    for copy in cube_copies:
        copy.wait()
    core_copy = send(blocks.at[pl.ds(0, 2)], blocks.at[pl.ds(2, 2)], (core_s, core_r), 0, moved(at, PART[1]))

    def unpack(shard):
        pads = []
        for pair in range(8):
            pieces = [blocks[shard, 2 * pair + k].astype(F32) for k in range(2)]
            for k in range(tiles):
                rows = jnp.concatenate([piece[8 * k : 8 * k + 8] for piece in pieces], 0)
                begin = shard * length + k * LANES
                cubes[16 * pair : 16 * pair + 16, begin : begin + LANES] = rows.astype(BF16)
            pads += [piece[8 * tiles :] for piece in pieces]
        return jnp.concatenate(pads, 0)

    pads = unpack(0) + unpack(1)
    core_copy.wait()
    pads = pads + unpack(2) + unpack(3)
    deriv = jnp.sum(pads, axis=1, keepdims=True)

    def block_of(z):
        rows = pl.ds(pl.multiple_of(z * LANES, LANES), LANES)
        columns = pl.ds(pl.multiple_of((at["l"] * 16 + z * 2 + at["c"]) * LANES, LANES), LANES)
        grad = dot(cubes[...], feat[rows, :], (((1,), (1,)), ((), ())))
        return grad - deriv * vec[:, columns].astype(F32)

    grad_copies = []
    for i, move in enumerate(RING):
        to = moved(at, move)
        grad_out[i] = block_of(to["z"]).astype(BF16)
        grad_copies.append(send(grad_out.at[i], grad_in.at[i], (grad_s, grad_r), i, to))
    updated = block_of(at["z"])
    for copy in wave_copies:
        copy.wait()
    for pair in range(8):
        pieces = [waves[2 * pair + k].astype(F32) for k in range(2)]
        for k in range(tiles):
            rows = jnp.concatenate([piece[8 * k : 8 * k + 8] for piece in pieces], 0)
            sources[16 * pair : 16 * pair + 16, k * LANES : (k + 1) * LANES] = rows.astype(BF16)
    for i, copy in enumerate(grad_copies):
        copy.wait()
        updated = updated + grad_in[i].astype(F32)
    updated = updated * (1.0 / (length * 32))

    gram[...] = fine_gram(updated)
    part = part_of(at)
    quarter = pl.ds(pl.multiple_of(part * 32, 32), 32)
    copies = []
    for i, move in enumerate(PART):
        to = moved(at, move)
        rows = pl.ds(pl.multiple_of(part_of(to) * 32, 32), 32)
        copies.append(send(gram.at[rows], gram_part.at[i], (g1_s, g1_r), i, to))
    total = gram[quarter, :]
    for i, copy in enumerate(copies):
        copy.wait()
        total = total + gram_part[i]
    gram_ring[...] = total.astype(BF16)
    copies = [
        send(gram_ring, gram_ring_in.at[i], (g2_s, g2_r), i, moved(at, move)) for i, move in enumerate(RING)
    ]
    total = gram_ring[...].astype(F32)
    for i, copy in enumerate(copies):
        copy.wait()
        total = total + gram_ring_in[i].astype(F32)
    gram_elec[...] = total.astype(BF16)
    copies = [
        send(gram_elec, gram_elec_in.at[i], (g3_s, g3_r), i, moved(at, move)) for i, move in enumerate(ELEC)
    ]
    total = gram_elec[...].astype(F32)
    for i, copy in enumerate(copies):
        copy.wait()
        total = total + gram_elec_in[i].astype(F32)
    gram_all[quarter, :] = total
    copies = [
        send(gram_all.at[quarter], gram_all.at[quarter], (g4_s, g4_r), i, moved(at, move))
        for i, move in enumerate(PART)
    ]
    for copy in copies:
        copy.wait()

    g = gram_all[...]
    row = lax.broadcasted_iota(jnp.int32, (LANES, LANES), 0)
    column = lax.broadcasted_iota(jnp.int32, (LANES, LANES), 1)
    unit = jnp.where(row == column, 1.0, 0.0)
    squares = jnp.sum(jnp.sum(g * unit, axis=1, keepdims=True), axis=0, keepdims=True)
    scale = START * math.sqrt(LANES) * lax.rsqrt(squares + 1e-06)
    g = g * scale * scale
    product = None
    for step in range(NS_STEPS):
        factor = 1.5 * unit - 0.5 * g
        product = factor if product is None else fine_dot(factor, product)
        if step < NS_STEPS - 1:
            g = fine_dot(fine_dot(factor, g), factor)
    unmixing[...] = fine_dot(product, updated * scale)


def sem_pairs(*counts):
    return [pltpu.SemaphoreType.DMA((count,)) for count in counts for _ in range(2)]


def shards(signals, vectors):
    channels, length = signals.shape
    count, columns = vectors.shape
    near, plane, ring, part = len(ELEC), len(PLANE), len(RING), len(PART)
    vmem = pl.BlockSpec(memory_space=pltpu.VMEM)
    return pl.pallas_call(
        kernel,
        out_shape=(
            jax.ShapeDtypeStruct((count, length), BF16),
            jax.ShapeDtypeStruct((count, LANES), F32),
        ),
        in_specs=[pl.BlockSpec(memory_space=pltpu.HBM)] * 2,
        out_specs=(vmem, vmem),
        scratch_shapes=[
            pltpu.VMEM((channels, length), BF16),
            pltpu.VMEM((count, columns), BF16),
            pltpu.VMEM((channels, LANES), BF16),
            pltpu.VMEM((channels, LANES + length), F32),
            pltpu.VMEM((columns, length), BF16),
            pltpu.VMEM((part, 64, LANES + length), BF16),
            pltpu.VMEM((part, 64, LANES + length), BF16),
            pltpu.VMEM((8 * LANES, (part + 1) * length), BF16),
            pltpu.VMEM((count, length), F32),
            pltpu.VMEM((near, 8, length), F32),
            pltpu.VMEM((part + 1, near + 1, 32, LANES), BF16),
            pltpu.VMEM((near + 1, 32, LANES), BF16),
            pltpu.VMEM((count, (part + 1) * length), BF16),
            pltpu.VMEM((ring, count, LANES), BF16),
            pltpu.VMEM((ring, count, LANES), BF16),
            pltpu.VMEM((LANES, LANES), F32),
            pltpu.VMEM((part, 32, LANES), F32),
            pltpu.VMEM((32, LANES), BF16),
            pltpu.VMEM((ring, 32, LANES), BF16),
            pltpu.VMEM((32, LANES), BF16),
            pltpu.VMEM((near, 32, LANES), BF16),
            pltpu.VMEM((LANES, LANES), F32),
            pltpu.SemaphoreType.DMA((2,)),
            *sem_pairs(1, part, near, near, plane, 1, near, ring, part, ring, near, part),
        ],
        compiler_params=pltpu.CompilerParams(
            collective_id=0, has_side_effects=True, vmem_limit_bytes=40 * 2**20
        ),
        cost_estimate=pl.CostEstimate(flops=10**9, bytes_accessed=2 * 10**6, transcendentals=0),
        name="separate",
    )(*[pltpu.with_memory_space_constraint(a, pltpu.HBM) for a in (signals, vectors)])


def solution(mesh):
    return jax.shard_map(
        shards,
        mesh=mesh,
        in_specs=(P("elec", "tm"), P(None, "elec")),
        out_specs=(P(None, "tm"), P(None, ("elec", "tm"))),
        check_vma=False,
    )
```

```python
import functools
import itertools
import math

import jax
import jax.numpy as jnp
from jax import lax
from jax.experimental import pallas as pl
from jax.experimental.pallas import tpu as pltpu
from jax.sharding import PartitionSpec as P

LAGS = 16
NS_STEPS = 6
START = 0.15
MESH = pl.DeviceIdType.MESH
SIZE = dict(x=4, h=4, l=2, z=8, c=2)
F32, BF16 = jnp.float32, jnp.bfloat16
LANES = 128


def hops(move):
    x, y, z = move.get("x", 0), 2 * move.get("h", 0) + move.get("l", 0), move.get("z", 0)
    return min(x, 4 - x) + min(y, 8 - y) + min(z, 8 - z)


def moves(*names):
    every = itertools.product(*[range(SIZE[name]) for name in names])
    found = [dict(zip(names, move)) for move in every if any(move)]
    return sorted(found, key=lambda move: -hops(move))


ELEC, PLANE, RING = moves("x", "h"), moves("x", "h", "l"), moves("z")
PART = [dict(l=1), dict(c=1), dict(l=1, c=1)]
BRICK, SHEET = moves("x", "l", "c"), moves("z", "h")


def unique(found):
    seen = {tuple(move.get(name, 0) for name in SIZE): None for move in found}
    return [dict(zip(SIZE, move)) for move in seen]


def place():
    elec, tm = lax.axis_index("elec"), lax.axis_index("tm")
    return dict(x=elec // 4, h=elec % 4, l=tm // 16, z=(tm // 2) % 8, c=tm % 2)


def moved(at, move):
    return {k: lax.rem(v + move.get(k, 0), SIZE[k]) for k, v in at.items()}


def elec_of(at):
    return at["x"] * 4 + at["h"]


def tm_of(at):
    return (at["l"] * 8 + at["z"]) * 2 + at["c"]


def brick_of(at):
    return (at["x"] * 2 + at["l"]) * 2 + at["c"]


def device(at):
    return {"elec": elec_of(at), "tm": tm_of(at)}


def send(src, dst, sems, slot, to):
    copy = pltpu.make_async_remote_copy(
        src_ref=src,
        dst_ref=dst,
        send_sem=sems[0].at[slot],
        recv_sem=sems[1].at[slot],
        device_id=to,
        device_id_type=MESH,
    )
    copy.start()
    return copy


def halves(a):
    top = a.astype(BF16)
    return top, (a - top.astype(F32)).astype(BF16)


def dot(a, b, dims=(((1,), (0,)), ((), ()))):
    return lax.dot_general(a, b, dims, preferred_element_type=F32)


def fine_dot(a, b):
    (a1, a2), (b1, b2) = halves(a), halves(b)
    return dot(jnp.concatenate([a1, a1, a2], 1), jnp.concatenate([b1, b2, b1], 0))


def fine_gram(a):
    a1, a2 = halves(a)
    both = (((1,), (1,)), ((), ()))
    return dot(jnp.concatenate([a1, a1, a2], 1), jnp.concatenate([a1, a2, a1], 1), both)


def lagged(row):
    return pltpu.roll(jnp.broadcast_to(row, (LAGS, LANES)), 0, 1, stride=1, stride_axis=0)


def kernel(
    sig_hbm, vec_hbm, sources, unmixing,
    sig, vec, tail, padded, ext, far_out, far_in, feat, partial, summed, spilled, blocks, waves, cubes,
    half, grad_out, grad_in, gram, gram_brick, gram_sum, gram_sheet, gram_all,
    load, tail_s, tail_r, far_s, far_r, rs1_s, rs1_r, rs2_s, rs2_r, cube_s, cube_r, core_s, core_r, wave_s, wave_r,
    grad_s, grad_r, g1_s, g1_r, g2_s, g2_r, g3_s, g3_r,
):
    at = place()
    elec, tm = elec_of(at), tm_of(at)
    length = sig.shape[1]
    tiles = length // LANES
    after, before = lax.rem(tm + 1, 32), lax.rem(tm + 31, 32)

    loads = [
        pltpu.make_async_copy(sig_hbm, sig, load.at[0]),
        pltpu.make_async_copy(vec_hbm, vec, load.at[1]),
    ]
    for copy in loads:
        copy.start()
    greeted = unique(PLANE + RING + PART + BRICK + SHEET)
    barrier = pltpu.get_barrier_semaphore()
    for move in greeted:
        pl.semaphore_signal(barrier, inc=1, device_id=device(moved(at, move)), device_id_type=MESH)
    for move in ELEC + [{}]:
        other = {"elec": elec_of(moved(at, move)), "tm": before}
        pl.semaphore_signal(barrier, inc=1, device_id=other, device_id_type=MESH)

    lane = lax.broadcasted_iota(jnp.int32, (LAGS, LANES), 1)
    late = lax.broadcasted_iota(jnp.int32, (LAGS, LANES), 0)
    spill = lane < late

    loads[0].wait()

    @pl.loop(0, 16)
    def _(block):
        rows = sig[pl.ds(block * 16, 16), :].astype(F32)
        for r in range(16):
            to = pl.ds((block * 16 + r) * LAGS, LAGS)
            turned = [lagged(rows[r : r + 1, k * LANES : (k + 1) * LANES]) for k in range(tiles)]
            for k, (a, b) in enumerate(zip([0.0] + turned, turned + [0.0])):
                ext[to, k * LANES : (k + 1) * LANES] = jnp.where(spill, a, b).astype(BF16)

    loads[1].wait()
    partial[...] = dot(vec[...], ext[...])
    pl.semaphore_wait(barrier, len(greeted) + len(ELEC) + 1)
    rs_copies, spill_copies = [], []
    for i, move in enumerate(ELEC + [{}]):
        to = moved(at, move)
        rows = pl.ds(pl.multiple_of(elec_of(to) * 8, 8), 8)
        if move:
            rs_copies.append(send(partial.at[rows, pl.ds(0, length)], summed.at[i], (rs1_s, rs1_r), i, device(to)))
        over = {"elec": elec_of(to), "tm": after}
        spill_copies.append(
            send(partial.at[rows, pl.ds(length, LANES)], spilled.at[i], (rs2_s, rs2_r), i, over)
        )
    tail_copy = send(
        sig.at[:, pl.ds(length - LANES, LANES)], tail, (tail_s, tail_r), 0, {"elec": elec, "tm": after}
    )

    padded[:, LANES:] = sig[...].astype(F32)
    for z in range(8):
        own = pl.multiple_of((at["l"] * 16 + z * 2 + at["c"]) * LANES, LANES)
        feat[z * LANES : (z + 1) * LANES, :length] = ext[pl.ds(own, LANES), :length]
    tail_copy.wait()
    first = jnp.where(tm > 0, 1.0, 0.0)
    padded[:, :LANES] = tail[...].astype(F32) * first

    far_copies = []
    for i, move in enumerate(PART):
        to = moved(at, move)
        starts = [pl.multiple_of((to["l"] * 16 + z * 2 + to["c"]) * 8, 8) for z in range(8)]
        far_out[i] = jnp.concatenate([padded[pl.ds(start, 8), :] for start in starts], 0).astype(BF16)
        far_copies.append(send(far_out.at[i], far_in.at[i], (far_s, far_r), i, device(to)))

    @pl.loop(0, 8)
    def _(z):
        start = pl.multiple_of((at["l"] * 16 + z * 2 + at["c"]) * 8, 8)
        rows = padded[pl.ds(start, 8), :LANES]
        for r in range(8):
            to = pl.ds((z * 8 + r) * LAGS, LAGS)
            feat[to, :LANES] = jnp.where(spill, lagged(rows[r : r + 1]), feat[to, :LANES].astype(F32)).astype(BF16)

    mine = pl.ds(pl.multiple_of(elec * 8, 8), 8)
    total = partial[mine, :length]
    for copy in rs_copies + spill_copies:
        copy.wait()
    for i in range(len(ELEC)):
        total = total + summed[i]
    over = spilled[0]
    for i in range(len(ELEC)):
        over = over + spilled[i + 1]
    total = jnp.concatenate([total[:, :LANES] + over * first, total[:, LANES:]], 1)

    def stacked(block, last):
        return jnp.concatenate([block[:, k * LANES : (k + 1) * LANES] for k in range(tiles)] + [last], 0).astype(BF16)

    deriv = jnp.sum(3.0 * total * total, axis=1, keepdims=True)
    high = deriv.astype(BF16).astype(F32)
    middle = (deriv - high).astype(BF16).astype(F32)
    low = deriv - high - middle
    lane = lax.broadcasted_iota(jnp.int32, (8, LANES), 1)
    pad = jnp.where(lane == 0, high, jnp.where(lane == 1, middle, jnp.where(lane == 2, low, 0.0)))
    blocks[0, elec] = stacked(total * total * total, pad)
    waves[elec] = stacked(total, jnp.zeros((8, LANES), F32))
    cube_copies = []
    for i, move in enumerate(PLANE):
        cube_copies.append(
            send(blocks.at[0, elec], blocks.at[move["l"], elec], (cube_s, cube_r), i, device(moved(at, move)))
        )
    wave_copies = [
        send(waves.at[elec], waves.at[elec], (wave_s, wave_r), i, device(moved(at, move)))
        for i, move in enumerate(ELEC)
    ]

    for i, copy in enumerate(far_copies):
        copy.wait()

        @pl.loop(0, 4)
        def _(block):
            rows = far_in[i, pl.ds(block * 16, 16), :].astype(F32)
            for r in range(16):
                to = pl.ds((block * 16 + r) * LAGS, LAGS)
                turned = [lagged(rows[r : r + 1, k * LANES : (k + 1) * LANES]) for k in range(tiles + 1)]
                for k in range(tiles):
                    begin = (i + 1) * length + k * LANES
                    feat[to, begin : begin + LANES] = jnp.where(spill, turned[k], turned[k + 1]).astype(BF16)

    for copy in cube_copies:
        copy.wait()
    core_copy = send(blocks.at[pl.ds(0, 2)], blocks.at[pl.ds(2, 2)], (core_s, core_r), 0, device(moved(at, PART[1])))

    def unpack(shard):
        pads = []
        for pair in range(8):
            pieces = [blocks[shard, 2 * pair + k].astype(F32) for k in range(2)]
            for k in range(tiles):
                rows = jnp.concatenate([piece[8 * k : 8 * k + 8] for piece in pieces], 0)
                begin = shard * length + k * LANES
                cubes[16 * pair : 16 * pair + 16, begin : begin + LANES] = rows.astype(BF16)
            pads += [piece[8 * tiles :] for piece in pieces]
        return jnp.concatenate(pads, 0)

    both = (((1,), (1,)), ((), ()))
    pads = unpack(0) + unpack(1)
    for z in range(8):
        half[z] = dot(cubes[:, : 2 * length], feat[z * LANES : (z + 1) * LANES, : 2 * length], both)
    core_copy.wait()
    pads = pads + unpack(2) + unpack(3)
    deriv = jnp.sum(pads, axis=1, keepdims=True)

    def block_of(z):
        rows = pl.ds(pl.multiple_of(z * LANES, LANES), LANES)
        columns = pl.ds(pl.multiple_of((at["l"] * 16 + z * 2 + at["c"]) * LANES, LANES), LANES)
        grad = half[z] + dot(cubes[:, 2 * length :], feat[rows, 2 * length :], both)
        return grad - deriv * vec[:, columns].astype(F32)

    grad_copies = []
    for i, move in enumerate(RING):
        to = moved(at, move)
        grad_out[i] = block_of(to["z"]).astype(BF16)
        grad_copies.append(send(grad_out.at[i], grad_in.at[i], (grad_s, grad_r), i, device(to)))
    updated = block_of(at["z"])
    for copy in wave_copies:
        copy.wait()
    for pair in range(8):
        pieces = [waves[2 * pair + k].astype(F32) for k in range(2)]
        for k in range(tiles):
            rows = jnp.concatenate([piece[8 * k : 8 * k + 8] for piece in pieces], 0)
            sources[16 * pair : 16 * pair + 16, k * LANES : (k + 1) * LANES] = rows.astype(BF16)
    for i, copy in enumerate(grad_copies):
        copy.wait()
        updated = updated + grad_in[i].astype(F32)
    updated = updated * (1.0 / (length * 32))

    gram[...] = fine_gram(updated)
    mine = pl.ds(pl.multiple_of(brick_of(at) * 8, 8), 8)
    copies = []
    for i, move in enumerate(BRICK):
        to = moved(at, move)
        rows = pl.ds(pl.multiple_of(brick_of(to) * 8, 8), 8)
        copies.append(send(gram.at[rows], gram_brick.at[i], (g1_s, g1_r), i, device(to)))
    total = gram[mine, :]
    for copy in copies:
        copy.wait()
    for i in range(len(BRICK)):
        total = total + gram_brick[i]
    gram_sum[...] = total
    copies = [
        send(gram_sum, gram_sheet.at[i], (g2_s, g2_r), i, device(moved(at, move))) for i, move in enumerate(SHEET)
    ]
    for copy in copies:
        copy.wait()
    for i in range(len(SHEET)):
        total = total + gram_sheet[i]
    gram_all[mine, :] = total
    copies = [
        send(gram_all.at[mine], gram_all.at[mine], (g3_s, g3_r), i, device(moved(at, move)))
        for i, move in enumerate(BRICK)
    ]
    for copy in copies:
        copy.wait()

    g = gram_all[...]
    row = lax.broadcasted_iota(jnp.int32, (LANES, LANES), 0)
    column = lax.broadcasted_iota(jnp.int32, (LANES, LANES), 1)
    unit = jnp.where(row == column, 1.0, 0.0)
    squares = jnp.sum(jnp.sum(g * unit, axis=1, keepdims=True), axis=0, keepdims=True)
    scale = START * math.sqrt(LANES) * lax.rsqrt(squares + 1e-06)
    g = g * scale * scale
    product = None
    for step in range(NS_STEPS):
        factor = 1.5 * unit - 0.5 * g
        product = factor if product is None else fine_dot(factor, product)
        if step < NS_STEPS - 1:
            g = fine_dot(fine_dot(factor, g), factor)
    unmixing[...] = fine_dot(product, updated * scale)


def sem_pairs(*counts):
    return [pltpu.SemaphoreType.DMA((count,)) for count in counts for _ in range(2)]


def shards(signals, vectors):
    channels, length = signals.shape
    count, columns = vectors.shape
    near, plane, ring, part, brick, sheet = (len(group) for group in (ELEC, PLANE, RING, PART, BRICK, SHEET))
    vmem = pl.BlockSpec(memory_space=pltpu.VMEM)
    return pl.pallas_call(
        kernel,
        out_shape=(
            jax.ShapeDtypeStruct((count, length), BF16),
            jax.ShapeDtypeStruct((count, LANES), F32),
        ),
        in_specs=[pl.BlockSpec(memory_space=pltpu.HBM)] * 2,
        out_specs=(vmem, vmem),
        scratch_shapes=[
            pltpu.VMEM((channels, length), BF16),
            pltpu.VMEM((count, columns), BF16),
            pltpu.VMEM((channels, LANES), BF16),
            pltpu.VMEM((channels, LANES + length), F32),
            pltpu.VMEM((columns, length + LANES), BF16),
            pltpu.VMEM((part, 64, LANES + length), BF16),
            pltpu.VMEM((part, 64, LANES + length), BF16),
            pltpu.VMEM((8 * LANES, (part + 1) * length), BF16),
            pltpu.VMEM((count, length + LANES), F32),
            pltpu.VMEM((near, 8, length), F32),
            pltpu.VMEM((near + 1, 8, LANES), F32),
            pltpu.VMEM((part + 1, near + 1, 32, LANES), BF16),
            pltpu.VMEM((near + 1, 32, LANES), BF16),
            pltpu.VMEM((count, (part + 1) * length), BF16),
            pltpu.VMEM((8, count, LANES), F32),
            pltpu.VMEM((ring, count, LANES), BF16),
            pltpu.VMEM((ring, count, LANES), BF16),
            pltpu.VMEM((LANES, LANES), F32),
            pltpu.VMEM((brick, 8, LANES), F32),
            pltpu.VMEM((8, LANES), F32),
            pltpu.VMEM((sheet, 8, LANES), F32),
            pltpu.VMEM((LANES, LANES), F32),
            pltpu.SemaphoreType.DMA((2,)),
            *sem_pairs(1, part, near, near + 1, plane, 1, near, ring, brick, sheet, brick),
        ],
        compiler_params=pltpu.CompilerParams(
            collective_id=0, has_side_effects=True, vmem_limit_bytes=40 * 2**20
        ),
        cost_estimate=pl.CostEstimate(flops=10**9, bytes_accessed=2 * 10**6, transcendentals=0),
        name="separate",
    )(*[pltpu.with_memory_space_constraint(a, pltpu.HBM) for a in (signals, vectors)])


def solution(mesh):
    return jax.shard_map(
        shards,
        mesh=mesh,
        in_specs=(P("elec", "tm"), P(None, "elec")),
        out_specs=(P(None, "tm"), P(None, ("elec", "tm"))),
        check_vma=False,
    )
```

```python
import functools
import itertools
import math

import jax
import jax.numpy as jnp
from jax import lax
from jax.experimental import pallas as pl
from jax.experimental.pallas import tpu as pltpu
from jax.sharding import PartitionSpec as P

LAGS = 16
NS_STEPS = 6
START = 0.15
MESH = pl.DeviceIdType.MESH
SIZE = dict(x=4, h=4, l=2, z=8, c=2)
F32, BF16 = jnp.float32, jnp.bfloat16
LANES = 128


def hops(move):
    x, y, z = move.get("x", 0), 2 * move.get("h", 0) + move.get("l", 0), move.get("z", 0)
    return min(x, 4 - x) + min(y, 8 - y) + min(z, 8 - z)


def moves(*names):
    every = itertools.product(*[range(SIZE[name]) for name in names])
    found = [dict(zip(names, move)) for move in every if any(move)]
    return sorted(found, key=lambda move: -hops(move))


ELEC, PLANE, RING = moves("x", "h"), moves("x", "h", "l"), moves("z")
PART = [dict(l=1), dict(c=1), dict(l=1, c=1)]
BRICK, SHEET = moves("x", "l", "c"), moves("z", "h")


def unique(found):
    seen = {tuple(move.get(name, 0) for name in SIZE): None for move in found}
    return [dict(zip(SIZE, move)) for move in seen]


def place():
    elec, tm = lax.axis_index("elec"), lax.axis_index("tm")
    return dict(x=elec // 4, h=elec % 4, l=tm // 16, z=(tm // 2) % 8, c=tm % 2)


def moved(at, move):
    return {k: lax.rem(v + move.get(k, 0), SIZE[k]) for k, v in at.items()}


def elec_of(at):
    return at["x"] * 4 + at["h"]


def tm_of(at):
    return (at["l"] * 8 + at["z"]) * 2 + at["c"]


def brick_of(at):
    return (at["x"] * 2 + at["l"]) * 2 + at["c"]


def device(at):
    return {"elec": elec_of(at), "tm": tm_of(at)}


def send(src, dst, sems, slot, to):
    copy = pltpu.make_async_remote_copy(
        src_ref=src,
        dst_ref=dst,
        send_sem=sems[0].at[slot],
        recv_sem=sems[1].at[slot],
        device_id=to,
        device_id_type=MESH,
    )
    copy.start()
    return copy


def halves(a):
    top = a.astype(BF16)
    return top, (a - top.astype(F32)).astype(BF16)


def dot(a, b, dims=(((1,), (0,)), ((), ()))):
    return lax.dot_general(a, b, dims, preferred_element_type=F32)


def fine_dot(a, b):
    (a1, a2), (b1, b2) = halves(a), halves(b)
    return dot(jnp.concatenate([a1, a1, a2], 1), jnp.concatenate([b1, b2, b1], 0))


def fine_gram(a):
    a1, a2 = halves(a)
    both = (((1,), (1,)), ((), ()))
    return dot(jnp.concatenate([a1, a1, a2], 1), jnp.concatenate([a1, a2, a1], 1), both)


def lagged(row, shift=0):
    return pltpu.roll(jnp.broadcast_to(row, (LAGS, LANES)), shift, 1, stride=1, stride_axis=0)


def packed(tile, shift):
    return jnp.sum(pltpu.roll(tile, shift, 1, stride=LAGS, stride_axis=0), axis=0, keepdims=True)


def before_first(row, r):
    return lagged(row, (LANES - (r + 1) * LAGS) % LANES)


def kernel(
    sig_hbm, vec_hbm, sources, unmixing,
    sig, vec, wide, tail_out, tail_in, ext, far_out, far_in, late_out, late_in, feat,
    partial, summed, spill_out, spill_in, blocks, waves, cubes,
    half, grad_out, grad_in, gram, gram_brick, gram_sum, gram_sheet, gram_all,
    load, tail_s, tail_r, far_s, far_r, late_s, late_r, rs1_s, rs1_r, rs2_s, rs2_r, cube_s, cube_r, core_s, core_r, wave_s, wave_r,
    grad_s, grad_r, g1_s, g1_r, g2_s, g2_r, g3_s, g3_r,
):
    at = place()
    elec, tm = elec_of(at), tm_of(at)
    length = sig.shape[1]
    tiles = length // LANES
    after, before = lax.rem(tm + 1, 32), lax.rem(tm + 31, 32)

    loads = [
        pltpu.make_async_copy(sig_hbm, sig, load.at[0]),
        pltpu.make_async_copy(vec_hbm, vec, load.at[1]),
    ]
    for copy in loads:
        copy.start()
    greeted = unique(PLANE + RING + PART)
    barrier = pltpu.get_barrier_semaphore()
    for move in greeted:
        pl.semaphore_signal(barrier, inc=1, device_id=device(moved(at, move)), device_id_type=MESH)
    for move in ELEC + [{}]:
        other = {"elec": elec_of(moved(at, move)), "tm": before}
        pl.semaphore_signal(barrier, inc=1, device_id=other, device_id_type=MESH)

    lane = lax.broadcasted_iota(jnp.int32, (LAGS, LANES), 1)
    late = lax.broadcasted_iota(jnp.int32, (LAGS, LANES), 0)
    spill = lane < late

    loads[0].wait()

    @pl.loop(0, 16)
    def _(block):
        rows = sig[pl.ds(block * 16, 16), :].astype(F32)
        for r in range(16):
            to = pl.ds((block * 16 + r) * LAGS, LAGS)
            turned = [lagged(rows[r : r + 1, k * LANES : (k + 1) * LANES]) for k in range(tiles)]
            for k, (a, b) in enumerate(zip([0.0] + turned, turned + [0.0])):
                ext[to, k * LANES : (k + 1) * LANES] = jnp.where(spill, a, b).astype(BF16)

    loads[1].wait()
    partial[...] = dot(vec[...], ext[...])
    spill_out[...] = jnp.concatenate([packed(partial[8 * k : 8 * k + 8, length:], 0) for k in range(16)], 0)
    pl.semaphore_wait(barrier, len(greeted) + len(ELEC) + 1)
    rs_copies, spill_copies = [], []
    for i, move in enumerate(ELEC + [{}]):
        to = moved(at, move)
        rows = pl.ds(pl.multiple_of(elec_of(to) * 8, 8), 8)
        if move:
            rs_copies.append(send(partial.at[rows, pl.ds(0, length)], summed.at[i], (rs1_s, rs1_r), i, device(to)))
        over = {"elec": elec_of(to), "tm": after}
        spill_copies.append(
            send(spill_out.at[pl.ds(elec_of(to), 1)], spill_in.at[pl.ds(i, 1)], (rs2_s, rs2_r), i, over)
        )
    wide[...] = sig[...].astype(F32)
    last = lax.broadcasted_iota(jnp.int32, (8, LANES), 1) >= LANES - LAGS
    tail_out[...] = jnp.concatenate(
        [
            packed(jnp.where(last, wide[8 * k : 8 * k + 8, length - LANES :], 0.0), LAGS)
            for k in range(wide.shape[0] // 8)
        ],
        0,
    )
    tail_copy = send(tail_out, tail_in, (tail_s, tail_r), 0, {"elec": elec, "tm": after})

    def start_of(to, z):
        return to["l"] * 16 + z * 2 + to["c"]

    for i, move in enumerate(PART):
        to = moved(at, move)
        starts = [pl.multiple_of(start_of(to, z) * 8, 8) for z in range(8)]
        far_out[i] = jnp.concatenate([wide[pl.ds(start, 8), :] for start in starts], 0).astype(BF16)
    for z in range(8):
        own = pl.multiple_of(start_of(at, z) * LANES, LANES)
        feat[z * LANES : (z + 1) * LANES, :length] = ext[pl.ds(own, LANES), :length]
    for copy in rs_copies:
        copy.wait_send()
    far_copies = [
        send(far_out.at[i], far_in.at[i], (far_s, far_r), i, device(moved(at, move))) for i, move in enumerate(PART)
    ]
    tail_copy.wait()
    first = jnp.where(tm > 0, 1.0, 0.0)
    late_copies = []
    for i, move in enumerate(PART):
        to = moved(at, move)
        late_out[i] = jnp.concatenate([tail_in[pl.ds(start_of(to, z), 1), :] for z in range(8)], 0) * first
        late_copies.append(send(late_out.at[i], late_in.at[i], (late_s, late_r), i, device(to)))

    @pl.loop(0, 8)
    def _(z):
        row = tail_in[pl.ds(start_of(at, z), 1), :] * first
        for r in range(8):
            to = pl.ds((z * 8 + r) * LAGS, LAGS)
            feat[to, :LANES] = jnp.where(spill, before_first(row, r), feat[to, :LANES].astype(F32)).astype(BF16)

    mine = pl.ds(pl.multiple_of(elec * 8, 8), 8)
    total = partial[mine, :length]
    for copy in rs_copies:
        copy.wait_recv()
    for copy in spill_copies:
        copy.wait()
    for i in range(len(ELEC)):
        total = total + summed[i]
    over = jnp.sum(spill_in[...], axis=0, keepdims=True) * first
    over = jnp.concatenate([pltpu.roll(over, (LANES - r * LAGS) % LANES, 1) for r in range(8)], 0)
    over = jnp.where(lax.broadcasted_iota(jnp.int32, (8, LANES), 1) < LAGS, over, 0.0)
    total = jnp.concatenate([total[:, :LANES] + over, total[:, LANES:]], 1)

    def stacked(block, last):
        return jnp.concatenate([block[:, k * LANES : (k + 1) * LANES] for k in range(tiles)] + [last], 0).astype(BF16)

    deriv = jnp.sum(3.0 * total * total, axis=1, keepdims=True)
    high = deriv.astype(BF16).astype(F32)
    middle = (deriv - high).astype(BF16).astype(F32)
    low = deriv - high - middle
    lane = lax.broadcasted_iota(jnp.int32, (8, LANES), 1)
    pad = jnp.where(lane == 0, high, jnp.where(lane == 1, middle, jnp.where(lane == 2, low, 0.0)))
    blocks[0, elec] = stacked(total * total * total, pad)
    waves[elec] = stacked(total, jnp.zeros((8, LANES), F32))
    cube_copies = []
    for i, move in enumerate(PLANE):
        cube_copies.append(
            send(blocks.at[0, elec], blocks.at[move["l"], elec], (cube_s, cube_r), i, device(moved(at, move)))
        )
    for i, (copy, late_copy) in enumerate(zip(far_copies, late_copies)):
        copy.wait()
        late_copy.wait()

        @pl.loop(0, 4)
        def _(block):
            rows = far_in[i, pl.ds(block * 16, 16), :].astype(F32)
            ends = late_in[i, pl.ds(block * 2, 2), :]
            for r in range(16):
                to = pl.ds((block * 16 + r) * LAGS, LAGS)
                turned = [before_first(ends[r // 8 : r // 8 + 1], r % 8)]
                turned += [lagged(rows[r : r + 1, k * LANES : (k + 1) * LANES]) for k in range(tiles)]
                for k in range(tiles):
                    begin = (i + 1) * length + k * LANES
                    feat[to, begin : begin + LANES] = jnp.where(spill, turned[k], turned[k + 1]).astype(BF16)

    for copy in cube_copies:
        copy.wait()
    core_copy = send(blocks.at[pl.ds(0, 2)], blocks.at[pl.ds(2, 2)], (core_s, core_r), 0, device(moved(at, PART[1])))

    def unpack(shard):
        pads = []
        for pair in range(8):
            pieces = [blocks[shard, 2 * pair + k].astype(F32) for k in range(2)]
            for k in range(tiles):
                rows = jnp.concatenate([piece[8 * k : 8 * k + 8] for piece in pieces], 0)
                begin = shard * length + k * LANES
                cubes[16 * pair : 16 * pair + 16, begin : begin + LANES] = rows.astype(BF16)
            pads += [piece[8 * tiles :] for piece in pieces]
        return jnp.concatenate(pads, 0)

    both = (((1,), (1,)), ((), ()))
    pads = unpack(0) + unpack(1)
    for z in range(8):
        half[z] = dot(cubes[:, : 2 * length], feat[z * LANES : (z + 1) * LANES, : 2 * length], both)
    core_copy.wait()
    pads = pads + unpack(2) + unpack(3)
    deriv = jnp.sum(pads, axis=1, keepdims=True)

    def block_of(z):
        rows = pl.ds(pl.multiple_of(z * LANES, LANES), LANES)
        columns = pl.ds(pl.multiple_of((at["l"] * 16 + z * 2 + at["c"]) * LANES, LANES), LANES)
        grad = half[z] + dot(cubes[:, 2 * length :], feat[rows, 2 * length :], both)
        return grad - deriv * vec[:, columns].astype(F32)

    grad_copies = []
    for i, move in enumerate(RING):
        to = moved(at, move)
        grad_out[i] = block_of(to["z"]).astype(BF16)
        grad_copies.append(send(grad_out.at[i], grad_in.at[i], (grad_s, grad_r), i, device(to)))
    wave_copies = [
        send(waves.at[elec], waves.at[elec], (wave_s, wave_r), i, device(moved(at, move)))
        for i, move in enumerate(ELEC)
    ]
    updated = block_of(at["z"])
    for copy in wave_copies:
        copy.wait()
    for pair in range(8):
        pieces = [waves[2 * pair + k].astype(F32) for k in range(2)]
        for k in range(tiles):
            rows = jnp.concatenate([piece[8 * k : 8 * k + 8] for piece in pieces], 0)
            sources[16 * pair : 16 * pair + 16, k * LANES : (k + 1) * LANES] = rows.astype(BF16)
    for i, copy in enumerate(grad_copies):
        copy.wait()
        updated = updated + grad_in[i].astype(F32)
    updated = updated * (1.0 / (length * 32))

    gram[...] = fine_gram(updated)
    mine = pl.ds(pl.multiple_of(brick_of(at) * 8, 8), 8)
    copies = []
    for i, move in enumerate(BRICK):
        to = moved(at, move)
        rows = pl.ds(pl.multiple_of(brick_of(to) * 8, 8), 8)
        copies.append(send(gram.at[rows], gram_brick.at[i], (g1_s, g1_r), i, device(to)))
    total = gram[mine, :]
    for copy in copies:
        copy.wait()
    for i in range(len(BRICK)):
        total = total + gram_brick[i]
    gram_sum[...] = total
    copies = [
        send(gram_sum, gram_sheet.at[i], (g2_s, g2_r), i, device(moved(at, move))) for i, move in enumerate(SHEET)
    ]
    for copy in copies:
        copy.wait()
    for i in range(len(SHEET)):
        total = total + gram_sheet[i]
    gram_all[mine, :] = total
    copies = [
        send(gram_all.at[mine], gram_all.at[mine], (g3_s, g3_r), i, device(moved(at, move)))
        for i, move in enumerate(BRICK)
    ]
    for copy in copies:
        copy.wait()

    g = gram_all[...]
    row = lax.broadcasted_iota(jnp.int32, (LANES, LANES), 0)
    column = lax.broadcasted_iota(jnp.int32, (LANES, LANES), 1)
    unit = jnp.where(row == column, 1.0, 0.0)
    squares = jnp.sum(jnp.sum(g * unit, axis=1, keepdims=True), axis=0, keepdims=True)
    scale = START * math.sqrt(LANES) * lax.rsqrt(squares + 1e-06)
    g = g * scale * scale
    product = None
    for step in range(NS_STEPS):
        factor = 1.5 * unit - 0.5 * g
        product = factor if product is None else fine_dot(factor, product)
        if step < NS_STEPS - 1:
            g = fine_dot(fine_dot(factor, g), factor)
    unmixing[...] = fine_dot(product, updated * scale)


def sem_pairs(*counts):
    return [pltpu.SemaphoreType.DMA((count,)) for count in counts for _ in range(2)]


def shards(signals, vectors):
    channels, length = signals.shape
    count, columns = vectors.shape
    near, plane, ring, part, brick, sheet = (len(group) for group in (ELEC, PLANE, RING, PART, BRICK, SHEET))
    vmem = pl.BlockSpec(memory_space=pltpu.VMEM)
    return pl.pallas_call(
        kernel,
        out_shape=(
            jax.ShapeDtypeStruct((count, length), BF16),
            jax.ShapeDtypeStruct((count, LANES), F32),
        ),
        in_specs=[pl.BlockSpec(memory_space=pltpu.HBM)] * 2,
        out_specs=(vmem, vmem),
        scratch_shapes=[
            pltpu.VMEM((channels, length), BF16),
            pltpu.VMEM((count, columns), BF16),
            pltpu.VMEM((channels, length), F32),
            pltpu.VMEM((channels // 8, LANES), F32),
            pltpu.VMEM((channels // 8, LANES), F32),
            pltpu.VMEM((columns, length + LANES), BF16),
            pltpu.VMEM((part, 64, length), BF16),
            pltpu.VMEM((part, 64, length), BF16),
            pltpu.VMEM((part, 8, LANES), F32),
            pltpu.VMEM((part, 8, LANES), F32),
            pltpu.VMEM((8 * LANES, (part + 1) * length), BF16),
            pltpu.VMEM((count, length + LANES), F32),
            pltpu.VMEM((near, 8, length), F32),
            pltpu.VMEM((near + 1, LANES), F32),
            pltpu.VMEM((near + 1, LANES), F32),
            pltpu.VMEM((part + 1, near + 1, 32, LANES), BF16),
            pltpu.VMEM((near + 1, 32, LANES), BF16),
            pltpu.VMEM((count, (part + 1) * length), BF16),
            pltpu.VMEM((8, count, LANES), F32),
            pltpu.VMEM((ring, count, LANES), BF16),
            pltpu.VMEM((ring, count, LANES), BF16),
            pltpu.VMEM((LANES, LANES), F32),
            pltpu.VMEM((brick, 8, LANES), F32),
            pltpu.VMEM((8, LANES), F32),
            pltpu.VMEM((sheet, 8, LANES), F32),
            pltpu.VMEM((LANES, LANES), F32),
            pltpu.SemaphoreType.DMA((2,)),
            *sem_pairs(1, part, part, near, near + 1, plane, 1, near, ring, brick, sheet, brick),
        ],
        compiler_params=pltpu.CompilerParams(
            collective_id=0, has_side_effects=True, vmem_limit_bytes=40 * 2**20
        ),
        cost_estimate=pl.CostEstimate(flops=10**9, bytes_accessed=2 * 10**6, transcendentals=0),
        name="separate",
    )(*[pltpu.with_memory_space_constraint(a, pltpu.HBM) for a in (signals, vectors)])


def solution(mesh):
    return jax.shard_map(
        shards,
        mesh=mesh,
        in_specs=(P("elec", "tm"), P(None, "elec")),
        out_specs=(P(None, "tm"), P(None, ("elec", "tm"))),
        check_vma=False,
    )
```

```python
import functools
import itertools
import math

import jax
import jax.numpy as jnp
from jax import lax
from jax.experimental import pallas as pl
from jax.experimental.pallas import tpu as pltpu
from jax.sharding import PartitionSpec as P

LAGS = 16
NS_STEPS = 6
START = 0.15
MESH = pl.DeviceIdType.MESH
SIZE = dict(x=4, h=4, l=2, z=8, c=2)
F32, BF16 = jnp.float32, jnp.bfloat16
LANES = 128


def hops(move):
    x, y, z = move.get("x", 0), 2 * move.get("h", 0) + move.get("l", 0), move.get("z", 0)
    return min(x, 4 - x) + min(y, 8 - y) + min(z, 8 - z)


def moves(*names):
    every = itertools.product(*[range(SIZE[name]) for name in names])
    found = [dict(zip(names, move)) for move in every if any(move)]
    return sorted(found, key=lambda move: -hops(move))


ELEC, PLANE, RING = moves("x", "h"), moves("x", "h", "l"), moves("z")
PART = [dict(l=1), dict(c=1), dict(l=1, c=1)]
BRICK, SHEET = moves("x", "l", "c"), moves("z", "h")


def unique(found):
    seen = {tuple(move.get(name, 0) for name in SIZE): None for move in found}
    return [dict(zip(SIZE, move)) for move in seen]


def place():
    elec, tm = lax.axis_index("elec"), lax.axis_index("tm")
    return dict(x=elec // 4, h=elec % 4, l=tm // 16, z=(tm // 2) % 8, c=tm % 2)


def moved(at, move):
    return {k: lax.rem(v + move.get(k, 0), SIZE[k]) for k, v in at.items()}


def elec_of(at):
    return at["x"] * 4 + at["h"]


def tm_of(at):
    return (at["l"] * 8 + at["z"]) * 2 + at["c"]


def brick_of(at):
    return (at["x"] * 2 + at["l"]) * 2 + at["c"]


def device(at):
    return {"elec": elec_of(at), "tm": tm_of(at)}


def remote(src, dst, sems, step, to):
    return pltpu.make_async_remote_copy(
        src_ref=src,
        dst_ref=dst,
        send_sem=sems[0].at[step],
        recv_sem=sems[1].at[step],
        device_id=to,
        device_id_type=MESH,
    )


(TAIL, FAR, LATE, SUM, SPILL, CUBE, CORE, WAVE, GRAD, GRAM1, GRAM2, GRAM3) = range(12)


def halves(a):
    top = a.astype(BF16)
    return top, (a - top.astype(F32)).astype(BF16)


def dot(a, b, dims=(((1,), (0,)), ((), ()))):
    return lax.dot_general(a, b, dims, preferred_element_type=F32)


def fine_dot(a, b):
    (a1, a2), (b1, b2) = halves(a), halves(b)
    return dot(jnp.concatenate([a1, a1, a2], 1), jnp.concatenate([b1, b2, b1], 0))


def fine_gram(a):
    a1, a2 = halves(a)
    both = (((1,), (1,)), ((), ()))
    return dot(jnp.concatenate([a1, a1, a2], 1), jnp.concatenate([a1, a2, a1], 1), both)


def lagged(row, shift=0):
    return pltpu.roll(jnp.broadcast_to(row, (LAGS, LANES)), shift, 1, stride=1, stride_axis=0)


def packed(tile, shift):
    return jnp.sum(pltpu.roll(tile, shift, 1, stride=LAGS, stride_axis=0), axis=0, keepdims=True)


def before_first(row, r):
    return lagged(row, (LANES - (r + 1) * LAGS) % LANES)


def kernel(
    sig_hbm, vec_hbm, sources, unmixing,
    sig, vec, wide, tail_out, tail_in, ext, far_out, far_in, late_out, late_in, feat,
    partial, summed, spill_out, spill_in, blocks, waves, cubes,
    half, grad_out, grad_in, gram, gram_brick, gram_sum, gram_sheet, gram_all,
    load, sent, got,
):
    at = place()
    elec, tm = elec_of(at), tm_of(at)
    length = sig.shape[1]
    tiles = length // LANES
    after, before = lax.rem(tm + 1, 32), lax.rem(tm + 31, 32)

    loads = [
        pltpu.make_async_copy(sig_hbm, sig, load.at[0]),
        pltpu.make_async_copy(vec_hbm, vec, load.at[1]),
    ]
    for copy in loads:
        copy.start()
    sems = (sent, got)
    partner = device(moved(at, PART[1]))

    def send(src, dst, step, to):
        remote(src, dst, sems, step, to).start()

    def left(step, ref):
        remote(ref, ref, sems, step, partner).wait_send()

    def came(step, ref):
        remote(ref, ref, sems, step, partner).wait_recv()

    greeted = unique(PLANE + RING + PART)
    barrier = pltpu.get_barrier_semaphore()
    for move in greeted:
        pl.semaphore_signal(barrier, inc=1, device_id=device(moved(at, move)), device_id_type=MESH)
    for move in ELEC + [{}]:
        other = {"elec": elec_of(moved(at, move)), "tm": before}
        pl.semaphore_signal(barrier, inc=1, device_id=other, device_id_type=MESH)

    lane = lax.broadcasted_iota(jnp.int32, (LAGS, LANES), 1)
    late = lax.broadcasted_iota(jnp.int32, (LAGS, LANES), 0)
    spill = lane < late

    loads[0].wait()

    @pl.loop(0, 16)
    def _(block):
        rows = sig[pl.ds(block * 16, 16), :].astype(F32)
        for r in range(16):
            to = pl.ds((block * 16 + r) * LAGS, LAGS)
            turned = [lagged(rows[r : r + 1, k * LANES : (k + 1) * LANES]) for k in range(tiles)]
            for k, (a, b) in enumerate(zip([0.0] + turned, turned + [0.0])):
                ext[to, k * LANES : (k + 1) * LANES] = jnp.where(spill, a, b).astype(BF16)

    loads[1].wait()
    partial[...] = dot(vec[...], ext[...])
    spill_out[...] = jnp.concatenate([packed(partial[8 * k : 8 * k + 8, length:], 0) for k in range(16)], 0)
    pl.semaphore_wait(barrier, len(greeted) + len(ELEC) + 1)
    for i, move in enumerate(ELEC + [{}]):
        to = moved(at, move)
        rows = pl.ds(pl.multiple_of(elec_of(to) * 8, 8), 8)
        if move:
            send(partial.at[rows, pl.ds(0, length)], summed.at[i], SUM, device(to))
        over = {"elec": elec_of(to), "tm": after}
        send(spill_out.at[pl.ds(elec_of(to), 1)], spill_in.at[pl.ds(i, 1)], SPILL, over)
    wide[...] = sig[...].astype(F32)
    last = lax.broadcasted_iota(jnp.int32, (8, LANES), 1) >= LANES - LAGS
    tail_out[...] = jnp.concatenate(
        [
            packed(jnp.where(last, wide[8 * k : 8 * k + 8, length - LANES :], 0.0), LAGS)
            for k in range(wide.shape[0] // 8)
        ],
        0,
    )
    send(tail_out, tail_in, TAIL, {"elec": elec, "tm": after})

    def start_of(to, z):
        return to["l"] * 16 + z * 2 + to["c"]

    for i, move in enumerate(PART):
        to = moved(at, move)
        starts = [pl.multiple_of(start_of(to, z) * 8, 8) for z in range(8)]
        far_out[i] = jnp.concatenate([wide[pl.ds(start, 8), :] for start in starts], 0).astype(BF16)
    for z in range(8):
        own = pl.multiple_of(start_of(at, z) * LANES, LANES)
        feat[z * LANES : (z + 1) * LANES, :length] = ext[pl.ds(own, LANES), :length]
    left(SUM, summed)
    for i, move in enumerate(PART):
        send(far_out.at[i], far_in.at[i], FAR, device(moved(at, move)))
    came(TAIL, tail_in)
    first = jnp.where(tm > 0, 1.0, 0.0)
    for i, move in enumerate(PART):
        to = moved(at, move)
        late_out[i] = jnp.concatenate([tail_in[pl.ds(start_of(to, z), 1), :] for z in range(8)], 0) * first
        send(late_out.at[i], late_in.at[i], LATE, device(to))

    @pl.loop(0, 8)
    def _(z):
        row = tail_in[pl.ds(start_of(at, z), 1), :] * first
        for r in range(8):
            to = pl.ds((z * 8 + r) * LAGS, LAGS)
            feat[to, :LANES] = jnp.where(spill, before_first(row, r), feat[to, :LANES].astype(F32)).astype(BF16)

    mine = pl.ds(pl.multiple_of(elec * 8, 8), 8)
    total = partial[mine, :length]
    came(SUM, summed)
    came(SPILL, spill_in)
    for i in range(len(ELEC)):
        total = total + summed[i]
    over = jnp.sum(spill_in[...], axis=0, keepdims=True) * first
    over = jnp.concatenate([pltpu.roll(over, (LANES - r * LAGS) % LANES, 1) for r in range(8)], 0)
    over = jnp.where(lax.broadcasted_iota(jnp.int32, (8, LANES), 1) < LAGS, over, 0.0)
    total = jnp.concatenate([total[:, :LANES] + over, total[:, LANES:]], 1)

    def stacked(block, last):
        return jnp.concatenate([block[:, k * LANES : (k + 1) * LANES] for k in range(tiles)] + [last], 0).astype(BF16)

    deriv = jnp.sum(3.0 * total * total, axis=1, keepdims=True)
    high = deriv.astype(BF16).astype(F32)
    middle = (deriv - high).astype(BF16).astype(F32)
    low = deriv - high - middle
    lane = lax.broadcasted_iota(jnp.int32, (8, LANES), 1)
    pad = jnp.where(lane == 0, high, jnp.where(lane == 1, middle, jnp.where(lane == 2, low, 0.0)))
    blocks[elec] = stacked(total * total * total, pad)
    waves[elec] = stacked(total, jnp.zeros((8, LANES), F32))
    for move in PLANE:
        send(blocks.at[elec], blocks.at[elec + 16 * move["l"]], CUBE, device(moved(at, move)))
    came(FAR, far_in)
    came(LATE, late_in)
    for i in range(len(PART)):

        @pl.loop(0, 4)
        def _(block):
            rows = far_in[i, pl.ds(block * 16, 16), :].astype(F32)
            ends = late_in[i, pl.ds(block * 2, 2), :]
            for r in range(16):
                to = pl.ds((block * 16 + r) * LAGS, LAGS)
                turned = [before_first(ends[r // 8 : r // 8 + 1], r % 8)]
                turned += [lagged(rows[r : r + 1, k * LANES : (k + 1) * LANES]) for k in range(tiles)]
                for k in range(tiles):
                    begin = (i + 1) * length + k * LANES
                    feat[to, begin : begin + LANES] = jnp.where(spill, turned[k], turned[k + 1]).astype(BF16)

    came(CUBE, blocks.at[pl.ds(0, len(PLANE))])
    left(CUBE, blocks.at[pl.ds(0, len(PLANE))])
    send(blocks.at[pl.ds(0, 32)], blocks.at[pl.ds(32, 32)], CORE, partner)

    def unpack(shard):
        pads = []
        for pair in range(8):
            pieces = [blocks[shard * 16 + 2 * pair + k].astype(F32) for k in range(2)]
            for k in range(tiles):
                rows = jnp.concatenate([piece[8 * k : 8 * k + 8] for piece in pieces], 0)
                begin = shard * length + k * LANES
                cubes[16 * pair : 16 * pair + 16, begin : begin + LANES] = rows.astype(BF16)
            pads += [piece[8 * tiles :] for piece in pieces]
        return jnp.concatenate(pads, 0)

    both = (((1,), (1,)), ((), ()))
    pads = unpack(0) + unpack(1)
    for z in range(8):
        half[z] = dot(cubes[:, : 2 * length], feat[z * LANES : (z + 1) * LANES, : 2 * length], both)
    came(CORE, blocks.at[pl.ds(32, 32)])
    pads = pads + unpack(2) + unpack(3)
    deriv = jnp.sum(pads, axis=1, keepdims=True)

    def block_of(z):
        rows = pl.ds(pl.multiple_of(z * LANES, LANES), LANES)
        columns = pl.ds(pl.multiple_of((at["l"] * 16 + z * 2 + at["c"]) * LANES, LANES), LANES)
        grad = half[z] + dot(cubes[:, 2 * length :], feat[rows, 2 * length :], both)
        return grad - deriv * vec[:, columns].astype(F32)

    for i, move in enumerate(RING):
        to = moved(at, move)
        grad_out[i] = block_of(to["z"]).astype(BF16)
        send(grad_out.at[i], grad_in.at[i], GRAD, device(to))
    for move in ELEC:
        send(waves.at[elec], waves.at[elec], WAVE, device(moved(at, move)))
    updated = block_of(at["z"])
    came(WAVE, waves.at[pl.ds(0, len(ELEC))])
    for pair in range(8):
        pieces = [waves[2 * pair + k].astype(F32) for k in range(2)]
        for k in range(tiles):
            rows = jnp.concatenate([piece[8 * k : 8 * k + 8] for piece in pieces], 0)
            sources[16 * pair : 16 * pair + 16, k * LANES : (k + 1) * LANES] = rows.astype(BF16)
    came(GRAD, grad_in)
    for i in range(len(RING)):
        updated = updated + grad_in[i].astype(F32)
    updated = updated * (1.0 / (length * 32))

    gram[...] = fine_gram(updated)
    mine = pl.ds(pl.multiple_of(brick_of(at) * 8, 8), 8)
    for i, move in enumerate(BRICK):
        to = moved(at, move)
        rows = pl.ds(pl.multiple_of(brick_of(to) * 8, 8), 8)
        send(gram.at[rows], gram_brick.at[i], GRAM1, device(to))
    total = gram[mine, :]
    came(GRAM1, gram_brick)
    for i in range(len(BRICK)):
        total = total + gram_brick[i]
    gram_sum[...] = total
    for i, move in enumerate(SHEET):
        send(gram_sum, gram_sheet.at[i], GRAM2, device(moved(at, move)))
    came(GRAM2, gram_sheet)
    for i in range(len(SHEET)):
        total = total + gram_sheet[i]
    gram_all[mine, :] = total
    for move in BRICK:
        send(gram_all.at[mine], gram_all.at[mine], GRAM3, device(moved(at, move)))
    came(GRAM3, gram_all.at[pl.ds(0, 8 * len(BRICK))])

    g = gram_all[...]
    row = lax.broadcasted_iota(jnp.int32, (LANES, LANES), 0)
    column = lax.broadcasted_iota(jnp.int32, (LANES, LANES), 1)
    unit = jnp.where(row == column, 1.0, 0.0)
    squares = jnp.sum(jnp.sum(g * unit, axis=1, keepdims=True), axis=0, keepdims=True)
    scale = START * math.sqrt(LANES) * lax.rsqrt(squares + 1e-06)
    g = g * scale * scale
    current = updated * scale
    for step in range(NS_STEPS):
        factor = 1.5 * unit - 0.5 * g
        current = fine_dot(factor, current)
        if step < NS_STEPS - 1:
            g = fine_dot(fine_dot(factor, g), factor)
    unmixing[...] = current

    left(TAIL, tail_in)
    left(FAR, far_in)
    left(LATE, late_in)
    left(SPILL, spill_in)
    left(CORE, blocks.at[pl.ds(32, 32)])
    left(WAVE, waves.at[pl.ds(0, len(ELEC))])
    left(GRAD, grad_in)
    left(GRAM1, gram_brick)
    left(GRAM2, gram_sheet)
    left(GRAM3, gram_all.at[pl.ds(0, 8 * len(BRICK))])


def shards(signals, vectors):
    channels, length = signals.shape
    count, columns = vectors.shape
    near, ring, part, brick, sheet = (len(group) for group in (ELEC, RING, PART, BRICK, SHEET))
    vmem = pl.BlockSpec(memory_space=pltpu.VMEM)
    return pl.pallas_call(
        kernel,
        out_shape=(
            jax.ShapeDtypeStruct((count, length), BF16),
            jax.ShapeDtypeStruct((count, LANES), F32),
        ),
        in_specs=[pl.BlockSpec(memory_space=pltpu.HBM)] * 2,
        out_specs=(vmem, vmem),
        scratch_shapes=[
            pltpu.VMEM((channels, length), BF16),
            pltpu.VMEM((count, columns), BF16),
            pltpu.VMEM((channels, length), F32),
            pltpu.VMEM((channels // 8, LANES), F32),
            pltpu.VMEM((channels // 8, LANES), F32),
            pltpu.VMEM((columns, length + LANES), BF16),
            pltpu.VMEM((part, 64, length), BF16),
            pltpu.VMEM((part, 64, length), BF16),
            pltpu.VMEM((part, 8, LANES), F32),
            pltpu.VMEM((part, 8, LANES), F32),
            pltpu.VMEM((8 * LANES, (part + 1) * length), BF16),
            pltpu.VMEM((count, length + LANES), F32),
            pltpu.VMEM((near, 8, length), F32),
            pltpu.VMEM((near + 1, LANES), F32),
            pltpu.VMEM((near + 1, LANES), F32),
            pltpu.VMEM(((part + 1) * (near + 1), 32, LANES), BF16),
            pltpu.VMEM((near + 1, 32, LANES), BF16),
            pltpu.VMEM((count, (part + 1) * length), BF16),
            pltpu.VMEM((8, count, LANES), F32),
            pltpu.VMEM((ring, count, LANES), BF16),
            pltpu.VMEM((ring, count, LANES), BF16),
            pltpu.VMEM((LANES, LANES), F32),
            pltpu.VMEM((brick, 8, LANES), F32),
            pltpu.VMEM((8, LANES), F32),
            pltpu.VMEM((sheet, 8, LANES), F32),
            pltpu.VMEM((LANES, LANES), F32),
            pltpu.SemaphoreType.DMA((2,)),
            pltpu.SemaphoreType.DMA((12,)),
            pltpu.SemaphoreType.DMA((12,)),
        ],
        compiler_params=pltpu.CompilerParams(
            collective_id=0, has_side_effects=True, vmem_limit_bytes=40 * 2**20
        ),
        cost_estimate=pl.CostEstimate(flops=10**9, bytes_accessed=2 * 10**6, transcendentals=0),
        name="separate",
    )(*[pltpu.with_memory_space_constraint(a, pltpu.HBM) for a in (signals, vectors)])


def solution(mesh):
    return jax.shard_map(
        shards,
        mesh=mesh,
        in_specs=(P("elec", "tm"), P(None, "elec")),
        out_specs=(P(None, "tm"), P(None, ("elec", "tm"))),
        check_vma=False,
    )
```

```python
import functools
import itertools
import math

import jax
import jax.numpy as jnp
from jax import lax
from jax.experimental import pallas as pl
from jax.experimental.pallas import tpu as pltpu
from jax.sharding import PartitionSpec as P

LAGS = 16
NS_STEPS = 6
START = 0.15
MESH = pl.DeviceIdType.MESH
SIZE = dict(x=4, h=4, l=2, z=8, c=2)
F32, BF16 = jnp.float32, jnp.bfloat16
LANES = 128


def hops(move):
    x, y, z = move.get("x", 0), 2 * move.get("h", 0) + move.get("l", 0), move.get("z", 0)
    return min(x, 4 - x) + min(y, 8 - y) + min(z, 8 - z)


def moves(*names):
    every = itertools.product(*[range(SIZE[name]) for name in names])
    found = [dict(zip(names, move)) for move in every if any(move)]
    return sorted(found, key=lambda move: -hops(move))


ELEC, PLANE, RING = moves("x", "h"), moves("x", "h", "l"), moves("z")
PART = [dict(l=1), dict(c=1), dict(l=1, c=1)]
ROW, SHEET = moves("x", "l"), moves("z", "h")


def unique(found):
    seen = {tuple(move.get(name, 0) for name in SIZE): None for move in found}
    return [dict(zip(SIZE, move)) for move in seen]


def place():
    elec, tm = lax.axis_index("elec"), lax.axis_index("tm")
    return dict(x=elec // 4, h=elec % 4, l=tm // 16, z=(tm // 2) % 8, c=tm % 2)


def moved(at, move):
    return {k: lax.rem(v + move.get(k, 0), SIZE[k]) for k, v in at.items()}


def elec_of(at):
    return at["x"] * 4 + at["h"]


def tm_of(at):
    return (at["l"] * 8 + at["z"]) * 2 + at["c"]


def row_of(at):
    return at["x"] * 2 + at["l"]


def device(at):
    return {"elec": elec_of(at), "tm": tm_of(at)}


def remote(src, dst, sems, step, to):
    return pltpu.make_async_remote_copy(
        src_ref=src,
        dst_ref=dst,
        send_sem=sems[0].at[step],
        recv_sem=sems[1].at[step],
        device_id=to,
        device_id_type=MESH,
    )


(TAIL, FAR, LATE, SUM, SPILL, CUBE, CROSS, CORE1, CORE2, WAVE, GRAD, GRAM1, GRAM2, GRAM3) = range(14)


def halves(a):
    top = a.astype(BF16)
    return top, (a - top.astype(F32)).astype(BF16)


def dot(a, b, dims=(((1,), (0,)), ((), ()))):
    return lax.dot_general(a, b, dims, preferred_element_type=F32)


def fine_dot(a, b):
    (a1, a2), (b1, b2) = halves(a), halves(b)
    return dot(jnp.concatenate([a1, a1, a2], 1), jnp.concatenate([b1, b2, b1], 0))


def fine_gram(a):
    a1, a2 = halves(a)
    both = (((1,), (1,)), ((), ()))
    return dot(jnp.concatenate([a1, a1, a2], 1), jnp.concatenate([a1, a2, a1], 1), both)


def lagged(row, shift=0):
    return pltpu.roll(jnp.broadcast_to(row, (LAGS, LANES)), shift, 1, stride=1, stride_axis=0)


def packed(tile, shift):
    return jnp.sum(pltpu.roll(tile, shift, 1, stride=LAGS, stride_axis=0), axis=0, keepdims=True)


def before_first(row, r):
    return lagged(row, (LANES - (r + 1) * LAGS) % LANES)


def kernel(
    sig_hbm, vec_hbm, sources, unmixing,
    sig, vec, wide, tail_out, tail_in, ext, far_out, far_in, late_out, late_in, feat,
    partial, summed, spill_out, spill_in, blocks, waves, cubes,
    half, grad_out, grad_in, gram, gram_row, gram_sum, gram_sheet, gram_all,
    load, sent, got,
):
    at = place()
    elec, tm = elec_of(at), tm_of(at)
    length = sig.shape[1]
    tiles = length // LANES
    after, before = lax.rem(tm + 1, 32), lax.rem(tm + 31, 32)

    loads = [
        pltpu.make_async_copy(sig_hbm, sig, load.at[0]),
        pltpu.make_async_copy(vec_hbm, vec, load.at[1]),
    ]
    for copy in loads:
        copy.start()
    sems = (sent, got)
    partner = device(moved(at, PART[1]))

    def send(src, dst, step, to):
        remote(src, dst, sems, step, to).start()

    def left(step, ref):
        remote(ref, ref, sems, step, partner).wait_send()

    def came(step, ref):
        remote(ref, ref, sems, step, partner).wait_recv()

    greeted = unique(PLANE + RING + PART)
    barrier = pltpu.get_barrier_semaphore()
    for move in ELEC + [{}]:
        other = {"elec": elec_of(moved(at, move)), "tm": before}
        pl.semaphore_signal(barrier, inc=1, device_id=other, device_id_type=MESH)
    for move in greeted:
        pl.semaphore_signal(barrier, inc=1, device_id=device(moved(at, move)), device_id_type=MESH)

    lane = lax.broadcasted_iota(jnp.int32, (LAGS, LANES), 1)
    late = lax.broadcasted_iota(jnp.int32, (LAGS, LANES), 0)
    spill = lane < late

    loads[0].wait()

    @pl.loop(0, 16)
    def _(block):
        rows = sig[pl.ds(block * 16, 16), :].astype(F32)
        for r in range(16):
            to = pl.ds((block * 16 + r) * LAGS, LAGS)
            turned = [lagged(rows[r : r + 1, k * LANES : (k + 1) * LANES]) for k in range(tiles)]
            for k, (a, b) in enumerate(zip([0.0] + turned, turned + [0.0])):
                ext[to, k * LANES : (k + 1) * LANES] = jnp.where(spill, a, b).astype(BF16)

    loads[1].wait()
    partial[...] = dot(vec[...], ext[...])
    spill_out[...] = jnp.concatenate([packed(partial[8 * k : 8 * k + 8, length:], 0) for k in range(16)], 0)
    pl.semaphore_wait(barrier, len(greeted) + len(ELEC) + 1)
    for i, move in enumerate(ELEC + [{}]):
        to = moved(at, move)
        rows = pl.ds(pl.multiple_of(elec_of(to) * 8, 8), 8)
        if move:
            send(partial.at[rows, pl.ds(0, length)], summed.at[i], SUM, device(to))
        over = {"elec": elec_of(to), "tm": after}
        send(spill_out.at[pl.ds(elec_of(to), 1)], spill_in.at[pl.ds(i, 1)], SPILL, over)
    wide[...] = sig[...].astype(F32)
    last = lax.broadcasted_iota(jnp.int32, (8, LANES), 1) >= LANES - LAGS
    tail_out[...] = jnp.concatenate(
        [
            packed(jnp.where(last, wide[8 * k : 8 * k + 8, length - LANES :], 0.0), LAGS)
            for k in range(wide.shape[0] // 8)
        ],
        0,
    )
    send(tail_out, tail_in, TAIL, {"elec": elec, "tm": after})

    def start_of(to, z):
        return to["l"] * 16 + z * 2 + to["c"]

    for i, move in enumerate(PART):
        to = moved(at, move)
        starts = [pl.multiple_of(start_of(to, z) * 8, 8) for z in range(8)]
        far_out[i] = jnp.concatenate([wide[pl.ds(start, 8), :] for start in starts], 0).astype(BF16)
    for z in range(8):
        own = pl.multiple_of(start_of(at, z) * LANES, LANES)
        feat[z * LANES : (z + 1) * LANES, :length] = ext[pl.ds(own, LANES), :length]
    left(SUM, summed)
    for i, move in enumerate(PART):
        send(far_out.at[i], far_in.at[i], FAR, device(moved(at, move)))
    came(TAIL, tail_in)
    first = jnp.where(tm > 0, 1.0, 0.0)
    for i, move in enumerate(PART):
        to = moved(at, move)
        late_out[i] = jnp.concatenate([tail_in[pl.ds(start_of(to, z), 1), :] for z in range(8)], 0) * first
        send(late_out.at[i], late_in.at[i], LATE, device(to))

    @pl.loop(0, 8)
    def _(z):
        row = tail_in[pl.ds(start_of(at, z), 1), :] * first
        for r in range(8):
            to = pl.ds((z * 8 + r) * LAGS, LAGS)
            feat[to, :LANES] = jnp.where(spill, before_first(row, r), feat[to, :LANES].astype(F32)).astype(BF16)

    mine = pl.ds(pl.multiple_of(elec * 8, 8), 8)
    total = partial[mine, :length]
    came(SUM, summed)
    came(SPILL, spill_in)
    for i in range(len(ELEC)):
        total = total + summed[i]
    over = jnp.sum(spill_in[...], axis=0, keepdims=True) * first
    over = jnp.concatenate([pltpu.roll(over, (LANES - r * LAGS) % LANES, 1) for r in range(8)], 0)
    over = jnp.where(lax.broadcasted_iota(jnp.int32, (8, LANES), 1) < LAGS, over, 0.0)
    total = jnp.concatenate([total[:, :LANES] + over, total[:, LANES:]], 1)

    def stacked(block, last):
        return jnp.concatenate([block[:, k * LANES : (k + 1) * LANES] for k in range(tiles)] + [last], 0).astype(BF16)

    deriv = jnp.sum(3.0 * total * total, axis=1, keepdims=True)
    high = deriv.astype(BF16).astype(F32)
    middle = (deriv - high).astype(BF16).astype(F32)
    low = deriv - high - middle
    lane = lax.broadcasted_iota(jnp.int32, (8, LANES), 1)
    pad = jnp.where(lane == 0, high, jnp.where(lane == 1, middle, jnp.where(lane == 2, low, 0.0)))
    blocks[elec] = stacked(total * total * total, pad)
    waves[elec] = stacked(total, jnp.zeros((8, LANES), F32))
    for move in ELEC:
        send(blocks.at[elec], blocks.at[elec], CUBE, device(moved(at, move)))
    for move in PLANE:
        if move["l"]:
            send(blocks.at[elec], blocks.at[elec + 16], CROSS, device(moved(at, move)))
    came(FAR, far_in)
    came(LATE, late_in)
    for i in range(len(PART)):

        @pl.loop(0, 4)
        def _(block):
            rows = far_in[i, pl.ds(block * 16, 16), :].astype(F32)
            ends = late_in[i, pl.ds(block * 2, 2), :]
            for r in range(16):
                to = pl.ds((block * 16 + r) * LAGS, LAGS)
                turned = [before_first(ends[r // 8 : r // 8 + 1], r % 8)]
                turned += [lagged(rows[r : r + 1, k * LANES : (k + 1) * LANES]) for k in range(tiles)]
                for k in range(tiles):
                    begin = (i + 1) * length + k * LANES
                    feat[to, begin : begin + LANES] = jnp.where(spill, turned[k], turned[k + 1]).astype(BF16)

    def unpack(shard):
        pads = []
        for pair in range(8):
            pieces = [blocks[shard * 16 + 2 * pair + k].astype(F32) for k in range(2)]
            for k in range(tiles):
                rows = jnp.concatenate([piece[8 * k : 8 * k + 8] for piece in pieces], 0)
                begin = shard * length + k * LANES
                cubes[16 * pair : 16 * pair + 16, begin : begin + LANES] = rows.astype(BF16)
            pads += [piece[8 * tiles :] for piece in pieces]
        return jnp.concatenate(pads, 0)

    both = (((1,), (1,)), ((), ()))
    came(CUBE, blocks.at[pl.ds(0, 15)])
    send(blocks.at[pl.ds(0, 16)], blocks.at[pl.ds(32, 16)], CORE1, partner)
    pads = unpack(0)
    came(CROSS, blocks.at[pl.ds(16, 16)])
    send(blocks.at[pl.ds(16, 16)], blocks.at[pl.ds(48, 16)], CORE2, partner)
    pads = pads + unpack(1)
    for z in range(8):
        half[z] = dot(cubes[:, : 2 * length], feat[z * LANES : (z + 1) * LANES, : 2 * length], both)
    came(CORE1, blocks.at[pl.ds(32, 16)])
    pads = pads + unpack(2)
    came(CORE2, blocks.at[pl.ds(48, 16)])
    pads = pads + unpack(3)
    deriv = jnp.sum(pads, axis=1, keepdims=True)

    def block_of(z):
        rows = pl.ds(pl.multiple_of(z * LANES, LANES), LANES)
        columns = pl.ds(pl.multiple_of((at["l"] * 16 + z * 2 + at["c"]) * LANES, LANES), LANES)
        grad = half[z] + dot(cubes[:, 2 * length :], feat[rows, 2 * length :], both)
        return grad - deriv * vec[:, columns].astype(F32)

    for i, move in enumerate(RING):
        to = moved(at, move)
        grad_out[i] = block_of(to["z"]).astype(BF16)
        send(grad_out.at[i], grad_in.at[i], GRAD, device(to))
    for move in ELEC:
        send(waves.at[elec], waves.at[elec], WAVE, device(moved(at, move)))
    updated = block_of(at["z"])
    came(WAVE, waves.at[pl.ds(0, len(ELEC))])
    for pair in range(8):
        pieces = [waves[2 * pair + k].astype(F32) for k in range(2)]
        for k in range(tiles):
            rows = jnp.concatenate([piece[8 * k : 8 * k + 8] for piece in pieces], 0)
            sources[16 * pair : 16 * pair + 16, k * LANES : (k + 1) * LANES] = rows.astype(BF16)
    came(GRAD, grad_in)
    for i in range(len(RING)):
        updated = updated + grad_in[i].astype(F32)
    updated = updated * (1.0 / (length * 32))

    gram[...] = fine_gram(updated)
    mine = pl.ds(pl.multiple_of(row_of(at) * 16, 16), 16)

    def scatter(move, slot):
        to = moved(at, move) | dict(c=1)
        rows = pl.ds(pl.multiple_of(row_of(to) * 16, 16), 16)
        send(gram.at[rows], gram_row.at[slot], GRAM1, device(to))

    for i, move in enumerate(ROW):
        scatter(move, i + 8 * at["c"])

    @pl.when(at["c"] == 0)
    def _():
        scatter({}, len(ROW))

    @pl.when(at["c"] == 1)
    def _():
        came(GRAM1, gram_row)
        total = gram[mine, :]
        for i in range(2 * len(ROW) + 1):
            total = total + gram_row[i]
        gram_sum[...] = total.astype(BF16)
        for i, move in enumerate(SHEET):
            send(gram_sum, gram_sheet.at[i], GRAM2, device(moved(at, move)))
        came(GRAM2, gram_sheet)
        total = gram_sum[...].astype(F32)
        for i in range(len(SHEET)):
            total = total + gram_sheet[i].astype(F32)
        gram_all[mine, :] = total
        for move in ROW + [{}]:
            send(gram_all.at[mine], gram_all.at[mine], GRAM3, device(moved(at, move) | dict(c=0)))
        for move in ROW:
            send(gram_all.at[mine], gram_all.at[mine], GRAM3, device(moved(at, move)))
        came(GRAM3, gram_all.at[pl.ds(0, 16 * len(ROW))])

    @pl.when(at["c"] == 0)
    def _():
        came(GRAM3, gram_all)

    g = gram_all[...]
    row = lax.broadcasted_iota(jnp.int32, (LANES, LANES), 0)
    column = lax.broadcasted_iota(jnp.int32, (LANES, LANES), 1)
    unit = jnp.where(row == column, 1.0, 0.0)
    squares = jnp.sum(jnp.sum(g * unit, axis=1, keepdims=True), axis=0, keepdims=True)
    scale = START * math.sqrt(LANES) * lax.rsqrt(squares + 1e-06)
    g = g * scale * scale
    current = updated * scale
    for step in range(NS_STEPS):
        factor = 1.5 * unit - 0.5 * g
        current = fine_dot(factor, current)
        if step < NS_STEPS - 1:
            g = fine_dot(fine_dot(factor, g), factor)
    unmixing[...] = current

    left(TAIL, tail_in)
    left(FAR, far_in)
    left(LATE, late_in)
    left(SPILL, spill_in)
    left(CUBE, blocks.at[pl.ds(0, 15)])
    left(CROSS, blocks.at[pl.ds(0, 16)])
    left(CORE1, blocks.at[pl.ds(0, 16)])
    left(CORE2, blocks.at[pl.ds(0, 16)])
    left(WAVE, waves.at[pl.ds(0, len(ELEC))])
    left(GRAD, grad_in)

    @pl.when(at["c"] == 0)
    def _():
        left(GRAM1, gram_all)

    @pl.when(at["c"] == 1)
    def _():
        left(GRAM1, gram_all.at[pl.ds(0, 16 * len(ROW))])
        left(GRAM2, gram_sheet)
        left(GRAM3, gram_row)


def shards(signals, vectors):
    channels, length = signals.shape
    count, columns = vectors.shape
    near, ring, part, row, sheet = (len(group) for group in (ELEC, RING, PART, ROW, SHEET))
    vmem = pl.BlockSpec(memory_space=pltpu.VMEM)
    return pl.pallas_call(
        kernel,
        out_shape=(
            jax.ShapeDtypeStruct((count, length), BF16),
            jax.ShapeDtypeStruct((count, LANES), F32),
        ),
        in_specs=[pl.BlockSpec(memory_space=pltpu.HBM)] * 2,
        out_specs=(vmem, vmem),
        scratch_shapes=[
            pltpu.VMEM((channels, length), BF16),
            pltpu.VMEM((count, columns), BF16),
            pltpu.VMEM((channels, length), F32),
            pltpu.VMEM((channels // 8, LANES), F32),
            pltpu.VMEM((channels // 8, LANES), F32),
            pltpu.VMEM((columns, length + LANES), BF16),
            pltpu.VMEM((part, 64, length), BF16),
            pltpu.VMEM((part, 64, length), BF16),
            pltpu.VMEM((part, 8, LANES), F32),
            pltpu.VMEM((part, 8, LANES), F32),
            pltpu.VMEM((8 * LANES, (part + 1) * length), BF16),
            pltpu.VMEM((count, length + LANES), F32),
            pltpu.VMEM((near, 8, length), F32),
            pltpu.VMEM((near + 1, LANES), F32),
            pltpu.VMEM((near + 1, LANES), F32),
            pltpu.VMEM(((part + 1) * (near + 1), 32, LANES), BF16),
            pltpu.VMEM((near + 1, 32, LANES), BF16),
            pltpu.VMEM((count, (part + 1) * length), BF16),
            pltpu.VMEM((8, count, LANES), F32),
            pltpu.VMEM((ring, count, LANES), BF16),
            pltpu.VMEM((ring, count, LANES), BF16),
            pltpu.VMEM((LANES, LANES), F32),
            pltpu.VMEM((2 * row + 1, 16, LANES), F32),
            pltpu.VMEM((16, LANES), BF16),
            pltpu.VMEM((sheet, 16, LANES), BF16),
            pltpu.VMEM((LANES, LANES), F32),
            pltpu.SemaphoreType.DMA((2,)),
            pltpu.SemaphoreType.DMA((14,)),
            pltpu.SemaphoreType.DMA((14,)),
        ],
        compiler_params=pltpu.CompilerParams(
            collective_id=0, has_side_effects=True, vmem_limit_bytes=40 * 2**20
        ),
        cost_estimate=pl.CostEstimate(flops=10**9, bytes_accessed=2 * 10**6, transcendentals=0),
        name="separate",
    )(*[pltpu.with_memory_space_constraint(a, pltpu.HBM) for a in (signals, vectors)])


def solution(mesh):
    return jax.shard_map(
        shards,
        mesh=mesh,
        in_specs=(P("elec", "tm"), P(None, "elec")),
        out_specs=(P(None, "tm"), P(None, ("elec", "tm"))),
        check_vma=False,
    )
```

```python
import functools
import itertools
import math

import jax
import jax.numpy as jnp
from jax import lax
from jax.experimental import pallas as pl
from jax.experimental.pallas import tpu as pltpu
from jax.sharding import PartitionSpec as P

LAGS = 16
NS_STEPS = 6
START = 0.15
MESH = pl.DeviceIdType.MESH
SIZE = dict(x=4, h=4, l=2, z=8, c=2)
F32, BF16 = jnp.float32, jnp.bfloat16
LANES = 128


def hops(move):
    x, y, z = move.get("x", 0), 2 * move.get("h", 0) + move.get("l", 0), move.get("z", 0)
    return min(x, 4 - x) + min(y, 8 - y) + min(z, 8 - z)


def moves(*names):
    every = itertools.product(*[range(SIZE[name]) for name in names])
    found = [dict(zip(names, move)) for move in every if any(move)]
    return sorted(found, key=lambda move: -hops(move))


ELEC, PLANE, RING = moves("x", "h"), moves("x", "h", "l"), moves("z")
PART = [dict(l=1), dict(c=1), dict(l=1, c=1)]
ROW, SHEET = moves("x", "l"), moves("z", "h")


def unique(found):
    seen = {tuple(move.get(name, 0) for name in SIZE): None for move in found}
    return [dict(zip(SIZE, move)) for move in seen]


def place():
    elec, tm = lax.axis_index("elec"), lax.axis_index("tm")
    return dict(x=elec >> 2, h=elec & 3, l=tm >> 4, z=(tm >> 1) & 7, c=tm & 1)


def moved(at, move):
    return {k: (v + move[k]) & (SIZE[k] - 1) if move.get(k, 0) else v for k, v in at.items()}


def elec_of(at):
    return at["x"] * 4 + at["h"]


def tm_of(at):
    return (at["l"] * 8 + at["z"]) * 2 + at["c"]


def row_of(at):
    return at["x"] * 2 + at["l"]


def device(at):
    return {"elec": elec_of(at), "tm": tm_of(at)}


def remote(src, dst, sems, step, to):
    return pltpu.make_async_remote_copy(
        src_ref=src,
        dst_ref=dst,
        send_sem=sems[0].at[step],
        recv_sem=sems[1].at[step],
        device_id=to,
        device_id_type=MESH,
    )


(TAIL, FAR, LATE, SUM, SPILL, CUBE1, CUBE2, CORE1, CORE2, WAVE, GRAD1, GRAD2, GRAM1, GRAM2, GRAM3) = range(15)


def halves(a):
    top = a.astype(BF16)
    return top, (a - top.astype(F32)).astype(BF16)


def dot(a, b, dims=(((1,), (0,)), ((), ()))):
    return lax.dot_general(a, b, dims, preferred_element_type=F32)


def fine_dot(a, b):
    (a1, a2), (b1, b2) = halves(a), halves(b)
    return dot(jnp.concatenate([a1, a1, a2], 1), jnp.concatenate([b1, b2, b1], 0))


def fine_gram(a):
    a1, a2 = halves(a)
    both = (((1,), (1,)), ((), ()))
    return dot(jnp.concatenate([a1, a1, a2], 1), jnp.concatenate([a1, a2, a1], 1), both)


def lagged(row, shift=0):
    return pltpu.roll(jnp.broadcast_to(row, (LAGS, LANES)), shift, 1, stride=1, stride_axis=0)


def packed(tile, shift):
    return jnp.sum(pltpu.roll(tile, shift, 1, stride=LAGS, stride_axis=0), axis=0, keepdims=True)


def before_first(row, r):
    return lagged(row, (LANES - (r + 1) * LAGS) % LANES)


def kernel(
    sig_hbm, vec_hbm, sources, unmixing,
    sig, vec, wide, tail_out, tail_in, ext, far_out, far_in, late_out, late_in, feat,
    partial, summed, spill_out, spill_in, blocks, waves, cubes,
    half, grad_out, grad_in, gram, gram_row, gram_sum, gram_sheet, gram_all,
    load, sent, got,
):
    at = place()
    elec, tm = elec_of(at), tm_of(at)
    length = sig.shape[1]
    tiles = length // LANES
    after, before = (tm + 1) & 31, (tm + 31) & 31

    loads = [
        pltpu.make_async_copy(sig_hbm, sig, load.at[0]),
        pltpu.make_async_copy(vec_hbm, vec, load.at[1]),
    ]
    for copy in loads:
        copy.start()
    sems = (sent, got)
    partner = device(moved(at, PART[1]))

    def send(src, dst, step, to):
        remote(src, dst, sems, step, to).start()

    def left(step, ref):
        remote(ref, ref, sems, step, partner).wait_send()

    def came(step, ref):
        remote(ref, ref, sems, step, partner).wait_recv()

    greeted = unique(PLANE + RING + PART)
    barrier = pltpu.get_barrier_semaphore()
    for move in ELEC + [{}]:
        other = {"elec": elec_of(moved(at, move)), "tm": before}
        pl.semaphore_signal(barrier, inc=1, device_id=other, device_id_type=MESH)
    for move in greeted:
        pl.semaphore_signal(barrier, inc=1, device_id=device(moved(at, move)), device_id_type=MESH)

    lane = lax.broadcasted_iota(jnp.int32, (LAGS, LANES), 1)
    late = lax.broadcasted_iota(jnp.int32, (LAGS, LANES), 0)
    spill = lane < late

    loads[0].wait()

    @pl.loop(0, 16)
    def _(block):
        rows = sig[pl.ds(block * 16, 16), :].astype(F32)
        for r in range(16):
            to = pl.ds((block * 16 + r) * LAGS, LAGS)
            turned = [lagged(rows[r : r + 1, k * LANES : (k + 1) * LANES]) for k in range(tiles)]
            for k, (a, b) in enumerate(zip([0.0] + turned, turned + [0.0])):
                ext[to, k * LANES : (k + 1) * LANES] = jnp.where(spill, a, b).astype(BF16)

    loads[1].wait()
    partial[...] = dot(vec[...], ext[...])
    spill_out[...] = jnp.concatenate([packed(partial[8 * k : 8 * k + 8, length:], 0) for k in range(16)], 0)
    pl.semaphore_wait(barrier, len(greeted) + len(ELEC) + 1)
    for x, h in itertools.product(range(4), (2, 1, 3, 0)):
        to = moved(at, dict(h=h)) | dict(x=x)
        slot = at["x"] * 4 + h
        rows = pl.ds(pl.multiple_of(elec_of(to) * 8, 8), 8)

        def send_sum():
            send(partial.at[rows, pl.ds(0, length)], summed.at[slot], SUM, device(to))

        if h:
            send_sum()
        else:
            pl.when(at["x"] != x)(send_sum)
        over = {"elec": elec_of(to), "tm": after}
        send(spill_out.at[pl.ds(elec_of(to), 1)], spill_in.at[pl.ds(slot, 1)], SPILL, over)
    wide[...] = sig[...].astype(F32)
    last = lax.broadcasted_iota(jnp.int32, (8, LANES), 1) >= LANES - LAGS
    tail_out[...] = jnp.concatenate(
        [
            packed(jnp.where(last, wide[8 * k : 8 * k + 8, length - LANES :], 0.0), LAGS)
            for k in range(wide.shape[0] // 8)
        ],
        0,
    )
    send(tail_out, tail_in, TAIL, {"elec": elec, "tm": after})

    def start_of(to, z):
        return to["l"] * 16 + z * 2 + to["c"]

    for i, move in enumerate(PART):
        to = moved(at, move)
        starts = [pl.multiple_of(start_of(to, z) * 8, 8) for z in range(8)]
        far_out[i] = jnp.concatenate([wide[pl.ds(start, 8), :] for start in starts], 0).astype(BF16)
    for z in range(8):
        own = pl.multiple_of(start_of(at, z) * LANES, LANES)
        feat[z * LANES : (z + 1) * LANES, :length] = ext[pl.ds(own, LANES), :length]
    left(SUM, summed.at[pl.ds(0, 15)])
    for i, move in enumerate(PART):
        send(far_out.at[i], far_in.at[i], FAR, device(moved(at, move)))
    came(TAIL, tail_in)
    first = jnp.where(tm > 0, 1.0, 0.0)
    for i, move in enumerate(PART):
        to = moved(at, move)
        late_out[i] = jnp.concatenate([tail_in[pl.ds(start_of(to, z), 1), :] for z in range(8)], 0) * first
        send(late_out.at[i], late_in.at[i], LATE, device(to))

    @pl.loop(0, 8)
    def _(z):
        row = tail_in[pl.ds(start_of(at, z), 1), :] * first
        for r in range(8):
            to = pl.ds((z * 8 + r) * LAGS, LAGS)
            feat[to, :LANES] = jnp.where(spill, before_first(row, r), feat[to, :LANES].astype(F32)).astype(BF16)

    mine = pl.ds(pl.multiple_of(elec * 8, 8), 8)
    summed[at["x"] * 4] = partial[mine, :length]
    came(SUM, summed.at[pl.ds(0, 15)])
    came(SPILL, spill_in)
    total = summed[0]
    for i in range(len(ELEC)):
        total = total + summed[i + 1]
    over = jnp.sum(spill_in[...], axis=0, keepdims=True) * first
    over = jnp.concatenate([pltpu.roll(over, (LANES - r * LAGS) % LANES, 1) for r in range(8)], 0)
    over = jnp.where(lax.broadcasted_iota(jnp.int32, (8, LANES), 1) < LAGS, over, 0.0)
    total = jnp.concatenate([total[:, :LANES] + over, total[:, LANES:]], 1)

    def stacked(block, last):
        return jnp.concatenate([block[:, k * LANES : (k + 1) * LANES] for k in range(tiles)] + [last], 0).astype(BF16)

    deriv = jnp.sum(3.0 * total * total, axis=1, keepdims=True)
    high = deriv.astype(BF16).astype(F32)
    middle = (deriv - high).astype(BF16).astype(F32)
    low = deriv - high - middle
    lane = lax.broadcasted_iota(jnp.int32, (8, LANES), 1)
    pad = jnp.where(lane == 0, high, jnp.where(lane == 1, middle, jnp.where(lane == 2, low, 0.0)))
    upper = at["x"] < 2
    own = (at["x"] >> 1) * 32 + (elec & 7)
    cube = CUBE1 + (at["x"] >> 1)
    blocks[own] = stacked(total * total * total, pad)
    waves[elec] = stacked(total, jnp.zeros((8, LANES), F32))
    for move in PLANE:
        send(blocks.at[own], blocks.at[own + 8 * move["l"]], cube, device(moved(at, move)))
    came(FAR, far_in)
    came(LATE, late_in)
    for i in range(len(PART)):

        @pl.loop(0, 4)
        def _(block):
            rows = far_in[i, pl.ds(block * 16, 16), :].astype(F32)
            ends = late_in[i, pl.ds(block * 2, 2), :]
            for r in range(16):
                to = pl.ds((block * 16 + r) * LAGS, LAGS)
                turned = [before_first(ends[r // 8 : r // 8 + 1], r % 8)]
                turned += [lagged(rows[r : r + 1, k * LANES : (k + 1) * LANES]) for k in range(tiles)]
                for k in range(tiles):
                    begin = (i + 1) * length + k * LANES
                    feat[to, begin : begin + LANES] = jnp.where(spill, turned[k], turned[k + 1]).astype(BF16)

    both = (((1,), (1,)), ((), ()))

    def unpack(part, shard):
        pads = []
        for pair in range(4):
            pieces = [blocks[part * 32 + shard * 8 + 2 * pair + k].astype(F32) for k in range(2)]
            for k in range(tiles):
                rows = jnp.concatenate([piece[8 * k : 8 * k + 8] for piece in pieces], 0)
                begin = shard * length + k * LANES
                cubes[64 * part + 16 * pair : 64 * part + 16 * pair + 16, begin : begin + LANES] = rows.astype(BF16)
            pads += [piece[8 * tiles :] for piece in pieces]
        return jnp.concatenate(pads, 0)

    own_grads = []
    for part in range(2):
        near, far = pl.ds(part * 32, 16), pl.ds(part * 32 + 16, 16)
        mixed = upper if part == 0 else jnp.logical_not(upper)

        @pl.when(mixed)
        def _():
            came(CUBE1 + part, blocks.at[pl.ds(0, 15)])

        @pl.when(jnp.logical_not(mixed))
        def _():
            came(CUBE1 + part, blocks.at[pl.ds(0, 16)])

        send(blocks.at[near], blocks.at[far], CORE1 + part, partner)
        these = slice(64 * part, 64 * part + 64)
        pads = unpack(part, 0) + unpack(part, 1)
        half[...] = dot(cubes[these, : 2 * length], feat[:, : 2 * length], both)
        came(CORE1 + part, blocks.at[far])
        pads = pads + unpack(part, 2) + unpack(part, 3)
        deriv = jnp.sum(pads, axis=1, keepdims=True)

        def block_of(z):
            rows = pl.ds(pl.multiple_of(z * LANES, LANES), LANES)
            columns = pl.ds(pl.multiple_of(start_of(at, z) * LANES, LANES), LANES)
            grad = half[:, rows] + dot(cubes[these, 2 * length :], feat[rows, 2 * length :], both)
            return grad - deriv * vec[these, columns].astype(F32)

        for i, move in enumerate(RING):
            to = moved(at, move)
            grad_out[part, i] = block_of(to["z"]).astype(BF16)
            send(grad_out.at[part, i], grad_in.at[part, i], GRAD1 + part, device(to))
        own_grads.append(block_of(at["z"]))
    for move in ELEC:
        send(waves.at[elec], waves.at[elec], WAVE, device(moved(at, move)))
    came(WAVE, waves.at[pl.ds(0, len(ELEC))])
    for pair in range(8):
        pieces = [waves[2 * pair + k].astype(F32) for k in range(2)]
        for k in range(tiles):
            rows = jnp.concatenate([piece[8 * k : 8 * k + 8] for piece in pieces], 0)
            sources[16 * pair : 16 * pair + 16, k * LANES : (k + 1) * LANES] = rows.astype(BF16)
    for part in range(2):
        came(GRAD1 + part, grad_in.at[part])
        for i in range(len(RING)):
            own_grads[part] = own_grads[part] + grad_in[part, i].astype(F32)
    updated = jnp.concatenate(own_grads, 0) * (1.0 / (length * 32))

    gram[...] = fine_gram(updated)
    mine = pl.ds(pl.multiple_of(row_of(at) * 16, 16), 16)

    def scatter(move, slot):
        to = moved(at, move) | dict(c=1)
        rows = pl.ds(pl.multiple_of(row_of(to) * 16, 16), 16)
        send(gram.at[rows], gram_row.at[slot], GRAM1, device(to))

    for i, move in enumerate(ROW):
        scatter(move, i + 8 * at["c"])

    @pl.when(at["c"] == 0)
    def _():
        scatter({}, len(ROW))

    @pl.when(at["c"] == 1)
    def _():
        came(GRAM1, gram_row)
        total = gram[mine, :]
        for i in range(2 * len(ROW) + 1):
            total = total + gram_row[i]
        gram_sum[...] = total.astype(BF16)
        for i, move in enumerate(SHEET):
            send(gram_sum, gram_sheet.at[i], GRAM2, device(moved(at, move)))
        came(GRAM2, gram_sheet)
        total = gram_sum[...].astype(F32)
        for i in range(len(SHEET)):
            total = total + gram_sheet[i].astype(F32)
        gram_all[mine, :] = total
        for move in ROW + [{}]:
            send(gram_all.at[mine], gram_all.at[mine], GRAM3, device(moved(at, move) | dict(c=0)))
        for move in ROW:
            send(gram_all.at[mine], gram_all.at[mine], GRAM3, device(moved(at, move)))
        came(GRAM3, gram_all.at[pl.ds(0, 16 * len(ROW))])

    @pl.when(at["c"] == 0)
    def _():
        came(GRAM3, gram_all)

    g = gram_all[...]
    row = lax.broadcasted_iota(jnp.int32, (LANES, LANES), 0)
    column = lax.broadcasted_iota(jnp.int32, (LANES, LANES), 1)
    unit = jnp.where(row == column, 1.0, 0.0)
    squares = jnp.sum(jnp.sum(g * unit, axis=1, keepdims=True), axis=0, keepdims=True)
    scale = START * math.sqrt(LANES) * lax.rsqrt(squares + 1e-06)
    g = g * scale * scale
    current = updated * scale
    for step in range(NS_STEPS):
        factor = 1.5 * unit - 0.5 * g
        current = fine_dot(factor, current)
        if step < NS_STEPS - 1:
            g = fine_dot(fine_dot(factor, g), factor)
    unmixing[...] = current

    left(TAIL, tail_in)
    left(FAR, far_in)
    left(LATE, late_in)
    left(SPILL, spill_in)
    left(cube, blocks.at[pl.ds(0, len(PLANE))])
    left(CORE1, blocks.at[pl.ds(0, 16)])
    left(CORE2, blocks.at[pl.ds(0, 16)])
    left(WAVE, waves.at[pl.ds(0, len(ELEC))])
    left(GRAD1, grad_in.at[0])
    left(GRAD2, grad_in.at[1])

    @pl.when(at["c"] == 0)
    def _():
        left(GRAM1, gram_all)

    @pl.when(at["c"] == 1)
    def _():
        left(GRAM1, gram_all.at[pl.ds(0, 16 * len(ROW))])
        left(GRAM2, gram_sheet)
        left(GRAM3, gram_row)


def shards(signals, vectors):
    channels, length = signals.shape
    count, columns = vectors.shape
    near, ring, part, row, sheet = (len(group) for group in (ELEC, RING, PART, ROW, SHEET))
    vmem = pl.BlockSpec(memory_space=pltpu.VMEM)
    return pl.pallas_call(
        kernel,
        out_shape=(
            jax.ShapeDtypeStruct((count, length), BF16),
            jax.ShapeDtypeStruct((count, LANES), F32),
        ),
        in_specs=[pl.BlockSpec(memory_space=pltpu.HBM)] * 2,
        out_specs=(vmem, vmem),
        scratch_shapes=[
            pltpu.VMEM((channels, length), BF16),
            pltpu.VMEM((count, columns), BF16),
            pltpu.VMEM((channels, length), F32),
            pltpu.VMEM((channels // 8, LANES), F32),
            pltpu.VMEM((channels // 8, LANES), F32),
            pltpu.VMEM((columns, length + LANES), BF16),
            pltpu.VMEM((part, 64, length), BF16),
            pltpu.VMEM((part, 64, length), BF16),
            pltpu.VMEM((part, 8, LANES), F32),
            pltpu.VMEM((part, 8, LANES), F32),
            pltpu.VMEM((8 * LANES, (part + 1) * length), BF16),
            pltpu.VMEM((count, length + LANES), F32),
            pltpu.VMEM((near + 1, 8, length), F32),
            pltpu.VMEM((near + 1, LANES), F32),
            pltpu.VMEM((near + 1, LANES), F32),
            pltpu.VMEM(((part + 1) * (near + 1), 32, LANES), BF16),
            pltpu.VMEM((near + 1, 32, LANES), BF16),
            pltpu.VMEM((count, (part + 1) * length), BF16),
            pltpu.VMEM((count // 2, 8 * LANES), F32),
            pltpu.VMEM((2, ring, count // 2, LANES), BF16),
            pltpu.VMEM((2, ring, count // 2, LANES), BF16),
            pltpu.VMEM((LANES, LANES), F32),
            pltpu.VMEM((2 * row + 1, 16, LANES), F32),
            pltpu.VMEM((16, LANES), BF16),
            pltpu.VMEM((sheet, 16, LANES), BF16),
            pltpu.VMEM((LANES, LANES), F32),
            pltpu.SemaphoreType.DMA((2,)),
            pltpu.SemaphoreType.DMA((15,)),
            pltpu.SemaphoreType.DMA((15,)),
        ],
        compiler_params=pltpu.CompilerParams(
            collective_id=0, has_side_effects=True, vmem_limit_bytes=40 * 2**20
        ),
        cost_estimate=pl.CostEstimate(flops=10**9, bytes_accessed=2 * 10**6, transcendentals=0),
        name="separate",
    )(*[pltpu.with_memory_space_constraint(a, pltpu.HBM) for a in (signals, vectors)])


def solution(mesh):
    return jax.shard_map(
        shards,
        mesh=mesh,
        in_specs=(P("elec", "tm"), P(None, "elec")),
        out_specs=(P(None, "tm"), P(None, ("elec", "tm"))),
        check_vma=False,
    )
```

```python
import functools
import itertools
import math

import jax
import jax.numpy as jnp
from jax import lax
from jax.experimental import pallas as pl
from jax.experimental.pallas import tpu as pltpu
from jax.sharding import PartitionSpec as P

LAGS = 16
NS_STEPS = 6
START = 0.15
MESH = pl.DeviceIdType.MESH
SIZE = dict(x=4, h=4, l=2, z=8, c=2)
F32, BF16 = jnp.float32, jnp.bfloat16
LANES = 128


def hops(move):
    x, y, z = move.get("x", 0), 2 * move.get("h", 0) + move.get("l", 0), move.get("z", 0)
    return min(x, 4 - x) + min(y, 8 - y) + min(z, 8 - z)


def moves(*names):
    every = itertools.product(*[range(SIZE[name]) for name in names])
    found = [dict(zip(names, move)) for move in every if any(move)]
    return sorted(found, key=lambda move: -hops(move))


ELEC, PLANE, RING = moves("x", "h"), moves("x", "h", "l"), moves("z")
PART = [dict(c=1), dict(l=1), dict(l=1, c=1)]
ROW, SHEET = moves("x", "l"), moves("z", "h")


def place():
    elec, tm = lax.axis_index("elec"), lax.axis_index("tm")
    return dict(x=elec >> 2, h=elec & 3, l=tm >> 4, z=(tm >> 1) & 7, c=tm & 1)


def moved(at, move):
    return {k: (v + move[k]) & (SIZE[k] - 1) if move.get(k, 0) else v for k, v in at.items()}


def elec_of(at):
    return at["x"] * 4 + at["h"]


def tm_of(at):
    return (at["l"] * 8 + at["z"]) * 2 + at["c"]


def row_of(at):
    return at["x"] * 2 + at["l"]


def device(at):
    return {"elec": elec_of(at), "tm": tm_of(at)}


def remote(src, dst, sems, step, to):
    return pltpu.make_async_remote_copy(
        src_ref=src,
        dst_ref=dst,
        send_sem=sems[0].at[step],
        recv_sem=sems[1].at[step],
        device_id=to,
        device_id_type=MESH,
    )


(TAIL, FAR, LATE, SUM, SPILL, CUBE, CROSS, CORE1, CORE2, WAVE, GRAD, GRAM1, GRAM2, GRAM3) = range(14)


def halves(a):
    top = a.astype(BF16)
    return top, (a - top.astype(F32)).astype(BF16)


def dot(a, b, dims=(((1,), (0,)), ((), ()))):
    return lax.dot_general(a, b, dims, preferred_element_type=F32)


def fine_dot(a, b):
    (a1, a2), (b1, b2) = halves(a), halves(b)
    return dot(jnp.concatenate([a1, a1, a2], 1), jnp.concatenate([b1, b2, b1], 0))


def fine_gram(a):
    a1, a2 = halves(a)
    both = (((1,), (1,)), ((), ()))
    return dot(jnp.concatenate([a1, a1, a2], 1), jnp.concatenate([a1, a2, a1], 1), both)


def lagged(row, shift=0):
    return pltpu.roll(jnp.broadcast_to(row, (LAGS, LANES)), shift, 1, stride=1, stride_axis=0)


def packed(tile, shift):
    return jnp.sum(pltpu.roll(tile, shift, 1, stride=LAGS, stride_axis=0), axis=0, keepdims=True)


def before_first(row, r):
    return lagged(row, (LANES - (r + 1) * LAGS) % LANES)


def kernel(
    sig_hbm, vec_hbm, sources, unmixing,
    sig, vec, wide, tail_out, tail_in, ext, far_out, far_in, late_out, late_in, feat,
    partial, summed, spill_out, spill_in, blocks, wave_out, waves, cubes,
    half, grad_out, grad_in, gram, gram_row, gram_sum, gram_sheet, gram_all,
    load, sent, got,
):
    at = place()
    elec, tm = elec_of(at), tm_of(at)
    length = sig.shape[1]
    tiles = length // LANES
    after, before = (tm + 1) & 31, (tm + 31) & 31
    core = at["c"]

    loads = [
        pltpu.make_async_copy(sig_hbm, sig, load.at[0]),
        pltpu.make_async_copy(vec_hbm, vec, load.at[1]),
    ]
    for copy in loads:
        copy.start()
    sems = (sent, got)
    partner = device(moved(at, dict(c=1)))

    def send(src, dst, step, to):
        remote(src, dst, sems, step, to).start()

    def left(step, ref):
        remote(ref, ref, sems, step, partner).wait_send()

    def came(step, ref):
        remote(ref, ref, sems, step, partner).wait_recv()

    barrier = pltpu.get_barrier_semaphore()

    def greet(to):
        pl.semaphore_signal(barrier, inc=1, device_id=to, device_id_type=MESH)

    @pl.when(core == 1)
    def _():
        for move in ELEC + [{}]:
            to = moved(at, move)
            greet({"elec": elec_of(to), "tm": (tm + 30) & 31})
            greet(device(to | dict(c=0)))
        for move in PLANE:
            greet(device(moved(at, move)))

    @pl.when(core == 0)
    def _():
        greet({"elec": elec, "tm": before})

    for move in RING + PART:
        greet(device(moved(at, move)))

    lane = lax.broadcasted_iota(jnp.int32, (LAGS, LANES), 1)
    late = lax.broadcasted_iota(jnp.int32, (LAGS, LANES), 0)
    spill = lane < late

    loads[0].wait()

    @pl.loop(0, 16)
    def _(block):
        rows = sig[pl.ds(block * 16, 16), :].astype(F32)
        for r in range(16):
            to = pl.ds((block * 16 + r) * LAGS, LAGS)
            turned = [lagged(rows[r : r + 1, k * LANES : (k + 1) * LANES]) for k in range(tiles)]
            for k, (a, b) in enumerate(zip([0.0] + turned, turned + [0.0])):
                ext[to, k * LANES : (k + 1) * LANES] = jnp.where(spill, a, b).astype(BF16)

    loads[1].wait()
    partial[...] = dot(vec[...], ext[...])
    spill_out[...] = jnp.concatenate([packed(partial[8 * k : 8 * k + 8, length:], 0) for k in range(16)], 0)
    every = len(RING) + len(PART) + len(ELEC) + 1

    @pl.when(core == 1)
    def _():
        pl.semaphore_wait(barrier, every + len(PLANE) + 1)

    @pl.when(core == 0)
    def _():
        pl.semaphore_wait(barrier, every)

    onward = (tm + 1 + core) & 31
    for i, move in enumerate(ELEC + [{}]):
        to = moved(at, move) | dict(c=1)
        rows = pl.ds(pl.multiple_of(elec_of(to) * 8, 8), 8)

        def send_sum():
            send(partial.at[rows, pl.ds(0, length)], summed.at[i + 16 * core], SUM, device(to))

        if move:
            send_sum()
        else:
            pl.when(core == 0)(send_sum)
        over = {"elec": elec_of(to), "tm": onward}
        send(spill_out.at[pl.ds(elec_of(to), 1)], spill_in.at[pl.ds(i + 16 * (1 - core), 1)], SPILL, over)
    wide[...] = sig[...].astype(F32)
    last = lax.broadcasted_iota(jnp.int32, (8, LANES), 1) >= LANES - LAGS
    tail_out[...] = jnp.concatenate(
        [
            packed(jnp.where(last, wide[8 * k : 8 * k + 8, length - LANES :], 0.0), LAGS)
            for k in range(wide.shape[0] // 8)
        ],
        0,
    )
    send(tail_out, tail_in, TAIL, {"elec": elec, "tm": after})

    def start_of(to, z):
        return to["l"] * 16 + z * 2 + to["c"]

    for i, move in enumerate(PART):
        to = moved(at, move)
        starts = [pl.multiple_of(start_of(to, z) * 8, 8) for z in range(8)]
        far_out[i] = jnp.concatenate([wide[pl.ds(start, 8), :] for start in starts], 0).astype(BF16)
    for z in range(8):
        own = pl.multiple_of(start_of(at, z) * LANES, LANES)
        feat[z * LANES : (z + 1) * LANES, :length] = ext[pl.ds(own, LANES), :length]

    @pl.when(core == 0)
    def _():
        left(SUM, summed.at[pl.ds(0, 16)])

    @pl.when(core == 1)
    def _():
        left(SUM, summed.at[pl.ds(0, 15)])

    for i, move in enumerate(PART):
        send(far_out.at[i], far_in.at[i], FAR, device(moved(at, move)))
    came(TAIL, tail_in)
    first = jnp.where(tm > 0, 1.0, 0.0)
    for i, move in enumerate(PART):
        to = moved(at, move)
        late_out[i] = jnp.concatenate([tail_in[pl.ds(start_of(to, z), 1), :] for z in range(8)], 0) * first
        send(late_out.at[i], late_in.at[i], LATE, device(to))

    @pl.loop(0, 8)
    def _(z):
        row = tail_in[pl.ds(start_of(at, z), 1), :] * first
        for r in range(8):
            to = pl.ds((z * 8 + r) * LAGS, LAGS)
            feat[to, :LANES] = jnp.where(spill, before_first(row, r), feat[to, :LANES].astype(F32)).astype(BF16)

    def stacked(block, last):
        return jnp.concatenate([block[:, k * LANES : (k + 1) * LANES] for k in range(tiles)] + [last], 0).astype(BF16)

    @pl.when(core == 1)
    def _():
        mine = pl.ds(pl.multiple_of(elec * 8, 8), 8)
        lane = lax.broadcasted_iota(jnp.int32, (8, LANES), 1)
        came(SUM, summed)
        came(SPILL, spill_in)
        for shard in range(2):
            total = summed[15] if shard == 0 else partial[mine, :length]
            for i in range(len(ELEC)):
                total = total + summed[i + 16 * shard]
            over = jnp.sum(spill_in[16 * shard : 16 * shard + 16], axis=0, keepdims=True)
            if shard == 0:
                over = over * jnp.where(tm > 1, 1.0, 0.0)
            over = jnp.concatenate([pltpu.roll(over, (LANES - r * LAGS) % LANES, 1) for r in range(8)], 0)
            over = jnp.where(lane < LAGS, over, 0.0)
            total = jnp.concatenate([total[:, :LANES] + over, total[:, LANES:]], 1)
            deriv = jnp.sum(3.0 * total * total, axis=1, keepdims=True)
            high = deriv.astype(BF16).astype(F32)
            middle = (deriv - high).astype(BF16).astype(F32)
            low = deriv - high - middle
            pad = jnp.where(lane == 0, high, jnp.where(lane == 1, middle, jnp.where(lane == 2, low, 0.0)))
            blocks[2 * elec + shard] = stacked(total * total * total, pad)
            wave_out[shard] = stacked(total, jnp.zeros((8, LANES), F32))
        own = pl.ds(2 * elec, 2)
        for move in ELEC:
            send(blocks.at[own], blocks.at[own], CUBE, device(moved(at, move)))
        for move in PLANE:
            if move["l"]:
                send(blocks.at[own], blocks.at[pl.ds(2 * elec + 32, 2)], CROSS, device(moved(at, move)))
        waves[elec] = wave_out[1]

    came(FAR, far_in)
    came(LATE, late_in)
    for i in range(len(PART)):

        @pl.loop(0, 4)
        def _(block):
            rows = far_in[i, pl.ds(block * 16, 16), :].astype(F32)
            ends = late_in[i, pl.ds(block * 2, 2), :]
            for r in range(16):
                to = pl.ds((block * 16 + r) * LAGS, LAGS)
                turned = [before_first(ends[r // 8 : r // 8 + 1], r % 8)]
                turned += [lagged(rows[r : r + 1, k * LANES : (k + 1) * LANES]) for k in range(tiles)]
                for k in range(tiles):
                    begin = (i + 1) * length + k * LANES
                    feat[to, begin : begin + LANES] = jnp.where(spill, turned[k], turned[k + 1]).astype(BF16)

    def unpack(shard):
        begin_at = 32 * (shard // 2) + (1 - core if shard % 2 else core)
        pads = []
        for pair in range(8):
            pieces = [blocks[begin_at + 2 * (2 * pair + k)].astype(F32) for k in range(2)]
            for k in range(tiles):
                rows = jnp.concatenate([piece[8 * k : 8 * k + 8] for piece in pieces], 0)
                begin = shard * length + k * LANES
                cubes[16 * pair : 16 * pair + 16, begin : begin + LANES] = rows.astype(BF16)
            pads += [piece[8 * tiles :] for piece in pieces]
        return jnp.concatenate(pads, 0)

    both = (((1,), (1,)), ((), ()))
    near, far = pl.ds(0, 32), pl.ds(32, 32)

    @pl.when(core == 1)
    def _():
        came(CUBE, blocks.at[pl.ds(0, 30)])
        send(blocks.at[near], blocks.at[near], CORE1, partner)

    @pl.when(core == 0)
    def _():
        came(CORE1, blocks.at[near])

    pads = unpack(0) + unpack(1)
    for z in range(8):
        half[z] = dot(cubes[:, : 2 * length], feat[z * LANES : (z + 1) * LANES, : 2 * length], both)

    @pl.when(core == 1)
    def _():
        came(CROSS, blocks.at[far])
        send(blocks.at[far], blocks.at[far], CORE2, partner)

    @pl.when(core == 0)
    def _():
        came(CORE2, blocks.at[far])

    pads = pads + unpack(2) + unpack(3)
    deriv = jnp.sum(pads, axis=1, keepdims=True)

    def block_of(z):
        rows = pl.ds(pl.multiple_of(z * LANES, LANES), LANES)
        columns = pl.ds(pl.multiple_of((at["l"] * 16 + z * 2 + at["c"]) * LANES, LANES), LANES)
        grad = half[z] + dot(cubes[:, 2 * length :], feat[rows, 2 * length :], both)
        return grad - deriv * vec[:, columns].astype(F32)

    for i, move in enumerate(RING):
        to = moved(at, move)
        grad_out[i] = block_of(to["z"]).astype(BF16)
        send(grad_out.at[i], grad_in.at[i], GRAD, device(to))

    @pl.when(core == 1)
    def _():
        for move in ELEC + [{}]:
            send(wave_out.at[0], waves.at[elec], WAVE, device(moved(at, move) | dict(c=0)))
        for move in ELEC:
            send(wave_out.at[1], waves.at[elec], WAVE, device(moved(at, move)))

    updated = block_of(at["z"])

    @pl.when(core == 0)
    def _():
        came(WAVE, waves)

    @pl.when(core == 1)
    def _():
        came(WAVE, waves.at[pl.ds(0, len(ELEC))])

    for pair in range(8):
        pieces = [waves[2 * pair + k].astype(F32) for k in range(2)]
        for k in range(tiles):
            rows = jnp.concatenate([piece[8 * k : 8 * k + 8] for piece in pieces], 0)
            sources[16 * pair : 16 * pair + 16, k * LANES : (k + 1) * LANES] = rows.astype(BF16)
    came(GRAD, grad_in)
    for i in range(len(RING)):
        updated = updated + grad_in[i].astype(F32)
    updated = updated * (1.0 / (length * 32))

    gram[...] = fine_gram(updated)
    mine = pl.ds(pl.multiple_of(row_of(at) * 16, 16), 16)

    def scatter(move, slot):
        to = moved(at, move) | dict(c=1)
        rows = pl.ds(pl.multiple_of(row_of(to) * 16, 16), 16)
        send(gram.at[rows], gram_row.at[slot], GRAM1, device(to))

    for i, move in enumerate(ROW):
        scatter(move, i + 8 * core)

    @pl.when(core == 0)
    def _():
        scatter({}, len(ROW))

    @pl.when(core == 1)
    def _():
        came(GRAM1, gram_row)
        total = gram[mine, :]
        for i in range(2 * len(ROW) + 1):
            total = total + gram_row[i]
        gram_sum[...] = total.astype(BF16)
        for i, move in enumerate(SHEET):
            send(gram_sum, gram_sheet.at[i], GRAM2, device(moved(at, move)))
        came(GRAM2, gram_sheet)
        total = gram_sum[...].astype(F32)
        for i in range(len(SHEET)):
            total = total + gram_sheet[i].astype(F32)
        gram_all[mine, :] = total
        for move in ROW + [{}]:
            send(gram_all.at[mine], gram_all.at[mine], GRAM3, device(moved(at, move) | dict(c=0)))
        for move in ROW:
            send(gram_all.at[mine], gram_all.at[mine], GRAM3, device(moved(at, move)))
        came(GRAM3, gram_all.at[pl.ds(0, 16 * len(ROW))])

    @pl.when(core == 0)
    def _():
        came(GRAM3, gram_all)

    g = gram_all[...]
    row = lax.broadcasted_iota(jnp.int32, (LANES, LANES), 0)
    column = lax.broadcasted_iota(jnp.int32, (LANES, LANES), 1)
    unit = jnp.where(row == column, 1.0, 0.0)
    squares = jnp.sum(jnp.sum(g * unit, axis=1, keepdims=True), axis=0, keepdims=True)
    scale = START * math.sqrt(LANES) * lax.rsqrt(squares + 1e-06)
    g = g * scale * scale
    current = updated * scale
    for step in range(NS_STEPS):
        factor = 1.5 * unit - 0.5 * g
        current = fine_dot(factor, current)
        if step < NS_STEPS - 1:
            g = fine_dot(fine_dot(factor, g), factor)
    unmixing[...] = current

    left(TAIL, tail_in)
    left(FAR, far_in)
    left(LATE, late_in)
    left(SPILL, spill_out)
    left(GRAD, grad_in)

    @pl.when(core == 0)
    def _():
        left(GRAM1, gram_all)

    @pl.when(core == 1)
    def _():
        left(GRAM1, gram_all.at[pl.ds(0, 16 * len(ROW))])
        left(GRAM2, gram_sheet)
        left(GRAM3, gram_row)
        left(CUBE, blocks.at[pl.ds(0, 30)])
        left(CROSS, blocks.at[pl.ds(0, 32)])
        left(CORE1, blocks.at[pl.ds(0, 32)])
        left(CORE2, blocks.at[pl.ds(0, 32)])
        left(WAVE, blocks.at[pl.ds(0, 31)])


def shards(signals, vectors):
    channels, length = signals.shape
    count, columns = vectors.shape
    near, ring, part, row, sheet = (len(group) for group in (ELEC, RING, PART, ROW, SHEET))
    vmem = pl.BlockSpec(memory_space=pltpu.VMEM)
    return pl.pallas_call(
        kernel,
        out_shape=(
            jax.ShapeDtypeStruct((count, length), BF16),
            jax.ShapeDtypeStruct((count, LANES), F32),
        ),
        in_specs=[pl.BlockSpec(memory_space=pltpu.HBM)] * 2,
        out_specs=(vmem, vmem),
        scratch_shapes=[
            pltpu.VMEM((channels, length), BF16),
            pltpu.VMEM((count, columns), BF16),
            pltpu.VMEM((channels, length), F32),
            pltpu.VMEM((channels // 8, LANES), F32),
            pltpu.VMEM((channels // 8, LANES), F32),
            pltpu.VMEM((columns, length + LANES), BF16),
            pltpu.VMEM((part, 64, length), BF16),
            pltpu.VMEM((part, 64, length), BF16),
            pltpu.VMEM((part, 8, LANES), F32),
            pltpu.VMEM((part, 8, LANES), F32),
            pltpu.VMEM((8 * LANES, (part + 1) * length), BF16),
            pltpu.VMEM((count, length + LANES), F32),
            pltpu.VMEM((2 * near + 1, 8, length), F32),
            pltpu.VMEM((near + 1, LANES), F32),
            pltpu.VMEM((2 * near + 2, LANES), F32),
            pltpu.VMEM(((part + 1) * (near + 1), 32, LANES), BF16),
            pltpu.VMEM((2, 32, LANES), BF16),
            pltpu.VMEM((near + 1, 32, LANES), BF16),
            pltpu.VMEM((count, (part + 1) * length), BF16),
            pltpu.VMEM((8, count, LANES), F32),
            pltpu.VMEM((ring, count, LANES), BF16),
            pltpu.VMEM((ring, count, LANES), BF16),
            pltpu.VMEM((LANES, LANES), F32),
            pltpu.VMEM((2 * row + 1, 16, LANES), F32),
            pltpu.VMEM((16, LANES), BF16),
            pltpu.VMEM((sheet, 16, LANES), BF16),
            pltpu.VMEM((LANES, LANES), F32),
            pltpu.SemaphoreType.DMA((2,)),
            pltpu.SemaphoreType.DMA((14,)),
            pltpu.SemaphoreType.DMA((14,)),
        ],
        compiler_params=pltpu.CompilerParams(
            collective_id=0, has_side_effects=True, vmem_limit_bytes=40 * 2**20
        ),
        cost_estimate=pl.CostEstimate(flops=10**9, bytes_accessed=2 * 10**6, transcendentals=0),
        name="separate",
    )(*[pltpu.with_memory_space_constraint(a, pltpu.HBM) for a in (signals, vectors)])


def solution(mesh):
    return jax.shard_map(
        shards,
        mesh=mesh,
        in_specs=(P("elec", "tm"), P(None, "elec")),
        out_specs=(P(None, "tm"), P(None, ("elec", "tm"))),
        check_vma=False,
    )
```

```python
import functools
import itertools
import math

import jax
import jax.numpy as jnp
from jax import lax
from jax.experimental import pallas as pl
from jax.experimental.pallas import tpu as pltpu
from jax.sharding import PartitionSpec as P

LAGS = 16
NS_STEPS = 6
START = 0.15
MESH = pl.DeviceIdType.MESH
SIZE = dict(x=4, h=4, l=2, z=8, c=2)
F32, BF16 = jnp.float32, jnp.bfloat16
LANES = 128


def hops(move):
    x, y, z = move.get("x", 0), 2 * move.get("h", 0) + move.get("l", 0), move.get("z", 0)
    return min(x, 4 - x) + min(y, 8 - y) + min(z, 8 - z)


def moves(*names):
    every = itertools.product(*[range(SIZE[name]) for name in names])
    found = [dict(zip(names, move)) for move in every if any(move)]
    return sorted(found, key=lambda move: -hops(move))


ELEC, PLANE, RING = moves("x", "h"), moves("x", "h", "l"), moves("z")
ROW, SHEET = moves("x", "l"), moves("z", "h")


def place():
    elec, tm = lax.axis_index("elec"), lax.axis_index("tm")
    return dict(x=elec >> 2, h=elec & 3, l=tm >> 4, z=(tm >> 1) & 7, c=tm & 1)


def moved(at, move):
    return {k: (v + move[k]) & (SIZE[k] - 1) if move.get(k, 0) else v for k, v in at.items()}


def elec_of(at):
    return at["x"] * 4 + at["h"]


def tm_of(at):
    return (at["l"] * 8 + at["z"]) * 2 + at["c"]


def row_of(at):
    return at["x"] * 2 + at["l"]


def device(at):
    return {"elec": elec_of(at), "tm": tm_of(at)}


def remote(src, dst, sems, step, to):
    return pltpu.make_async_remote_copy(
        src_ref=src,
        dst_ref=dst,
        send_sem=sems[0].at[step],
        recv_sem=sems[1].at[step],
        device_id=to,
        device_id_type=MESH,
    )


(TAIL, FAR, LATE, SUM, SPILL, CUBE, CROSS, WAVE, GRAD, FRESH, GRAM1, GRAM2, GRAM3) = range(13)


def halves(a):
    top = a.astype(BF16)
    return top, (a - top.astype(F32)).astype(BF16)


def dot(a, b, dims=(((1,), (0,)), ((), ()))):
    return lax.dot_general(a, b, dims, preferred_element_type=F32)


def fine_dot(a, b):
    (a1, a2), (b1, b2) = halves(a), halves(b)
    return dot(jnp.concatenate([a1, a1, a2], 1), jnp.concatenate([b1, b2, b1], 0))


def fine_gram(a):
    a1, a2 = halves(a)
    both = (((1,), (1,)), ((), ()))
    return dot(jnp.concatenate([a1, a1, a2], 1), jnp.concatenate([a1, a2, a1], 1), both)


def lagged(row, shift=0):
    return pltpu.roll(jnp.broadcast_to(row, (LAGS, LANES)), shift, 1, stride=1, stride_axis=0)


def packed(tile, shift):
    return jnp.sum(pltpu.roll(tile, shift, 1, stride=LAGS, stride_axis=0), axis=0, keepdims=True)


def before_first(row, r):
    return lagged(row, (LANES - (r + 1) * LAGS) % LANES)


def kernel(
    sig_hbm, vec_hbm, sources, unmixing,
    sig, vec, tail_out, tail_in, ext, far_in, late_in, feat,
    partial, summed, spill_out, spill_in, blocks, wave_out, waves, cubes,
    half, grad_out, grad_in, fresh_out, fresh, gram, gram_row, gram_sum, gram_sheet, gram_all,
    load, sent, got,
):
    at = place()
    elec, tm = elec_of(at), tm_of(at)
    length = sig.shape[1]
    tiles = length // LANES
    after, before = (tm + 1) & 31, (tm + 31) & 31
    core = at["c"]

    loads = [
        pltpu.make_async_copy(sig_hbm, sig, load.at[0]),
        pltpu.make_async_copy(vec_hbm, vec, load.at[1]),
    ]
    for copy in loads:
        copy.start()
    sems = (sent, got)
    partner = device(moved(at, dict(c=1)))

    def send(src, dst, step, to):
        remote(src, dst, sems, step, to).start()

    def left(step, ref):
        remote(ref, ref, sems, step, partner).wait_send()

    def came(step, ref):
        remote(ref, ref, sems, step, partner).wait_recv()

    barrier = pltpu.get_barrier_semaphore()

    def greet(to):
        pl.semaphore_signal(barrier, inc=1, device_id=to, device_id_type=MESH)

    @pl.when(core == 1)
    def _():
        for move in ELEC + [{}]:
            to = moved(at, move)
            greet({"elec": elec_of(to), "tm": (tm + 30) & 31})
            greet(device(to | dict(c=0)))
        for move in PLANE + RING:
            greet(device(moved(at, move)))
        greet(device(moved(at, dict(l=1, c=1))))

    @pl.when(core == 0)
    def _():
        greet({"elec": elec, "tm": before})

    lane = lax.broadcasted_iota(jnp.int32, (LAGS, LANES), 1)
    late = lax.broadcasted_iota(jnp.int32, (LAGS, LANES), 0)
    spill = lane < late

    loads[0].wait()

    @pl.loop(0, 16)
    def _(block):
        rows = sig[pl.ds(block * 16, 16), :].astype(F32)
        for r in range(16):
            to = pl.ds((block * 16 + r) * LAGS, LAGS)
            turned = [lagged(rows[r : r + 1, k * LANES : (k + 1) * LANES]) for k in range(tiles)]
            for k, (a, b) in enumerate(zip([0.0] + turned, turned + [0.0])):
                ext[to, k * LANES : (k + 1) * LANES] = jnp.where(spill, a, b).astype(BF16)

    loads[1].wait()
    partial[...] = dot(vec[...], ext[...])
    spill_out[...] = jnp.concatenate([packed(partial[8 * k : 8 * k + 8, length:], 0) for k in range(16)], 0)

    @pl.when(core == 1)
    def _():
        pl.semaphore_wait(barrier, len(ELEC) + 1 + len(PLANE) + len(RING) + 1)

    @pl.when(core == 0)
    def _():
        pl.semaphore_wait(barrier, len(ELEC) + 2)

    onward = (tm + 1 + core) & 31
    for i, move in enumerate(ELEC + [{}]):
        to = moved(at, move) | dict(c=1)
        rows = pl.ds(pl.multiple_of(elec_of(to) * 8, 8), 8)

        def send_sum():
            send(partial.at[rows, pl.ds(0, length)], summed.at[i + 16 * core], SUM, device(to))

        if move:
            send_sum()
        else:
            pl.when(core == 0)(send_sum)
        over = {"elec": elec_of(to), "tm": onward}
        send(spill_out.at[pl.ds(elec_of(to), 1)], spill_in.at[pl.ds(i + 16 * (1 - core), 1)], SPILL, over)
    last = lax.broadcasted_iota(jnp.int32, (8, LANES), 1) >= LANES - LAGS
    ends = sig[:, length - LANES :].astype(F32)
    tail_out[...] = jnp.concatenate(
        [packed(jnp.where(last, ends[8 * k : 8 * k + 8], 0.0), LAGS) for k in range(ends.shape[0] // 8)], 0
    )
    send(tail_out, tail_in, TAIL, {"elec": elec, "tm": after})

    other = moved(at, dict(l=1)) | dict(c=1)
    here = pl.ds(pl.multiple_of(at["l"] * 128, 128), 128)
    there = pl.ds(pl.multiple_of(other["l"] * 128, 128), 128)

    @pl.when(core == 0)
    def _():
        left(SUM, summed.at[pl.ds(0, 16)])
        send(sig.at[here], far_in.at[0], FAR, partner)

    @pl.when(core == 1)
    def _():
        left(SUM, summed.at[pl.ds(0, 15)])

    send(sig.at[there], far_in.at[2 - core], FAR, device(other))
    came(TAIL, tail_in)

    @pl.when((core == 0) & (tm == 0))
    def _():
        tail_in[...] = jnp.zeros_like(tail_in)

    here_ends = pl.ds(pl.multiple_of(at["l"] * 16, 16), 16)
    there_ends = pl.ds(pl.multiple_of(other["l"] * 16, 16), 16)

    @pl.when(core == 0)
    def _():
        send(tail_in.at[here_ends], late_in.at[0], LATE, partner)

    send(tail_in.at[there_ends], late_in.at[2 - core], LATE, device(other))

    def stacked(block, last):
        return jnp.concatenate([block[:, k * LANES : (k + 1) * LANES] for k in range(tiles)] + [last], 0).astype(BF16)

    @pl.when(core == 1)
    def _():
        mine = pl.ds(pl.multiple_of(elec * 8, 8), 8)
        lane = lax.broadcasted_iota(jnp.int32, (8, LANES), 1)
        came(SUM, summed)
        came(SPILL, spill_in)
        for shard in range(2):
            total = summed[15] if shard == 0 else partial[mine, :length]
            for i in range(len(ELEC)):
                total = total + summed[i + 16 * shard]
            over = jnp.sum(spill_in[16 * shard : 16 * shard + 16], axis=0, keepdims=True)
            if shard == 0:
                over = over * jnp.where(tm > 1, 1.0, 0.0)
            over = jnp.concatenate([pltpu.roll(over, (LANES - r * LAGS) % LANES, 1) for r in range(8)], 0)
            over = jnp.where(lane < LAGS, over, 0.0)
            total = jnp.concatenate([total[:, :LANES] + over, total[:, LANES:]], 1)
            deriv = jnp.sum(3.0 * total * total, axis=1, keepdims=True)
            high = deriv.astype(BF16).astype(F32)
            middle = (deriv - high).astype(BF16).astype(F32)
            low = deriv - high - middle
            pad = jnp.where(lane == 0, high, jnp.where(lane == 1, middle, jnp.where(lane == 2, low, 0.0)))
            blocks[2 * elec + shard] = stacked(total * total * total, pad)
            wave_out[shard] = stacked(total, jnp.zeros((8, LANES), F32))
        own = pl.ds(2 * elec, 2)
        for move in ELEC:
            send(blocks.at[own], blocks.at[own], CUBE, device(moved(at, move)))
        for move in PLANE:
            if move["l"]:
                send(blocks.at[own], blocks.at[pl.ds(2 * elec + 32, 2)], CROSS, device(moved(at, move)))
        waves[elec] = wave_out[1]

    both = (((1,), (1,)), ((), ()))

    def unpack(shard):
        begin_at = 32 * (shard // 2) + 1 - shard % 2
        pads = []
        for pair in range(8):
            pieces = [blocks[begin_at + 2 * (2 * pair + k)].astype(F32) for k in range(2)]
            for k in range(tiles):
                rows = jnp.concatenate([piece[8 * k : 8 * k + 8] for piece in pieces], 0)
                begin = shard * length + k * LANES
                cubes[16 * pair : 16 * pair + 16, begin : begin + LANES] = rows.astype(BF16)
            pads += [piece[8 * tiles :] for piece in pieces]
        return jnp.concatenate(pads, 0)

    @pl.when(core == 1)
    def _():
        feat[:, :length] = ext[pl.ds(pl.multiple_of(at["l"] * 2048, 2048), 2048), :length]

        @pl.loop(0, 8)
        def _(block):
            ends = tail_in[pl.ds(at["l"] * 16 + block * 2, 2), :]
            for r in range(16):
                to = pl.ds((block * 16 + r) * LAGS, LAGS)
                turned = before_first(ends[r // 8 : r // 8 + 1], r % 8)
                feat[to, :LANES] = jnp.where(spill, turned, feat[to, :LANES].astype(F32)).astype(BF16)

        came(FAR, far_in)
        came(LATE, late_in)
        for i in range(3):

            @pl.loop(0, 8)
            def _(block):
                rows = far_in[i, pl.ds(block * 16, 16), :].astype(F32)
                ends = late_in[i, pl.ds(block * 2, 2), :]
                for r in range(16):
                    to = pl.ds((block * 16 + r) * LAGS, LAGS)
                    turned = [before_first(ends[r // 8 : r // 8 + 1], r % 8)]
                    turned += [lagged(rows[r : r + 1, k * LANES : (k + 1) * LANES]) for k in range(tiles)]
                    for k in range(tiles):
                        begin = (i + 1) * length + k * LANES
                        feat[to, begin : begin + LANES] = jnp.where(spill, turned[k], turned[k + 1]).astype(BF16)

        came(CUBE, blocks.at[pl.ds(0, 30)])
        pads = unpack(0) + unpack(1)
        for z in range(8):
            half[z] = dot(cubes[:, : 2 * length], feat[z * 256 : z * 256 + 256, : 2 * length], both)
        came(CROSS, blocks.at[pl.ds(32, 32)])
        pads = pads + unpack(2) + unpack(3)
        deriv = jnp.sum(pads, axis=1, keepdims=True)

        def block_of(z):
            rows = pl.ds(pl.multiple_of(z * 256, 256), 256)
            columns = pl.ds(pl.multiple_of((at["l"] * 8 + z) * 256, 256), 256)
            grad = half[z] + dot(cubes[:, 2 * length :], feat[rows, 2 * length :], both)
            return grad - deriv * vec[:, columns].astype(F32)

        for i, move in enumerate(RING):
            to = moved(at, move)
            grad_out[i] = block_of(to["z"]).astype(BF16)
            send(grad_out.at[i], grad_in.at[i], GRAD, device(to))
        for move in ELEC + [{}]:
            send(wave_out.at[0], waves.at[elec], WAVE, device(moved(at, move) | dict(c=0)))
        for move in ELEC:
            send(wave_out.at[1], waves.at[elec], WAVE, device(moved(at, move)))
        updated = block_of(at["z"])
        came(GRAD, grad_in)
        for i in range(len(RING)):
            updated = updated + grad_in[i].astype(F32)
        updated = updated * (1.0 / (length * 32))
        fresh_out[...] = updated[:, :LANES]
        fresh[...] = updated[:, LANES:]
        gram[...] = fine_gram(updated)

    mine = pl.ds(pl.multiple_of(row_of(at) * 16, 16), 16)

    @pl.when(core == 1)
    def _():
        for i, move in enumerate(ROW):
            to = moved(at, move)
            rows = pl.ds(pl.multiple_of(row_of(to) * 16, 16), 16)
            send(gram.at[rows], gram_row.at[i], GRAM1, device(to))
        send(fresh_out, fresh, FRESH, partner)
        came(GRAM1, gram_row)
        total = gram[mine, :]
        for i in range(len(ROW)):
            total = total + gram_row[i]
        gram_sum[...] = total.astype(BF16)
        for i, move in enumerate(SHEET):
            send(gram_sum, gram_sheet.at[i], GRAM2, device(moved(at, move)))
        came(GRAM2, gram_sheet)
        total = gram_sum[...].astype(F32)
        for i in range(len(SHEET)):
            total = total + gram_sheet[i].astype(F32)
        gram_all[mine, :] = total
        for move in ROW + [{}]:
            send(gram_all.at[mine], gram_all.at[mine], GRAM3, device(moved(at, move) | dict(c=0)))
        for move in ROW:
            send(gram_all.at[mine], gram_all.at[mine], GRAM3, device(moved(at, move)))
        came(GRAM3, gram_all.at[pl.ds(0, 16 * len(ROW))])

    @pl.when(core == 0)
    def _():
        came(GRAM3, gram_all)
        came(FRESH, fresh)

    @pl.when(core == 0)
    def _():
        came(WAVE, waves)

    @pl.when(core == 1)
    def _():
        came(WAVE, waves.at[pl.ds(0, len(ELEC))])

    for pair in range(8):
        pieces = [waves[2 * pair + k].astype(F32) for k in range(2)]
        for k in range(tiles):
            rows = jnp.concatenate([piece[8 * k : 8 * k + 8] for piece in pieces], 0)
            sources[16 * pair : 16 * pair + 16, k * LANES : (k + 1) * LANES] = rows.astype(BF16)

    g = gram_all[...]
    row = lax.broadcasted_iota(jnp.int32, (LANES, LANES), 0)
    column = lax.broadcasted_iota(jnp.int32, (LANES, LANES), 1)
    unit = jnp.where(row == column, 1.0, 0.0)
    squares = jnp.sum(jnp.sum(g * unit, axis=1, keepdims=True), axis=0, keepdims=True)
    scale = START * math.sqrt(LANES) * lax.rsqrt(squares + 1e-06)
    g = g * scale * scale
    current = fresh[...] * scale
    for step in range(NS_STEPS):
        factor = 1.5 * unit - 0.5 * g
        current = fine_dot(factor, current)
        if step < NS_STEPS - 1:
            g = fine_dot(fine_dot(factor, g), factor)
    unmixing[...] = current

    left(TAIL, tail_in)
    left(SPILL, spill_out)

    @pl.when(core == 0)
    def _():
        left(FAR, far_in.at[pl.ds(0, 2)])
        left(LATE, late_in.at[pl.ds(0, 2)])

    @pl.when(core == 1)
    def _():
        left(FAR, far_in.at[0])
        left(LATE, late_in.at[0])
        left(CUBE, blocks.at[pl.ds(0, 30)])
        left(CROSS, blocks.at[pl.ds(0, 32)])
        left(WAVE, blocks.at[pl.ds(0, 31)])
        left(GRAD, grad_in)
        left(FRESH, fresh)
        left(GRAM1, gram_row)
        left(GRAM2, gram_sheet)
        left(GRAM3, summed.at[pl.ds(0, 10)])


def shards(signals, vectors):
    channels, length = signals.shape
    count, columns = vectors.shape
    near, ring, row, sheet = (len(group) for group in (ELEC, RING, ROW, SHEET))
    vmem = pl.BlockSpec(memory_space=pltpu.VMEM)
    return pl.pallas_call(
        kernel,
        out_shape=(
            jax.ShapeDtypeStruct((count, length), BF16),
            jax.ShapeDtypeStruct((count, LANES), F32),
        ),
        in_specs=[pl.BlockSpec(memory_space=pltpu.HBM)] * 2,
        out_specs=(vmem, vmem),
        scratch_shapes=[
            pltpu.VMEM((channels, length), BF16),
            pltpu.VMEM((count, columns), BF16),
            pltpu.VMEM((channels // 8, LANES), F32),
            pltpu.VMEM((channels // 8, LANES), F32),
            pltpu.VMEM((columns, length + LANES), BF16),
            pltpu.VMEM((3, channels // 2, length), BF16),
            pltpu.VMEM((3, channels // 16, LANES), F32),
            pltpu.VMEM((columns // 2, 4 * length), BF16),
            pltpu.VMEM((count, length + LANES), F32),
            pltpu.VMEM((2 * near + 1, 8, length), F32),
            pltpu.VMEM((near + 1, LANES), F32),
            pltpu.VMEM((2 * near + 2, LANES), F32),
            pltpu.VMEM((4 * (near + 1), 32, LANES), BF16),
            pltpu.VMEM((2, 32, LANES), BF16),
            pltpu.VMEM((near + 1, 32, LANES), BF16),
            pltpu.VMEM((count, 4 * length), BF16),
            pltpu.VMEM((8, count, 2 * LANES), F32),
            pltpu.VMEM((ring, count, 2 * LANES), BF16),
            pltpu.VMEM((ring, count, 2 * LANES), BF16),
            pltpu.VMEM((count, LANES), F32),
            pltpu.VMEM((count, LANES), F32),
            pltpu.VMEM((LANES, LANES), F32),
            pltpu.VMEM((row, 16, LANES), F32),
            pltpu.VMEM((16, LANES), BF16),
            pltpu.VMEM((sheet, 16, LANES), BF16),
            pltpu.VMEM((LANES, LANES), F32),
            pltpu.SemaphoreType.DMA((2,)),
            pltpu.SemaphoreType.DMA((13,)),
            pltpu.SemaphoreType.DMA((13,)),
        ],
        compiler_params=pltpu.CompilerParams(
            collective_id=0, has_side_effects=True, vmem_limit_bytes=40 * 2**20
        ),
        cost_estimate=pl.CostEstimate(flops=10**9, bytes_accessed=2 * 10**6, transcendentals=0),
        name="separate",
    )(*[pltpu.with_memory_space_constraint(a, pltpu.HBM) for a in (signals, vectors)])


def solution(mesh):
    return jax.shard_map(
        shards,
        mesh=mesh,
        in_specs=(P("elec", "tm"), P(None, "elec")),
        out_specs=(P(None, "tm"), P(None, ("elec", "tm"))),
        check_vma=False,
    )
```

```python
import functools
import itertools
import math

import jax
import jax.numpy as jnp
from jax import lax
from jax.experimental import pallas as pl
from jax.experimental.pallas import tpu as pltpu
from jax.sharding import PartitionSpec as P

LAGS = 16
NS_STEPS = 6
START = 0.15
MESH = pl.DeviceIdType.MESH
SIZE = dict(x=4, h=4, l=2, z=8, c=2)
F32, BF16 = jnp.float32, jnp.bfloat16
LANES = 128


def hops(move):
    x, y, z = move.get("x", 0), 2 * move.get("h", 0) + move.get("l", 0), move.get("z", 0)
    return min(x, 4 - x) + min(y, 8 - y) + min(z, 8 - z)


def moves(*names):
    every = itertools.product(*[range(SIZE[name]) for name in names])
    found = [dict(zip(names, move)) for move in every if any(move)]
    return sorted(found, key=lambda move: -hops(move))


ELEC, PLANE, RING = moves("x", "h"), moves("x", "h", "l"), moves("z")
ROW, SHEET = moves("x", "l"), moves("z", "h")


def place():
    elec, tm = lax.axis_index("elec"), lax.axis_index("tm")
    return dict(x=elec >> 2, h=elec & 3, l=tm >> 4, z=(tm >> 1) & 7, c=tm & 1)


def moved(at, move):
    return {k: (v + move[k]) & (SIZE[k] - 1) if move.get(k, 0) else v for k, v in at.items()}


def elec_of(at):
    return at["x"] * 4 + at["h"]


def tm_of(at):
    return (at["l"] * 8 + at["z"]) * 2 + at["c"]


def row_of(at):
    return at["x"] * 2 + at["l"]


def device(at):
    return {"elec": elec_of(at), "tm": tm_of(at)}


def remote(src, dst, sems, step, to):
    return pltpu.make_async_remote_copy(
        src_ref=src,
        dst_ref=dst,
        send_sem=sems[0].at[step],
        recv_sem=sems[1].at[step],
        device_id=to,
        device_id_type=MESH,
    )


(TAIL, FAR, LATE, SUM, SPILL, CUBE, CROSS, DERIV, WAVE0, WAVE1, GRAD, FRESH, GRAM1, GRAM2, GRAM3) = range(15)


def halves(a):
    top = a.astype(BF16)
    return top, (a - top.astype(F32)).astype(BF16)


def dot(a, b, dims=(((1,), (0,)), ((), ()))):
    return lax.dot_general(a, b, dims, preferred_element_type=F32)


def fine_dot(a, b):
    (a1, a2), (b1, b2) = halves(a), halves(b)
    return dot(jnp.concatenate([a1, a1, a2], 1), jnp.concatenate([b1, b2, b1], 0))


def fine_gram(a):
    a1, a2 = halves(a)
    both = (((1,), (1,)), ((), ()))
    return dot(jnp.concatenate([a1, a1, a2], 1), jnp.concatenate([a1, a2, a1], 1), both)


def lagged(row, shift=0):
    return pltpu.roll(jnp.broadcast_to(row, (LAGS, LANES)), shift, 1, stride=1, stride_axis=0)


def packed(tile, shift):
    return jnp.sum(pltpu.roll(tile, shift, 1, stride=LAGS, stride_axis=0), axis=0, keepdims=True)


def before_first(row, r):
    return lagged(row, (LANES - (r + 1) * LAGS) % LANES)


def kernel(
    sig_hbm, vec_hbm, sources, unmixing,
    sig, vec, tail_out, tail_in, ext, far_in, late_in, feat,
    partial, summed, spill_out, spill_in, blocks, deriv_out, derivs, wave_out, waves, cubes,
    half, grad_out, grad_in, fresh_out, fresh, gram, gram_row, gram_sum, gram_sheet, gram_all,
    load, sent, got,
):
    at = place()
    elec, tm = elec_of(at), tm_of(at)
    length = sig.shape[1]
    tiles = length // LANES
    after, before = (tm + 1) & 31, (tm + 31) & 31
    core = at["c"]

    loads = [
        pltpu.make_async_copy(sig_hbm, sig, load.at[0]),
        pltpu.make_async_copy(vec_hbm, vec, load.at[1]),
    ]
    for copy in loads:
        copy.start()
    sems = (sent, got)
    partner = device(moved(at, dict(c=1)))

    def send(src, dst, step, to):
        remote(src, dst, sems, step, to).start()

    def left(step, ref):
        remote(ref, ref, sems, step, partner).wait_send()

    def came(step, ref):
        remote(ref, ref, sems, step, partner).wait_recv()

    barrier = pltpu.get_barrier_semaphore()

    def greet(to):
        pl.semaphore_signal(barrier, inc=1, device_id=to, device_id_type=MESH)

    @pl.when(core == 1)
    def _():
        for move in ELEC + [{}]:
            to = moved(at, move)
            greet({"elec": elec_of(to), "tm": (tm + 30) & 31})
            greet(device(to | dict(c=0)))
        for move in PLANE + RING:
            greet(device(moved(at, move)))
        greet(device(moved(at, dict(l=1, c=1))))

    @pl.when(core == 0)
    def _():
        greet({"elec": elec, "tm": before})

    lane = lax.broadcasted_iota(jnp.int32, (LAGS, LANES), 1)
    late = lax.broadcasted_iota(jnp.int32, (LAGS, LANES), 0)
    spill = lane < late

    loads[0].wait()

    @pl.loop(0, 16)
    def _(block):
        rows = sig[pl.ds(block * 16, 16), :].astype(F32)
        for r in range(16):
            to = pl.ds((block * 16 + r) * LAGS, LAGS)
            turned = [lagged(rows[r : r + 1, k * LANES : (k + 1) * LANES]) for k in range(tiles)]
            for k, (a, b) in enumerate(zip([0.0] + turned, turned + [0.0])):
                ext[to, k * LANES : (k + 1) * LANES] = jnp.where(spill, a, b).astype(BF16)

    loads[1].wait()
    partial[...] = dot(vec[...], ext[...])
    spill_out[...] = jnp.concatenate([packed(partial[8 * k : 8 * k + 8, length:], 0) for k in range(16)], 0)

    @pl.when(core == 1)
    def _():
        pl.semaphore_wait(barrier, len(ELEC) + 1 + len(PLANE) + len(RING) + 1)

    @pl.when(core == 0)
    def _():
        pl.semaphore_wait(barrier, len(ELEC) + 2)

    onward = (tm + 1 + core) & 31
    for i, move in enumerate(ELEC + [{}]):
        to = moved(at, move) | dict(c=1)
        rows = pl.ds(pl.multiple_of(elec_of(to) * 8, 8), 8)

        def send_sum():
            send(partial.at[rows, pl.ds(0, length)], summed.at[i + 16 * core], SUM, device(to))

        if move:
            send_sum()
        else:
            pl.when(core == 0)(send_sum)
        over = {"elec": elec_of(to), "tm": onward}
        send(spill_out.at[pl.ds(elec_of(to), 1)], spill_in.at[pl.ds(i + 16 * (1 - core), 1)], SPILL, over)
    last = lax.broadcasted_iota(jnp.int32, (8, LANES), 1) >= LANES - LAGS
    ends = sig[:, length - LANES :].astype(F32)
    tail_out[...] = jnp.concatenate(
        [packed(jnp.where(last, ends[8 * k : 8 * k + 8], 0.0), LAGS) for k in range(ends.shape[0] // 8)], 0
    )
    send(tail_out, tail_in, TAIL, {"elec": elec, "tm": after})

    other = moved(at, dict(l=1)) | dict(c=1)
    here = pl.ds(pl.multiple_of(at["l"] * 128, 128), 128)
    there = pl.ds(pl.multiple_of(other["l"] * 128, 128), 128)

    @pl.when(core == 0)
    def _():
        left(SUM, summed.at[pl.ds(0, 16)])
        send(sig.at[here], far_in.at[0], FAR, partner)

    @pl.when(core == 1)
    def _():
        left(SUM, summed.at[pl.ds(0, 15)])

    send(sig.at[there], far_in.at[2 - core], FAR, device(other))
    came(TAIL, tail_in)

    @pl.when((core == 0) & (tm == 0))
    def _():
        tail_in[...] = jnp.zeros_like(tail_in)

    here_ends = pl.ds(pl.multiple_of(at["l"] * 16, 16), 16)
    there_ends = pl.ds(pl.multiple_of(other["l"] * 16, 16), 16)

    @pl.when(core == 0)
    def _():
        send(tail_in.at[here_ends], late_in.at[0], LATE, partner)

    send(tail_in.at[there_ends], late_in.at[2 - core], LATE, device(other))

    def stacked(block):
        return jnp.concatenate([block[:, k * LANES : (k + 1) * LANES] for k in range(tiles)], 0)

    @pl.when(core == 1)
    def _():
        mine = pl.ds(pl.multiple_of(elec * 8, 8), 8)
        lane = lax.broadcasted_iota(jnp.int32, (8, LANES), 1)
        came(SUM, summed)
        came(SPILL, spill_in)
        deriv, cubed = 0.0, []
        for shard in range(2):
            total = summed[15] if shard == 0 else partial[mine, :length]
            for i in range(len(ELEC)):
                total = total + summed[i + 16 * shard]
            over = jnp.sum(spill_in[16 * shard : 16 * shard + 16], axis=0, keepdims=True)
            if shard == 0:
                over = over * jnp.where(tm > 1, 1.0, 0.0)
            over = jnp.concatenate([pltpu.roll(over, (LANES - r * LAGS) % LANES, 1) for r in range(8)], 0)
            over = jnp.where(lane < LAGS, over, 0.0)
            total = jnp.concatenate([total[:, :LANES] + over, total[:, LANES:]], 1)
            deriv = deriv + jnp.sum(3.0 * total * total, axis=1, keepdims=True)
            cubed.append(stacked(total * total * total))
            wave_out[shard] = jnp.concatenate([stacked(total), jnp.zeros((8, LANES), F32)], 0).astype(BF16)
        blocks[elec] = jnp.concatenate(cubed, 0).astype(BF16)
        for move in ELEC:
            send(blocks.at[elec], blocks.at[elec], CUBE, device(moved(at, move)))
        for move in PLANE:
            if move["l"]:
                send(blocks.at[elec], blocks.at[elec + 16], CROSS, device(moved(at, move)))
        deriv = packed(jnp.where(lane == 0, deriv, 0.0), 0)
        deriv_out[0:1] = deriv
        derivs[pl.ds(elec, 1)] = deriv
        for move in PLANE:
            row = pl.ds(elec + 16 * move["l"], 1)
            send(deriv_out.at[pl.ds(0, 1)], derivs.at[row], DERIV, device(moved(at, move)))
        waves[elec] = wave_out[1]

    both = (((1,), (1,)), ((), ()))

    def unpack(part):
        for pair in range(8):
            pieces = [blocks[16 * part + 2 * pair + k].astype(F32) for k in range(2)]
            for c, k in itertools.product(range(2), range(tiles)):
                rows = jnp.concatenate([piece[24 * c + 8 * k : 24 * c + 8 * k + 8] for piece in pieces], 0)
                begin = (2 * part + 1 - c) * length + k * LANES
                cubes[16 * pair : 16 * pair + 16, begin : begin + LANES] = rows.astype(BF16)

    @pl.when(core == 1)
    def _():
        feat[:, :length] = ext[pl.ds(pl.multiple_of(at["l"] * 2048, 2048), 2048), :length]

        @pl.loop(0, 8)
        def _(block):
            ends = tail_in[pl.ds(at["l"] * 16 + block * 2, 2), :]
            for r in range(16):
                to = pl.ds((block * 16 + r) * LAGS, LAGS)
                turned = before_first(ends[r // 8 : r // 8 + 1], r % 8)
                feat[to, :LANES] = jnp.where(spill, turned, feat[to, :LANES].astype(F32)).astype(BF16)

        came(FAR, far_in)
        came(LATE, late_in)
        for i in range(3):

            @pl.loop(0, 8)
            def _(block):
                rows = far_in[i, pl.ds(block * 16, 16), :].astype(F32)
                ends = late_in[i, pl.ds(block * 2, 2), :]
                for r in range(16):
                    to = pl.ds((block * 16 + r) * LAGS, LAGS)
                    turned = [before_first(ends[r // 8 : r // 8 + 1], r % 8)]
                    turned += [lagged(rows[r : r + 1, k * LANES : (k + 1) * LANES]) for k in range(tiles)]
                    for k in range(tiles):
                        begin = (i + 1) * length + k * LANES
                        feat[to, begin : begin + LANES] = jnp.where(spill, turned[k], turned[k + 1]).astype(BF16)

        came(CUBE, blocks.at[pl.ds(0, 15)])
        unpack(0)
        for z in range(8):
            half[z] = dot(cubes[:, : 2 * length], feat[z * 256 : z * 256 + 256, : 2 * length], both)
        came(CROSS, blocks.at[pl.ds(16, 16)])
        unpack(1)
        came(DERIV, derivs.at[pl.ds(0, 31)])
        deriv = derivs[:16] + derivs[16:]
        deriv = jnp.concatenate([jnp.broadcast_to(deriv[k : k + 1], (8, LANES)) for k in range(16)], 0)
        place_of = (lax.broadcasted_iota(jnp.int32, (LANES, LANES), 0) & 7) * LAGS
        lane = lax.broadcasted_iota(jnp.int32, (LANES, LANES), 1)
        deriv = jnp.sum(jnp.where(lane == place_of, deriv, 0.0), axis=1, keepdims=True)

        def block_of(z):
            rows = pl.ds(pl.multiple_of(z * 256, 256), 256)
            columns = pl.ds(pl.multiple_of((at["l"] * 8 + z) * 256, 256), 256)
            grad = half[z] + dot(cubes[:, 2 * length :], feat[rows, 2 * length :], both)
            return grad - deriv * vec[:, columns].astype(F32)

        for i, move in enumerate(RING):
            to = moved(at, move)
            grad_out[i] = block_of(to["z"]).astype(BF16)
            send(grad_out.at[i], grad_in.at[i], GRAD, device(to))
        for move in ELEC + [{}]:
            send(wave_out.at[0], waves.at[elec], WAVE0, device(moved(at, move) | dict(c=0)))
        for move in ELEC:
            send(wave_out.at[1], waves.at[elec], WAVE1, device(moved(at, move)))
        updated = block_of(at["z"])
        came(GRAD, grad_in)
        for i in range(len(RING)):
            updated = updated + grad_in[i].astype(F32)
        updated = updated * (1.0 / (length * 32))
        fresh_out[...] = updated[:, :LANES]
        fresh[...] = updated[:, LANES:]
        gram[...] = fine_gram(updated)

    mine = pl.ds(pl.multiple_of(row_of(at) * 16, 16), 16)

    @pl.when(core == 1)
    def _():
        for i, move in enumerate(ROW):
            to = moved(at, move)
            rows = pl.ds(pl.multiple_of(row_of(to) * 16, 16), 16)
            send(gram.at[rows], gram_row.at[i], GRAM1, device(to))
        send(fresh_out, fresh, FRESH, partner)
        came(GRAM1, gram_row)
        total = gram[mine, :]
        for i in range(len(ROW)):
            total = total + gram_row[i]
        gram_sum[...] = total.astype(BF16)
        for i, move in enumerate(SHEET):
            send(gram_sum, gram_sheet.at[i], GRAM2, device(moved(at, move)))
        came(GRAM2, gram_sheet)
        total = gram_sum[...].astype(F32)
        for i in range(len(SHEET)):
            total = total + gram_sheet[i].astype(F32)
        gram_all[mine, :] = total
        for move in ROW + [{}]:
            send(gram_all.at[mine], gram_all.at[mine], GRAM3, device(moved(at, move) | dict(c=0)))
        for move in ROW:
            send(gram_all.at[mine], gram_all.at[mine], GRAM3, device(moved(at, move)))
        came(GRAM3, gram_all.at[pl.ds(0, 16 * len(ROW))])

    @pl.when(core == 0)
    def _():
        came(GRAM3, gram_all)
        came(FRESH, fresh)

    @pl.when(core == 0)
    def _():
        came(WAVE0, waves)

    @pl.when(core == 1)
    def _():
        came(WAVE1, waves.at[pl.ds(0, len(ELEC))])

    for pair in range(8):
        pieces = [waves[2 * pair + k].astype(F32) for k in range(2)]
        for k in range(tiles):
            rows = jnp.concatenate([piece[8 * k : 8 * k + 8] for piece in pieces], 0)
            sources[16 * pair : 16 * pair + 16, k * LANES : (k + 1) * LANES] = rows.astype(BF16)

    g = gram_all[...]
    row = lax.broadcasted_iota(jnp.int32, (LANES, LANES), 0)
    column = lax.broadcasted_iota(jnp.int32, (LANES, LANES), 1)
    unit = jnp.where(row == column, 1.0, 0.0)
    squares = jnp.sum(jnp.sum(g * unit, axis=1, keepdims=True), axis=0, keepdims=True)
    scale = START * math.sqrt(LANES) * lax.rsqrt(squares + 1e-06)
    g = g * scale * scale
    current = fresh[...] * scale
    for step in range(NS_STEPS):
        factor = 1.5 * unit - 0.5 * g
        current = fine_dot(factor, current)
        if step < NS_STEPS - 1:
            g = fine_dot(fine_dot(factor, g), factor)
    unmixing[...] = current

    left(TAIL, tail_in)
    left(SPILL, spill_out)

    @pl.when(core == 0)
    def _():
        left(FAR, far_in.at[pl.ds(0, 2)])
        left(LATE, late_in.at[pl.ds(0, 2)])

    @pl.when(core == 1)
    def _():
        left(FAR, far_in.at[0])
        left(LATE, late_in.at[0])
        left(CUBE, blocks.at[pl.ds(0, 15)])
        left(CROSS, blocks.at[pl.ds(0, 16)])
        left(DERIV, derivs.at[pl.ds(0, 31)])
        left(WAVE0, waves)
        left(WAVE1, waves.at[pl.ds(0, len(ELEC))])
        left(GRAD, grad_in)
        left(FRESH, fresh)
        left(GRAM1, gram_row)
        left(GRAM2, gram_sheet)
        left(GRAM3, summed.at[pl.ds(0, 10)])


def shards(signals, vectors):
    channels, length = signals.shape
    count, columns = vectors.shape
    near, ring, row, sheet = (len(group) for group in (ELEC, RING, ROW, SHEET))
    vmem = pl.BlockSpec(memory_space=pltpu.VMEM)
    return pl.pallas_call(
        kernel,
        out_shape=(
            jax.ShapeDtypeStruct((count, length), BF16),
            jax.ShapeDtypeStruct((count, LANES), F32),
        ),
        in_specs=[pl.BlockSpec(memory_space=pltpu.HBM)] * 2,
        out_specs=(vmem, vmem),
        scratch_shapes=[
            pltpu.VMEM((channels, length), BF16),
            pltpu.VMEM((count, columns), BF16),
            pltpu.VMEM((channels // 8, LANES), F32),
            pltpu.VMEM((channels // 8, LANES), F32),
            pltpu.VMEM((columns, length + LANES), BF16),
            pltpu.VMEM((3, channels // 2, length), BF16),
            pltpu.VMEM((3, channels // 16, LANES), F32),
            pltpu.VMEM((columns // 2, 4 * length), BF16),
            pltpu.VMEM((count, length + LANES), F32),
            pltpu.VMEM((2 * near + 1, 8, length), F32),
            pltpu.VMEM((near + 1, LANES), F32),
            pltpu.VMEM((2 * near + 2, LANES), F32),
            pltpu.VMEM((2 * (near + 1), 48, LANES), BF16),
            pltpu.VMEM((8, LANES), F32),
            pltpu.VMEM((2 * (near + 1), LANES), F32),
            pltpu.VMEM((2, 32, LANES), BF16),
            pltpu.VMEM((near + 1, 32, LANES), BF16),
            pltpu.VMEM((count, 4 * length), BF16),
            pltpu.VMEM((8, count, 2 * LANES), F32),
            pltpu.VMEM((ring, count, 2 * LANES), BF16),
            pltpu.VMEM((ring, count, 2 * LANES), BF16),
            pltpu.VMEM((count, LANES), F32),
            pltpu.VMEM((count, LANES), F32),
            pltpu.VMEM((LANES, LANES), F32),
            pltpu.VMEM((row, 16, LANES), F32),
            pltpu.VMEM((16, LANES), BF16),
            pltpu.VMEM((sheet, 16, LANES), BF16),
            pltpu.VMEM((LANES, LANES), F32),
            pltpu.SemaphoreType.DMA((2,)),
            pltpu.SemaphoreType.DMA((15,)),
            pltpu.SemaphoreType.DMA((15,)),
        ],
        compiler_params=pltpu.CompilerParams(
            collective_id=0, has_side_effects=True, vmem_limit_bytes=40 * 2**20
        ),
        cost_estimate=pl.CostEstimate(flops=10**9, bytes_accessed=2 * 10**6, transcendentals=0),
        name="separate",
    )(*[pltpu.with_memory_space_constraint(a, pltpu.HBM) for a in (signals, vectors)])


def solution(mesh):
    return jax.shard_map(
        shards,
        mesh=mesh,
        in_specs=(P("elec", "tm"), P(None, "elec")),
        out_specs=(P(None, "tm"), P(None, ("elec", "tm"))),
        check_vma=False,
    )
```

```python
import functools
import itertools
import math

import jax
import jax.numpy as jnp
from jax import lax
from jax.experimental import pallas as pl
from jax.experimental.pallas import tpu as pltpu
from jax.sharding import PartitionSpec as P

LAGS = 16
NS_STEPS = 6
START = 0.15
MESH = pl.DeviceIdType.MESH
SIZE = dict(x=4, h=4, l=2, z=8, c=2)
F32, BF16 = jnp.float32, jnp.bfloat16
LANES = 128


def hops(move):
    x, y, z = move.get("x", 0), 2 * move.get("h", 0) + move.get("l", 0), move.get("z", 0)
    return min(x, 4 - x) + min(y, 8 - y) + min(z, 8 - z)


def moves(*names):
    every = itertools.product(*[range(SIZE[name]) for name in names])
    found = [dict(zip(names, move)) for move in every if any(move)]
    return sorted(found, key=lambda move: -hops(move))


ELEC, PLANE, RING = moves("x", "h"), moves("x", "h", "l"), moves("z")
ROW, SHEET = moves("x", "l"), moves("z", "h")


def place():
    elec, tm = lax.axis_index("elec"), lax.axis_index("tm")
    return dict(x=elec >> 2, h=elec & 3, l=tm >> 4, z=(tm >> 1) & 7, c=tm & 1)


def moved(at, move):
    return {k: (v + move[k]) & (SIZE[k] - 1) if move.get(k, 0) else v for k, v in at.items()}


def elec_of(at):
    return at["x"] * 4 + at["h"]


def tm_of(at):
    return (at["l"] * 8 + at["z"]) * 2 + at["c"]


def row_of(at):
    return at["x"] * 2 + at["l"]


def device(at):
    return {"elec": elec_of(at), "tm": tm_of(at)}


def remote(src, dst, sems, step, to):
    return pltpu.make_async_remote_copy(
        src_ref=src,
        dst_ref=dst,
        send_sem=sems[0].at[step],
        recv_sem=sems[1].at[step],
        device_id=to,
        device_id_type=MESH,
    )


(TAIL, FAR, FAR0, LATE, LATE0, SUM, SPILL, CUBE, CROSS, DERIV, WAVE0, WAVE1, GRAD, FRESH, GRAM1, GRAM2, GRAM3) = range(17)


def halves(a):
    top = a.astype(BF16)
    return top, (a - top.astype(F32)).astype(BF16)


def dot(a, b, dims=(((1,), (0,)), ((), ()))):
    return lax.dot_general(a, b, dims, preferred_element_type=F32)


def fine_dot(a, b):
    (a1, a2), (b1, b2) = halves(a), halves(b)
    return dot(jnp.concatenate([a1, a1, a2], 1), jnp.concatenate([b1, b2, b1], 0))


def fine_gram(a):
    a1, a2 = halves(a)
    both = (((1,), (1,)), ((), ()))
    return dot(jnp.concatenate([a1, a1, a2], 1), jnp.concatenate([a1, a2, a1], 1), both)


def lagged(row, shift=0):
    return pltpu.roll(jnp.broadcast_to(row, (LAGS, LANES)), shift, 1, stride=1, stride_axis=0)


def packed(tile, shift):
    return jnp.sum(pltpu.roll(tile, shift, 1, stride=LAGS, stride_axis=0), axis=0, keepdims=True)


def before_first(row, r):
    return lagged(row, (LANES - (r + 1) * LAGS) % LANES)


def kernel(
    sig_hbm, vec_hbm, sources, unmixing,
    sig, vec, tail_out, tail_in, ext, far_in, late_in, feat,
    partial, summed, spill_out, spill_in, blocks, deriv_out, derivs, wave_out, waves, cubes,
    half, grad_out, grad_in, fresh_out, fresh, gram, gram_row, gram_sum, gram_sheet, gram_all,
    load, sent, got,
):
    at = place()
    elec, tm = elec_of(at), tm_of(at)
    length = sig.shape[1]
    tiles = length // LANES
    after, before = (tm + 1) & 31, (tm + 31) & 31
    core = at["c"]

    loads = [
        pltpu.make_async_copy(sig_hbm, sig, load.at[0]),
        pltpu.make_async_copy(vec_hbm, vec, load.at[1]),
    ]
    for copy in loads:
        copy.start()
    sems = (sent, got)
    partner = device(moved(at, dict(c=1)))

    def send(src, dst, step, to):
        remote(src, dst, sems, step, to).start()

    def left(step, ref):
        remote(ref, ref, sems, step, partner).wait_send()

    def came(step, ref):
        remote(ref, ref, sems, step, partner).wait_recv()

    barrier = pltpu.get_barrier_semaphore()

    def greet(to):
        pl.semaphore_signal(barrier, inc=1, device_id=to, device_id_type=MESH)

    @pl.when(core == 1)
    def _():
        for move in ELEC + [{}]:
            to = moved(at, move)
            greet({"elec": elec_of(to), "tm": (tm + 30) & 31})
            greet(device(to | dict(c=0)))
        for move in PLANE + RING:
            greet(device(moved(at, move)))
        greet(device(moved(at, dict(l=1, c=1))))

    @pl.when(core == 0)
    def _():
        greet({"elec": elec, "tm": before})

    lane = lax.broadcasted_iota(jnp.int32, (LAGS, LANES), 1)
    late = lax.broadcasted_iota(jnp.int32, (LAGS, LANES), 0)
    spill = lane < late

    loads[0].wait()

    @pl.loop(0, 16)
    def _(block):
        rows = sig[pl.ds(block * 16, 16), :].astype(F32)
        for r in range(16):
            to = pl.ds((block * 16 + r) * LAGS, LAGS)
            turned = [lagged(rows[r : r + 1, k * LANES : (k + 1) * LANES]) for k in range(tiles)]
            for k, (a, b) in enumerate(zip([0.0] + turned, turned + [0.0])):
                ext[to, k * LANES : (k + 1) * LANES] = jnp.where(spill, a, b).astype(BF16)

    loads[1].wait()
    partial[...] = dot(vec[...], ext[...])
    spill_out[...] = jnp.concatenate([packed(partial[8 * k : 8 * k + 8, length:], 0) for k in range(16)], 0)

    @pl.when(core == 1)
    def _():
        pl.semaphore_wait(barrier, len(ELEC) + 1 + len(PLANE) + len(RING) + 1)

    @pl.when(core == 0)
    def _():
        pl.semaphore_wait(barrier, len(ELEC) + 2)

    onward = (tm + 1 + core) & 31
    for i, move in enumerate(ELEC + [{}]):
        to = moved(at, move) | dict(c=1)
        rows = pl.ds(pl.multiple_of(elec_of(to) * 8, 8), 8)

        def send_sum():
            send(partial.at[rows, pl.ds(0, length)], summed.at[i + 16 * core], SUM, device(to))

        if move:
            send_sum()
        else:
            pl.when(core == 0)(send_sum)
        over = {"elec": elec_of(to), "tm": onward}
        send(spill_out.at[pl.ds(elec_of(to), 1)], spill_in.at[pl.ds(i + 16 * (1 - core), 1)], SPILL, over)
    last = lax.broadcasted_iota(jnp.int32, (8, LANES), 1) >= LANES - LAGS
    ends = sig[:, length - LANES :].astype(F32)
    tail_out[...] = jnp.concatenate(
        [packed(jnp.where(last, ends[8 * k : 8 * k + 8], 0.0), LAGS) for k in range(ends.shape[0] // 8)], 0
    )
    send(tail_out, tail_in, TAIL, {"elec": elec, "tm": after})

    other = moved(at, dict(l=1)) | dict(c=1)
    here = pl.ds(pl.multiple_of(at["l"] * 128, 128), 128)
    there = pl.ds(pl.multiple_of(other["l"] * 128, 128), 128)

    @pl.when(core == 0)
    def _():
        left(SUM, summed.at[pl.ds(0, 16)])
        send(sig.at[here], far_in.at[0], FAR0, partner)

    @pl.when(core == 1)
    def _():
        left(SUM, summed.at[pl.ds(0, 15)])

    send(sig.at[there], far_in.at[2 - core], FAR, device(other))
    came(TAIL, tail_in)

    @pl.when((core == 0) & (tm == 0))
    def _():
        tail_in[...] = jnp.zeros_like(tail_in)

    here_ends = pl.ds(pl.multiple_of(at["l"] * 16, 16), 16)
    there_ends = pl.ds(pl.multiple_of(other["l"] * 16, 16), 16)

    @pl.when(core == 0)
    def _():
        send(tail_in.at[here_ends], late_in.at[0], LATE0, partner)

    send(tail_in.at[there_ends], late_in.at[2 - core], LATE, device(other))

    def stacked(block):
        return jnp.concatenate([block[:, k * LANES : (k + 1) * LANES] for k in range(tiles)], 0)

    def lag_far(i):
        @pl.loop(0, 8)
        def _(block):
            rows = far_in[i, pl.ds(block * 16, 16), :].astype(F32)
            ends = late_in[i, pl.ds(block * 2, 2), :]
            for r in range(16):
                to = pl.ds((block * 16 + r) * LAGS, LAGS)
                turned = [before_first(ends[r // 8 : r // 8 + 1], r % 8)]
                turned += [lagged(rows[r : r + 1, k * LANES : (k + 1) * LANES]) for k in range(tiles)]
                for k in range(tiles):
                    begin = (i + 1) * length + k * LANES
                    feat[to, begin : begin + LANES] = jnp.where(spill, turned[k], turned[k + 1]).astype(BF16)

    @pl.when(core == 1)
    def _():
        feat[:, :length] = ext[pl.ds(pl.multiple_of(at["l"] * 2048, 2048), 2048), :length]

        @pl.loop(0, 8)
        def _(block):
            ends = tail_in[pl.ds(at["l"] * 16 + block * 2, 2), :]
            for r in range(16):
                to = pl.ds((block * 16 + r) * LAGS, LAGS)
                turned = before_first(ends[r // 8 : r // 8 + 1], r % 8)
                feat[to, :LANES] = jnp.where(spill, turned, feat[to, :LANES].astype(F32)).astype(BF16)

        came(FAR0, far_in.at[0])
        came(LATE0, late_in.at[0])
        lag_far(0)

        mine = pl.ds(pl.multiple_of(elec * 8, 8), 8)
        lane = lax.broadcasted_iota(jnp.int32, (8, LANES), 1)
        came(SUM, summed)
        came(SPILL, spill_in)
        deriv, cubed = 0.0, []
        for shard in range(2):
            total = summed[15] if shard == 0 else partial[mine, :length]
            for i in range(len(ELEC)):
                total = total + summed[i + 16 * shard]
            over = jnp.sum(spill_in[16 * shard : 16 * shard + 16], axis=0, keepdims=True)
            if shard == 0:
                over = over * jnp.where(tm > 1, 1.0, 0.0)
            over = jnp.concatenate([pltpu.roll(over, (LANES - r * LAGS) % LANES, 1) for r in range(8)], 0)
            over = jnp.where(lane < LAGS, over, 0.0)
            total = jnp.concatenate([total[:, :LANES] + over, total[:, LANES:]], 1)
            deriv = deriv + jnp.sum(3.0 * total * total, axis=1, keepdims=True)
            cubed.append(stacked(total * total * total))
            wave_out[shard] = jnp.concatenate([stacked(total), jnp.zeros((8, LANES), F32)], 0).astype(BF16)
        blocks[elec] = jnp.concatenate(cubed, 0).astype(BF16)
        for move in ELEC:
            send(blocks.at[elec], blocks.at[elec], CUBE, device(moved(at, move)))
        for move in PLANE:
            if move["l"]:
                send(blocks.at[elec], blocks.at[elec + 16], CROSS, device(moved(at, move)))
        deriv = packed(jnp.where(lane == 0, deriv, 0.0), 0)
        deriv_out[0:1] = deriv
        derivs[pl.ds(elec, 1)] = deriv
        for move in PLANE:
            row = pl.ds(elec + 16 * move["l"], 1)
            send(deriv_out.at[pl.ds(0, 1)], derivs.at[row], DERIV, device(moved(at, move)))
        waves[elec] = wave_out[1]

    both = (((1,), (1,)), ((), ()))

    def unpack(part):
        for pair in range(8):
            pieces = [blocks[16 * part + 2 * pair + k].astype(F32) for k in range(2)]
            for c, k in itertools.product(range(2), range(tiles)):
                rows = jnp.concatenate([piece[24 * c + 8 * k : 24 * c + 8 * k + 8] for piece in pieces], 0)
                begin = (2 * part + 1 - c) * length + k * LANES
                cubes[16 * pair : 16 * pair + 16, begin : begin + LANES] = rows.astype(BF16)

    @pl.when(core == 1)
    def _():
        came(FAR, far_in.at[pl.ds(1, 2)])
        came(LATE, late_in.at[pl.ds(1, 2)])
        lag_far(1)
        lag_far(2)
        came(CUBE, blocks.at[pl.ds(0, 15)])
        unpack(0)
        for z in range(8):
            half[z] = dot(cubes[:, : 2 * length], feat[z * 256 : z * 256 + 256, : 2 * length], both)
        came(CROSS, blocks.at[pl.ds(16, 16)])
        unpack(1)
        came(DERIV, derivs.at[pl.ds(0, 31)])
        deriv = derivs[:16] + derivs[16:]
        deriv = jnp.concatenate([jnp.broadcast_to(deriv[k : k + 1], (8, LANES)) for k in range(16)], 0)
        place_of = (lax.broadcasted_iota(jnp.int32, (LANES, LANES), 0) & 7) * LAGS
        lane = lax.broadcasted_iota(jnp.int32, (LANES, LANES), 1)
        deriv = jnp.sum(jnp.where(lane == place_of, deriv, 0.0), axis=1, keepdims=True)

        def block_of(z):
            rows = pl.ds(pl.multiple_of(z * 256, 256), 256)
            columns = pl.ds(pl.multiple_of((at["l"] * 8 + z) * 256, 256), 256)
            grad = half[z] + dot(cubes[:, 2 * length :], feat[rows, 2 * length :], both)
            return grad - deriv * vec[:, columns].astype(F32)

        for i, move in enumerate(RING):
            to = moved(at, move)
            grad_out[i] = block_of(to["z"]).astype(BF16)
            send(grad_out.at[i], grad_in.at[i], GRAD, device(to))
        for move in ELEC + [{}]:
            send(wave_out.at[0], waves.at[elec], WAVE0, device(moved(at, move) | dict(c=0)))
        for move in ELEC:
            send(wave_out.at[1], waves.at[elec], WAVE1, device(moved(at, move)))
        updated = block_of(at["z"])
        came(GRAD, grad_in)
        for i in range(len(RING)):
            updated = updated + grad_in[i].astype(F32)
        updated = updated * (1.0 / (length * 32))
        fresh_out[...] = updated[:, :LANES]
        fresh[...] = updated[:, LANES:]
        gram[...] = fine_gram(updated)

    mine = pl.ds(pl.multiple_of(row_of(at) * 16, 16), 16)

    @pl.when(core == 1)
    def _():
        for i, move in enumerate(ROW):
            to = moved(at, move)
            rows = pl.ds(pl.multiple_of(row_of(to) * 16, 16), 16)
            send(gram.at[rows], gram_row.at[i], GRAM1, device(to))
        send(fresh_out, fresh, FRESH, partner)
        came(GRAM1, gram_row)
        total = gram[mine, :]
        for i in range(len(ROW)):
            total = total + gram_row[i]
        gram_sum[...] = total.astype(BF16)
        for i, move in enumerate(SHEET):
            send(gram_sum, gram_sheet.at[i], GRAM2, device(moved(at, move)))
        came(GRAM2, gram_sheet)
        total = gram_sum[...].astype(F32)
        for i in range(len(SHEET)):
            total = total + gram_sheet[i].astype(F32)
        gram_all[mine, :] = total
        for move in ROW + [{}]:
            send(gram_all.at[mine], gram_all.at[mine], GRAM3, device(moved(at, move) | dict(c=0)))
        for move in ROW:
            send(gram_all.at[mine], gram_all.at[mine], GRAM3, device(moved(at, move)))
        came(GRAM3, gram_all.at[pl.ds(0, 16 * len(ROW))])

    @pl.when(core == 0)
    def _():
        came(GRAM3, gram_all)
        came(FRESH, fresh)

    @pl.when(core == 0)
    def _():
        came(WAVE0, waves)

    @pl.when(core == 1)
    def _():
        came(WAVE1, waves.at[pl.ds(0, len(ELEC))])

    for pair in range(8):
        pieces = [waves[2 * pair + k].astype(F32) for k in range(2)]
        for k in range(tiles):
            rows = jnp.concatenate([piece[8 * k : 8 * k + 8] for piece in pieces], 0)
            sources[16 * pair : 16 * pair + 16, k * LANES : (k + 1) * LANES] = rows.astype(BF16)

    g = gram_all[...]
    row = lax.broadcasted_iota(jnp.int32, (LANES, LANES), 0)
    column = lax.broadcasted_iota(jnp.int32, (LANES, LANES), 1)
    unit = jnp.where(row == column, 1.0, 0.0)
    squares = jnp.sum(jnp.sum(g * unit, axis=1, keepdims=True), axis=0, keepdims=True)
    scale = START * math.sqrt(LANES) * lax.rsqrt(squares + 1e-06)
    g = g * scale * scale
    current = fresh[...] * scale
    for step in range(NS_STEPS):
        factor = 1.5 * unit - 0.5 * g
        current = fine_dot(factor, current)
        if step < NS_STEPS - 1:
            g = fine_dot(fine_dot(factor, g), factor)
    unmixing[...] = current

    left(TAIL, tail_in)
    left(SPILL, spill_out)

    @pl.when(core == 0)
    def _():
        left(FAR, far_in.at[0])
        left(FAR0, far_in.at[0])
        left(LATE, late_in.at[0])
        left(LATE0, late_in.at[0])

    @pl.when(core == 1)
    def _():
        left(FAR, far_in.at[0])
        left(LATE, late_in.at[0])
        left(CUBE, blocks.at[pl.ds(0, 15)])
        left(CROSS, blocks.at[pl.ds(0, 16)])
        left(DERIV, derivs.at[pl.ds(0, 31)])
        left(WAVE0, waves)
        left(WAVE1, waves.at[pl.ds(0, len(ELEC))])
        left(GRAD, grad_in)
        left(FRESH, fresh)
        left(GRAM1, gram_row)
        left(GRAM2, gram_sheet)
        left(GRAM3, summed.at[pl.ds(0, 10)])


def shards(signals, vectors):
    channels, length = signals.shape
    count, columns = vectors.shape
    near, ring, row, sheet = (len(group) for group in (ELEC, RING, ROW, SHEET))
    vmem = pl.BlockSpec(memory_space=pltpu.VMEM)
    return pl.pallas_call(
        kernel,
        out_shape=(
            jax.ShapeDtypeStruct((count, length), BF16),
            jax.ShapeDtypeStruct((count, LANES), F32),
        ),
        in_specs=[pl.BlockSpec(memory_space=pltpu.HBM)] * 2,
        out_specs=(vmem, vmem),
        scratch_shapes=[
            pltpu.VMEM((channels, length), BF16),
            pltpu.VMEM((count, columns), BF16),
            pltpu.VMEM((channels // 8, LANES), F32),
            pltpu.VMEM((channels // 8, LANES), F32),
            pltpu.VMEM((columns, length + LANES), BF16),
            pltpu.VMEM((3, channels // 2, length), BF16),
            pltpu.VMEM((3, channels // 16, LANES), F32),
            pltpu.VMEM((columns // 2, 4 * length), BF16),
            pltpu.VMEM((count, length + LANES), F32),
            pltpu.VMEM((2 * near + 1, 8, length), F32),
            pltpu.VMEM((near + 1, LANES), F32),
            pltpu.VMEM((2 * near + 2, LANES), F32),
            pltpu.VMEM((2 * (near + 1), 48, LANES), BF16),
            pltpu.VMEM((8, LANES), F32),
            pltpu.VMEM((2 * (near + 1), LANES), F32),
            pltpu.VMEM((2, 32, LANES), BF16),
            pltpu.VMEM((near + 1, 32, LANES), BF16),
            pltpu.VMEM((count, 4 * length), BF16),
            pltpu.VMEM((8, count, 2 * LANES), F32),
            pltpu.VMEM((ring, count, 2 * LANES), BF16),
            pltpu.VMEM((ring, count, 2 * LANES), BF16),
            pltpu.VMEM((count, LANES), F32),
            pltpu.VMEM((count, LANES), F32),
            pltpu.VMEM((LANES, LANES), F32),
            pltpu.VMEM((row, 16, LANES), F32),
            pltpu.VMEM((16, LANES), BF16),
            pltpu.VMEM((sheet, 16, LANES), BF16),
            pltpu.VMEM((LANES, LANES), F32),
            pltpu.SemaphoreType.DMA((2,)),
            pltpu.SemaphoreType.DMA((17,)),
            pltpu.SemaphoreType.DMA((17,)),
        ],
        compiler_params=pltpu.CompilerParams(
            collective_id=0, has_side_effects=True, vmem_limit_bytes=40 * 2**20
        ),
        cost_estimate=pl.CostEstimate(flops=10**9, bytes_accessed=2 * 10**6, transcendentals=0),
        name="separate",
    )(*[pltpu.with_memory_space_constraint(a, pltpu.HBM) for a in (signals, vectors)])


def solution(mesh):
    return jax.shard_map(
        shards,
        mesh=mesh,
        in_specs=(P("elec", "tm"), P(None, "elec")),
        out_specs=(P(None, "tm"), P(None, ("elec", "tm"))),
        check_vma=False,
    )
```

```python
import functools
import itertools
import math

import jax
import jax.numpy as jnp
from jax import lax
from jax.experimental import pallas as pl
from jax.experimental.pallas import tpu as pltpu
from jax.sharding import PartitionSpec as P

LAGS = 16
NS_STEPS = 6
START = 0.15
MESH = pl.DeviceIdType.MESH
SIZE = dict(x=4, h=4, l=2, z=8, c=2)
F32, BF16 = jnp.float32, jnp.bfloat16
LANES = 128


def hops(move):
    x, y, z = move.get("x", 0), 2 * move.get("h", 0) + move.get("l", 0), move.get("z", 0)
    return min(x, 4 - x) + min(y, 8 - y) + min(z, 8 - z)


def moves(*names):
    every = itertools.product(*[range(SIZE[name]) for name in names])
    found = [dict(zip(names, move)) for move in every if any(move)]
    return sorted(found, key=lambda move: -hops(move))


ELEC, PLANE, RING = moves("x", "h"), moves("x", "h", "l"), moves("z")
ROW, SHEET = moves("x", "l"), moves("z", "h")


def place():
    elec, tm = lax.axis_index("elec"), lax.axis_index("tm")
    return dict(x=elec >> 2, h=elec & 3, l=tm >> 4, z=(tm >> 1) & 7, c=tm & 1)


def moved(at, move):
    return {k: (v + move[k]) & (SIZE[k] - 1) if move.get(k, 0) else v for k, v in at.items()}


def elec_of(at):
    return at["x"] * 4 + at["h"]


def tm_of(at):
    return (at["l"] * 8 + at["z"]) * 2 + at["c"]


def row_of(at):
    return at["x"] * 2 + at["l"]


def device(at):
    return {"elec": elec_of(at), "tm": tm_of(at)}


def remote(src, dst, sems, step, to):
    return pltpu.make_async_remote_copy(
        src_ref=src,
        dst_ref=dst,
        send_sem=sems[0].at[step],
        recv_sem=sems[1].at[step],
        device_id=to,
        device_id_type=MESH,
    )


(TAIL, FAR, LATE, SUM, SPILL, CUBE, CROSS, DERIV, WAVE0, WAVE1, GRAD, FRESH, GRAM1, GRAM2, GRAM3) = range(15)


def halves(a):
    top = a.astype(BF16)
    return top, (a - top.astype(F32)).astype(BF16)


def dot(a, b, dims=(((1,), (0,)), ((), ()))):
    return lax.dot_general(a, b, dims, preferred_element_type=F32)


def fine_dot(a, b):
    (a1, a2), (b1, b2) = halves(a), halves(b)
    return dot(jnp.concatenate([a1, a1, a2], 1), jnp.concatenate([b1, b2, b1], 0))


def fine_gram(a):
    a1, a2 = halves(a)
    both = (((1,), (1,)), ((), ()))
    return dot(jnp.concatenate([a1, a1, a2], 1), jnp.concatenate([a1, a2, a1], 1), both)


def lagged(row, shift=0):
    return pltpu.roll(jnp.broadcast_to(row, (LAGS, LANES)), shift, 1, stride=1, stride_axis=0)


def packed(tile, shift):
    return jnp.sum(pltpu.roll(tile, shift, 1, stride=LAGS, stride_axis=0), axis=0, keepdims=True)


def before_first(row, r):
    return lagged(row, (LANES - (r + 1) * LAGS) % LANES)


def kernel(
    sig_hbm, vec_hbm, sources, unmixing,
    sig, vec, tail_out, tail_in, ext, far_in, late_in, feat,
    partial, summed, spill_out, spill_in, blocks, deriv_out, derivs, wave_out, waves, cubes,
    half, grad_out, grad_in, fresh_out, fresh, gram, gram_row, gram_sum, gram_sheet, gram_all,
    load, sent, got,
):
    at = place()
    elec, tm = elec_of(at), tm_of(at)
    length = sig.shape[1]
    tiles = length // LANES
    after, before = (tm + 1) & 31, (tm + 31) & 31
    core = at["c"]

    loads = [
        pltpu.make_async_copy(sig_hbm, sig, load.at[0]),
        pltpu.make_async_copy(vec_hbm, vec, load.at[1]),
    ]
    for copy in loads:
        copy.start()
    sems = (sent, got)
    partner = device(moved(at, dict(c=1)))

    def send(src, dst, step, to):
        remote(src, dst, sems, step, to).start()

    def left(step, ref):
        remote(ref, ref, sems, step, partner).wait_send()

    def came(step, ref):
        remote(ref, ref, sems, step, partner).wait_recv()

    barrier = pltpu.get_barrier_semaphore()

    def greet(to):
        pl.semaphore_signal(barrier, inc=1, device_id=to, device_id_type=MESH)

    @pl.when(core == 1)
    def _():
        for move in ELEC + [{}]:
            to = moved(at, move)
            greet({"elec": elec_of(to), "tm": (tm + 30) & 31})
            greet(device(to | dict(c=0)))
            if move:
                greet(device(to))
        for move in PLANE:
            if move["l"]:
                greet(device(moved(at, move)))
        for move in RING:
            greet(device(moved(at, move)))
        greet(device(moved(at, dict(l=1, c=1))))

    @pl.when(core == 0)
    def _():
        greet({"elec": elec, "tm": before})

    lane = lax.broadcasted_iota(jnp.int32, (LAGS, LANES), 1)
    late = lax.broadcasted_iota(jnp.int32, (LAGS, LANES), 0)
    spill = lane < late

    loads[0].wait()

    @pl.loop(0, 16)
    def _(block):
        rows = sig[pl.ds(block * 16, 16), :].astype(F32)
        for r in range(16):
            to = pl.ds((block * 16 + r) * LAGS, LAGS)
            turned = [lagged(rows[r : r + 1, k * LANES : (k + 1) * LANES]) for k in range(tiles)]
            for k, (a, b) in enumerate(zip([0.0] + turned, turned + [0.0])):
                ext[to, k * LANES : (k + 1) * LANES] = jnp.where(spill, a, b).astype(BF16)

    loads[1].wait()
    partial[...] = dot(vec[...], ext[...])
    spill_out[...] = jnp.concatenate([packed(partial[8 * k : 8 * k + 8, length:], 0) for k in range(16)], 0)

    @pl.when(core == 1)
    def _():
        pl.semaphore_wait(barrier, len(ELEC) + 1 + len(PLANE) + len(RING) + 1)

    @pl.when(core == 0)
    def _():
        pl.semaphore_wait(barrier, len(ELEC) + 2)

    onward = (tm + 1 + core) & 31
    for i, move in enumerate(ELEC + [{}]):
        to = moved(at, move) | dict(c=1)
        rows = pl.ds(pl.multiple_of(elec_of(to) * 8, 8), 8)

        def send_sum():
            send(partial.at[rows, pl.ds(0, length)], summed.at[i + 16 * core], SUM, device(to))

        if move:
            send_sum()
        else:
            pl.when(core == 0)(send_sum)
        over = {"elec": elec_of(to), "tm": onward}
        send(spill_out.at[pl.ds(elec_of(to), 1)], spill_in.at[pl.ds(i + 16 * (1 - core), 1)], SPILL, over)
    last = lax.broadcasted_iota(jnp.int32, (8, LANES), 1) >= LANES - LAGS
    ends = sig[:, length - LANES :].astype(F32)
    tail_out[...] = jnp.concatenate(
        [packed(jnp.where(last, ends[8 * k : 8 * k + 8], 0.0), LAGS) for k in range(ends.shape[0] // 8)], 0
    )
    send(tail_out, tail_in, TAIL, {"elec": elec, "tm": after})

    other = moved(at, dict(l=1)) | dict(c=1)
    here = pl.ds(pl.multiple_of(at["l"] * 128, 128), 128)
    there = pl.ds(pl.multiple_of(other["l"] * 128, 128), 128)

    @pl.when(core == 0)
    def _():
        left(SUM, summed.at[pl.ds(0, 16)])
        send(sig.at[here], far_in.at[0], FAR, partner)

    @pl.when(core == 1)
    def _():
        left(SUM, summed.at[pl.ds(0, 15)])

    send(sig.at[there], far_in.at[2 - core], FAR, device(other))
    came(TAIL, tail_in)

    @pl.when((core == 0) & (tm == 0))
    def _():
        tail_in[...] = jnp.zeros_like(tail_in)

    here_ends = pl.ds(pl.multiple_of(at["l"] * 16, 16), 16)
    there_ends = pl.ds(pl.multiple_of(other["l"] * 16, 16), 16)

    @pl.when(core == 0)
    def _():
        send(tail_in.at[here_ends], late_in.at[0], LATE, partner)

    send(tail_in.at[there_ends], late_in.at[2 - core], LATE, device(other))

    def stacked(block):
        return jnp.concatenate([block[:, k * LANES : (k + 1) * LANES] for k in range(tiles)], 0)

    @pl.when(core == 1)
    def _():
        mine = pl.ds(pl.multiple_of(elec * 8, 8), 8)
        lane = lax.broadcasted_iota(jnp.int32, (8, LANES), 1)
        came(SUM, summed)
        came(SPILL, spill_in)
        deriv, cubed = 0.0, []
        for shard in range(2):
            total = summed[15] if shard == 0 else partial[mine, :length]
            for i in range(len(ELEC)):
                total = total + summed[i + 16 * shard]
            over = jnp.sum(spill_in[16 * shard : 16 * shard + 16], axis=0, keepdims=True)
            if shard == 0:
                over = over * jnp.where(tm > 1, 1.0, 0.0)
            over = jnp.concatenate([pltpu.roll(over, (LANES - r * LAGS) % LANES, 1) for r in range(8)], 0)
            over = jnp.where(lane < LAGS, over, 0.0)
            total = jnp.concatenate([total[:, :LANES] + over, total[:, LANES:]], 1)
            deriv = deriv + jnp.sum(3.0 * total * total, axis=1, keepdims=True)
            cubed.append(stacked(total * total * total))
            wave_out[shard] = jnp.concatenate([stacked(total), jnp.zeros((8, LANES), F32)], 0).astype(BF16)
        blocks[elec] = jnp.concatenate(cubed, 0).astype(BF16)
        for move in ELEC:
            send(blocks.at[elec], blocks.at[elec], CUBE, device(moved(at, move)))
        for move in PLANE:
            if move["l"]:
                send(blocks.at[elec], blocks.at[elec + 16], CROSS, device(moved(at, move)))
        deriv = packed(jnp.where(lane == 0, deriv, 0.0), 0)
        deriv_out[0:1] = deriv
        derivs[pl.ds(elec, 1)] = deriv
        for move in PLANE:
            row = pl.ds(elec + 16 * move["l"], 1)
            send(deriv_out.at[pl.ds(0, 1)], derivs.at[row], DERIV, device(moved(at, move)))
        waves[elec] = wave_out[1]

    both = (((1,), (1,)), ((), ()))

    def unpack(part):
        for pair in range(8):
            pieces = [blocks[16 * part + 2 * pair + k].astype(F32) for k in range(2)]
            for c, k in itertools.product(range(2), range(tiles)):
                rows = jnp.concatenate([piece[24 * c + 8 * k : 24 * c + 8 * k + 8] for piece in pieces], 0)
                begin = (2 * part + 1 - c) * length + k * LANES
                cubes[16 * pair : 16 * pair + 16, begin : begin + LANES] = rows.astype(BF16)

    @pl.when(core == 1)
    def _():
        feat[:, :length] = ext[pl.ds(pl.multiple_of(at["l"] * 2048, 2048), 2048), :length]

        @pl.loop(0, 8)
        def _(block):
            ends = tail_in[pl.ds(at["l"] * 16 + block * 2, 2), :]
            for r in range(16):
                to = pl.ds((block * 16 + r) * LAGS, LAGS)
                turned = before_first(ends[r // 8 : r // 8 + 1], r % 8)
                feat[to, :LANES] = jnp.where(spill, turned, feat[to, :LANES].astype(F32)).astype(BF16)

        came(FAR, far_in)
        came(LATE, late_in)
        for i in range(3):

            @pl.loop(0, 8)
            def _(block):
                rows = far_in[i, pl.ds(block * 16, 16), :].astype(F32)
                ends = late_in[i, pl.ds(block * 2, 2), :]
                for r in range(16):
                    to = pl.ds((block * 16 + r) * LAGS, LAGS)
                    turned = [before_first(ends[r // 8 : r // 8 + 1], r % 8)]
                    turned += [lagged(rows[r : r + 1, k * LANES : (k + 1) * LANES]) for k in range(tiles)]
                    for k in range(tiles):
                        begin = (i + 1) * length + k * LANES
                        feat[to, begin : begin + LANES] = jnp.where(spill, turned[k], turned[k + 1]).astype(BF16)

        came(CUBE, blocks.at[pl.ds(0, 15)])
        unpack(0)
        for z in range(8):
            half[z] = dot(cubes[:, : 2 * length], feat[z * 256 : z * 256 + 256, : 2 * length], both)
        came(CROSS, blocks.at[pl.ds(16, 16)])
        unpack(1)
        came(DERIV, derivs.at[pl.ds(0, 31)])
        deriv = derivs[:16] + derivs[16:]
        deriv = jnp.concatenate([jnp.broadcast_to(deriv[k : k + 1], (8, LANES)) for k in range(16)], 0)
        place_of = (lax.broadcasted_iota(jnp.int32, (LANES, LANES), 0) & 7) * LAGS
        lane = lax.broadcasted_iota(jnp.int32, (LANES, LANES), 1)
        deriv = jnp.sum(jnp.where(lane == place_of, deriv, 0.0), axis=1, keepdims=True)

        def block_of(z):
            rows = pl.ds(pl.multiple_of(z * 256, 256), 256)
            columns = pl.ds(pl.multiple_of((at["l"] * 8 + z) * 256, 256), 256)
            grad = half[z] + dot(cubes[:, 2 * length :], feat[rows, 2 * length :], both)
            return grad - deriv * vec[:, columns].astype(F32)

        for i, move in enumerate(RING):
            to = moved(at, move)
            grad_out[i] = block_of(to["z"]).astype(BF16)
            send(grad_out.at[i], grad_in.at[i], GRAD, device(to))
        for move in ELEC + [{}]:
            send(wave_out.at[0], waves.at[elec], WAVE0, device(moved(at, move) | dict(c=0)))
        for move in ELEC:
            send(wave_out.at[1], waves.at[elec], WAVE1, device(moved(at, move)))
        updated = block_of(at["z"])
        came(GRAD, grad_in)
        for i in range(len(RING)):
            updated = updated + grad_in[i].astype(F32)
        updated = updated * (1.0 / (length * 32))
        fresh_out[...] = updated[:, :LANES]
        fresh[...] = updated[:, LANES:]
        gram[...] = fine_gram(updated)

    def gather_sources():
        for pair in range(8):
            pieces = [waves[2 * pair + k].astype(F32) for k in range(2)]
            for k in range(tiles):
                rows = jnp.concatenate([piece[8 * k : 8 * k + 8] for piece in pieces], 0)
                sources[16 * pair : 16 * pair + 16, k * LANES : (k + 1) * LANES] = rows.astype(BF16)

    mine = pl.ds(pl.multiple_of(row_of(at) * 16, 16), 16)

    @pl.when(core == 1)
    def _():
        for i, move in enumerate(ROW):
            to = moved(at, move)
            rows = pl.ds(pl.multiple_of(row_of(to) * 16, 16), 16)
            send(gram.at[rows], gram_row.at[i], GRAM1, device(to))
        send(fresh_out, fresh, FRESH, partner)
        came(WAVE1, waves.at[pl.ds(0, len(ELEC))])
        gather_sources()
        came(GRAM1, gram_row)
        total = gram[mine, :]
        for i in range(len(ROW)):
            total = total + gram_row[i]
        gram_sum[...] = total.astype(BF16)
        for i, move in enumerate(SHEET):
            send(gram_sum, gram_sheet.at[i], GRAM2, device(moved(at, move)))
        came(GRAM2, gram_sheet)
        total = gram_sum[...].astype(F32)
        for i in range(len(SHEET)):
            total = total + gram_sheet[i].astype(F32)
        gram_all[mine, :] = total
        for move in ROW + [{}]:
            send(gram_all.at[mine], gram_all.at[mine], GRAM3, device(moved(at, move) | dict(c=0)))
        for move in ROW:
            send(gram_all.at[mine], gram_all.at[mine], GRAM3, device(moved(at, move)))
        came(GRAM3, gram_all.at[pl.ds(0, 16 * len(ROW))])

    @pl.when(core == 0)
    def _():
        came(WAVE0, waves)
        gather_sources()
        came(FRESH, fresh)
        came(GRAM3, gram_all)

    g = gram_all[...]
    row = lax.broadcasted_iota(jnp.int32, (LANES, LANES), 0)
    column = lax.broadcasted_iota(jnp.int32, (LANES, LANES), 1)
    unit = jnp.where(row == column, 1.0, 0.0)
    squares = jnp.sum(jnp.sum(g * unit, axis=1, keepdims=True), axis=0, keepdims=True)
    scale = START * math.sqrt(LANES) * lax.rsqrt(squares + 1e-06)
    g = g * scale * scale
    current = fresh[...] * scale
    for step in range(NS_STEPS):
        factor = 1.5 * unit - 0.5 * g
        current = fine_dot(factor, current)
        if step < NS_STEPS - 1:
            g = fine_dot(fine_dot(factor, g), factor)
    unmixing[...] = current

    left(TAIL, tail_in)
    left(SPILL, spill_out)

    @pl.when(core == 0)
    def _():
        left(FAR, far_in.at[pl.ds(0, 2)])
        left(LATE, late_in.at[pl.ds(0, 2)])

    @pl.when(core == 1)
    def _():
        left(FAR, far_in.at[0])
        left(LATE, late_in.at[0])
        left(CUBE, blocks.at[pl.ds(0, 15)])
        left(CROSS, blocks.at[pl.ds(0, 16)])
        left(DERIV, derivs.at[pl.ds(0, 31)])
        left(WAVE0, waves)
        left(WAVE1, waves.at[pl.ds(0, len(ELEC))])
        left(GRAD, grad_in)
        left(FRESH, fresh)
        left(GRAM1, gram_row)
        left(GRAM2, gram_sheet)
        left(GRAM3, summed.at[pl.ds(0, 10)])


def shards(signals, vectors):
    channels, length = signals.shape
    count, columns = vectors.shape
    near, ring, row, sheet = (len(group) for group in (ELEC, RING, ROW, SHEET))
    vmem = pl.BlockSpec(memory_space=pltpu.VMEM)
    return pl.pallas_call(
        kernel,
        out_shape=(
            jax.ShapeDtypeStruct((count, length), BF16),
            jax.ShapeDtypeStruct((count, LANES), F32),
        ),
        in_specs=[pl.BlockSpec(memory_space=pltpu.HBM)] * 2,
        out_specs=(vmem, vmem),
        scratch_shapes=[
            pltpu.VMEM((channels, length), BF16),
            pltpu.VMEM((count, columns), BF16),
            pltpu.VMEM((channels // 8, LANES), F32),
            pltpu.VMEM((channels // 8, LANES), F32),
            pltpu.VMEM((columns, length + LANES), BF16),
            pltpu.VMEM((3, channels // 2, length), BF16),
            pltpu.VMEM((3, channels // 16, LANES), F32),
            pltpu.VMEM((columns // 2, 4 * length), BF16),
            pltpu.VMEM((count, length + LANES), F32),
            pltpu.VMEM((2 * near + 1, 8, length), F32),
            pltpu.VMEM((near + 1, LANES), F32),
            pltpu.VMEM((2 * near + 2, LANES), F32),
            pltpu.VMEM((2 * (near + 1), 48, LANES), BF16),
            pltpu.VMEM((8, LANES), F32),
            pltpu.VMEM((2 * (near + 1), LANES), F32),
            pltpu.VMEM((2, 32, LANES), BF16),
            pltpu.VMEM((near + 1, 32, LANES), BF16),
            pltpu.VMEM((count, 4 * length), BF16),
            pltpu.VMEM((8, count, 2 * LANES), F32),
            pltpu.VMEM((ring, count, 2 * LANES), BF16),
            pltpu.VMEM((ring, count, 2 * LANES), BF16),
            pltpu.VMEM((count, LANES), F32),
            pltpu.VMEM((count, LANES), F32),
            pltpu.VMEM((LANES, LANES), F32),
            pltpu.VMEM((row, 16, LANES), F32),
            pltpu.VMEM((16, LANES), BF16),
            pltpu.VMEM((sheet, 16, LANES), BF16),
            pltpu.VMEM((LANES, LANES), F32),
            pltpu.SemaphoreType.DMA((2,)),
            pltpu.SemaphoreType.DMA((15,)),
            pltpu.SemaphoreType.DMA((15,)),
        ],
        compiler_params=pltpu.CompilerParams(
            collective_id=0, has_side_effects=True, vmem_limit_bytes=40 * 2**20
        ),
        cost_estimate=pl.CostEstimate(flops=10**9, bytes_accessed=2 * 10**6, transcendentals=0),
        name="separate",
    )(*[pltpu.with_memory_space_constraint(a, pltpu.HBM) for a in (signals, vectors)])


def solution(mesh):
    return jax.shard_map(
        shards,
        mesh=mesh,
        in_specs=(P("elec", "tm"), P(None, "elec")),
        out_specs=(P(None, "tm"), P(None, ("elec", "tm"))),
        check_vma=False,
    )
```

```python
import functools
import itertools
import math

import jax
import jax.numpy as jnp
from jax import lax
from jax.experimental import pallas as pl
from jax.experimental.pallas import tpu as pltpu
from jax.sharding import PartitionSpec as P

LAGS = 16
NS_STEPS = 6
START = 0.15
MESH = pl.DeviceIdType.MESH
SIZE = dict(x=4, h=4, l=2, z=8, c=2)
F32, BF16 = jnp.float32, jnp.bfloat16
LANES = 128


def hops(move):
    x, y, z = move.get("x", 0), 2 * move.get("h", 0) + move.get("l", 0), move.get("z", 0)
    return min(x, 4 - x) + min(y, 8 - y) + min(z, 8 - z)


def moves(*names):
    every = itertools.product(*[range(SIZE[name]) for name in names])
    found = [dict(zip(names, move)) for move in every if any(move)]
    return sorted(found, key=lambda move: -hops(move))


ELEC, PLANE, RING = moves("x", "h"), moves("x", "h", "l"), moves("z")
ROW, SHEET = moves("x", "l"), moves("z", "h")


def place():
    elec, tm = lax.axis_index("elec"), lax.axis_index("tm")
    return dict(x=elec >> 2, h=elec & 3, l=tm >> 4, z=(tm >> 1) & 7, c=tm & 1)


def moved(at, move):
    return {k: (v + move[k]) & (SIZE[k] - 1) if move.get(k, 0) else v for k, v in at.items()}


def elec_of(at):
    return at["x"] * 4 + at["h"]


def tm_of(at):
    return (at["l"] * 8 + at["z"]) * 2 + at["c"]


def row_of(at):
    return at["x"] * 2 + at["l"]


def device(at):
    return {"elec": elec_of(at), "tm": tm_of(at)}


def remote(src, dst, sems, step, to):
    return pltpu.make_async_remote_copy(
        src_ref=src,
        dst_ref=dst,
        send_sem=sems[0].at[step],
        recv_sem=sems[1].at[step],
        device_id=to,
        device_id_type=MESH,
    )


(TAIL, FAR, LATE, SUM, SPILL, CUBE, CROSS, DERIV, WAVE0, WAVE1, GRAD, FRESH, GRAM1, GRAM2, GRAM3) = range(15)


def halves(a):
    top = a.astype(BF16)
    return top, (a - top.astype(F32)).astype(BF16)


def dot(a, b, dims=(((1,), (0,)), ((), ()))):
    return lax.dot_general(a, b, dims, preferred_element_type=F32)


def fine_dot(a, b):
    (a1, a2), (b1, b2) = halves(a), halves(b)
    return dot(jnp.concatenate([a1, a1, a2], 1), jnp.concatenate([b1, b2, b1], 0))


def fine_gram(a):
    a1, a2 = halves(a)
    both = (((1,), (1,)), ((), ()))
    return dot(jnp.concatenate([a1, a1, a2], 1), jnp.concatenate([a1, a2, a1], 1), both)


def lagged(row, shift=0):
    return pltpu.roll(jnp.broadcast_to(row, (LAGS, LANES)), shift, 1, stride=1, stride_axis=0)


def packed(tile, shift):
    return jnp.sum(pltpu.roll(tile, shift, 1, stride=LAGS, stride_axis=0), axis=0, keepdims=True)


def before_first(row, r):
    return lagged(row, (LANES - (r + 1) * LAGS) % LANES)


def kernel(
    sig_hbm, vec_hbm, sources, unmixing,
    sig, vec, tail_out, tail_in, ext, far_in, late_in, feat,
    partial, summed, spill_out, spill_in, blocks, deriv_out, derivs, wave_out, waves, cubes,
    half, grad_out, grad_in, fresh_out, fresh, gram, gram_row, gram_sum, gram_sheet, gram_all,
    load, sent, got,
):
    at = place()
    elec, tm = elec_of(at), tm_of(at)
    length = sig.shape[1]
    tiles = length // LANES
    after, before = (tm + 1) & 31, (tm + 31) & 31
    core = at["c"]

    loads = [
        pltpu.make_async_copy(sig_hbm, sig, load.at[0]),
        pltpu.make_async_copy(vec_hbm, vec, load.at[1]),
    ]
    for copy in loads:
        copy.start()
    sems = (sent, got)
    partner = device(moved(at, dict(c=1)))

    def send(src, dst, step, to):
        remote(src, dst, sems, step, to).start()

    def left(step, ref):
        remote(ref, ref, sems, step, partner).wait_send()

    def came(step, ref):
        remote(ref, ref, sems, step, partner).wait_recv()

    barrier = pltpu.get_barrier_semaphore()

    def greet(to):
        pl.semaphore_signal(barrier, inc=1, device_id=to, device_id_type=MESH)

    @pl.when(core == 1)
    def _():
        for move in ELEC + [{}]:
            to = moved(at, move)
            greet({"elec": elec_of(to), "tm": (tm + 30) & 31})
            greet(device(to | dict(c=0)))
            if move:
                greet(device(to))
        for move in RING + [dict(l=1)]:
            greet(device(moved(at, move)))
        greet(device(moved(at, dict(l=1, c=1))))

    @pl.when(core == 0)
    def _():
        greet({"elec": elec, "tm": before})

    lane = lax.broadcasted_iota(jnp.int32, (LAGS, LANES), 1)
    late = lax.broadcasted_iota(jnp.int32, (LAGS, LANES), 0)
    spill = lane < late

    loads[0].wait()

    @pl.loop(0, 16)
    def _(block):
        rows = sig[pl.ds(block * 16, 16), :].astype(F32)
        for r in range(16):
            to = pl.ds((block * 16 + r) * LAGS, LAGS)
            turned = [lagged(rows[r : r + 1, k * LANES : (k + 1) * LANES]) for k in range(tiles)]
            for k, (a, b) in enumerate(zip([0.0] + turned, turned + [0.0])):
                ext[to, k * LANES : (k + 1) * LANES] = jnp.where(spill, a, b).astype(BF16)

    loads[1].wait()
    partial[...] = dot(vec[...], ext[...])
    spill_out[...] = jnp.concatenate([packed(partial[8 * k : 8 * k + 8, length:], 0) for k in range(16)], 0)

    @pl.when(core == 1)
    def _():
        pl.semaphore_wait(barrier, 2 * len(ELEC) + len(RING) + 3)

    @pl.when(core == 0)
    def _():
        pl.semaphore_wait(barrier, len(ELEC) + 2)

    onward = (tm + 1 + core) & 31
    for i, move in enumerate(ELEC + [{}]):
        to = moved(at, move) | dict(c=1)
        rows = pl.ds(pl.multiple_of(elec_of(to) * 8, 8), 8)

        def send_sum():
            send(partial.at[rows, pl.ds(0, length)], summed.at[i + 16 * core], SUM, device(to))

        if move:
            send_sum()
        else:
            pl.when(core == 0)(send_sum)
        over = {"elec": elec_of(to), "tm": onward}
        send(spill_out.at[pl.ds(elec_of(to), 1)], spill_in.at[pl.ds(i + 16 * (1 - core), 1)], SPILL, over)
    last = lax.broadcasted_iota(jnp.int32, (8, LANES), 1) >= LANES - LAGS
    ends = sig[:, length - LANES :].astype(F32)
    tail_out[...] = jnp.concatenate(
        [packed(jnp.where(last, ends[8 * k : 8 * k + 8], 0.0), LAGS) for k in range(ends.shape[0] // 8)], 0
    )
    send(tail_out, tail_in, TAIL, {"elec": elec, "tm": after})

    other = moved(at, dict(l=1)) | dict(c=1)
    here = pl.ds(pl.multiple_of(at["l"] * 128, 128), 128)
    there = pl.ds(pl.multiple_of(other["l"] * 128, 128), 128)

    @pl.when(core == 0)
    def _():
        left(SUM, summed.at[pl.ds(0, 16)])
        send(sig.at[here], far_in.at[0], FAR, partner)

    @pl.when(core == 1)
    def _():
        left(SUM, summed.at[pl.ds(0, 15)])

    send(sig.at[there], far_in.at[2 - core], FAR, device(other))
    came(TAIL, tail_in)

    @pl.when((core == 0) & (tm == 0))
    def _():
        tail_in[...] = jnp.zeros_like(tail_in)

    here_ends = pl.ds(pl.multiple_of(at["l"] * 16, 16), 16)
    there_ends = pl.ds(pl.multiple_of(other["l"] * 16, 16), 16)

    @pl.when(core == 0)
    def _():
        send(tail_in.at[here_ends], late_in.at[0], LATE, partner)

    send(tail_in.at[there_ends], late_in.at[2 - core], LATE, device(other))

    def stacked(block):
        return jnp.concatenate([block[:, k * LANES : (k + 1) * LANES] for k in range(tiles)], 0)

    @pl.when(core == 1)
    def _():
        mine = pl.ds(pl.multiple_of(elec * 8, 8), 8)
        lane = lax.broadcasted_iota(jnp.int32, (8, LANES), 1)
        came(FAR, far_in)
        came(SUM, summed)
        came(SPILL, spill_in)
        deriv, cubed = 0.0, []
        for shard in range(2):
            total = summed[15] if shard == 0 else partial[mine, :length]
            for i in range(len(ELEC)):
                total = total + summed[i + 16 * shard]
            over = jnp.sum(spill_in[16 * shard : 16 * shard + 16], axis=0, keepdims=True)
            if shard == 0:
                over = over * jnp.where(tm > 1, 1.0, 0.0)
            over = jnp.concatenate([pltpu.roll(over, (LANES - r * LAGS) % LANES, 1) for r in range(8)], 0)
            over = jnp.where(lane < LAGS, over, 0.0)
            total = jnp.concatenate([total[:, :LANES] + over, total[:, LANES:]], 1)
            deriv = deriv + jnp.sum(3.0 * total * total, axis=1, keepdims=True)
            cubed.append(stacked(total * total * total))
            wave_out[shard] = jnp.concatenate([stacked(total), jnp.zeros((8, LANES), F32)], 0).astype(BF16)
        blocks[elec] = jnp.concatenate(cubed, 0).astype(BF16)
        for move in ELEC:
            send(blocks.at[elec], blocks.at[elec], CUBE, device(moved(at, move)))
        for move in PLANE:
            if move["l"]:
                send(blocks.at[elec], blocks.at[elec + 16], CROSS, device(moved(at, move)))
        deriv = packed(jnp.where(lane == 0, deriv, 0.0), 0)
        deriv_out[0:1] = deriv
        derivs[pl.ds(elec, 1)] = deriv
        for move in PLANE:
            row = pl.ds(elec + 16 * move["l"], 1)
            send(deriv_out.at[pl.ds(0, 1)], derivs.at[row], DERIV, device(moved(at, move)))
        waves[elec] = wave_out[1]

    both = (((1,), (1,)), ((), ()))

    def unpack(part):
        for pair in range(8):
            pieces = [blocks[16 * part + 2 * pair + k].astype(F32) for k in range(2)]
            for c, k in itertools.product(range(2), range(tiles)):
                rows = jnp.concatenate([piece[24 * c + 8 * k : 24 * c + 8 * k + 8] for piece in pieces], 0)
                begin = (2 * part + 1 - c) * length + k * LANES
                cubes[16 * pair : 16 * pair + 16, begin : begin + LANES] = rows.astype(BF16)

    @pl.when(core == 1)
    def _():
        feat[:, :length] = ext[pl.ds(pl.multiple_of(at["l"] * 2048, 2048), 2048), :length]

        @pl.loop(0, 8)
        def _(block):
            ends = tail_in[pl.ds(at["l"] * 16 + block * 2, 2), :]
            for r in range(16):
                to = pl.ds((block * 16 + r) * LAGS, LAGS)
                turned = before_first(ends[r // 8 : r // 8 + 1], r % 8)
                feat[to, :LANES] = jnp.where(spill, turned, feat[to, :LANES].astype(F32)).astype(BF16)

        came(LATE, late_in)
        for i in range(3):

            @pl.loop(0, 8)
            def _(block):
                rows = far_in[i, pl.ds(block * 16, 16), :].astype(F32)
                ends = late_in[i, pl.ds(block * 2, 2), :]
                for r in range(16):
                    to = pl.ds((block * 16 + r) * LAGS, LAGS)
                    turned = [before_first(ends[r // 8 : r // 8 + 1], r % 8)]
                    turned += [lagged(rows[r : r + 1, k * LANES : (k + 1) * LANES]) for k in range(tiles)]
                    for k in range(tiles):
                        begin = (i + 1) * length + k * LANES
                        feat[to, begin : begin + LANES] = jnp.where(spill, turned[k], turned[k + 1]).astype(BF16)

        came(CUBE, blocks.at[pl.ds(0, 15)])
        unpack(0)
        for z in range(8):
            half[z] = dot(cubes[:, : 2 * length], feat[z * 256 : z * 256 + 256, : 2 * length], both)
        came(CROSS, blocks.at[pl.ds(16, 16)])
        unpack(1)
        came(DERIV, derivs.at[pl.ds(0, 31)])
        deriv = derivs[:16] + derivs[16:]
        deriv = jnp.concatenate([jnp.broadcast_to(deriv[k : k + 1], (8, LANES)) for k in range(16)], 0)
        place_of = (lax.broadcasted_iota(jnp.int32, (LANES, LANES), 0) & 7) * LAGS
        lane = lax.broadcasted_iota(jnp.int32, (LANES, LANES), 1)
        deriv = jnp.sum(jnp.where(lane == place_of, deriv, 0.0), axis=1, keepdims=True)

        def block_of(z):
            rows = pl.ds(pl.multiple_of(z * 256, 256), 256)
            columns = pl.ds(pl.multiple_of((at["l"] * 8 + z) * 256, 256), 256)
            grad = half[z] + dot(cubes[:, 2 * length :], feat[rows, 2 * length :], both)
            return grad - deriv * vec[:, columns].astype(F32)

        for i, move in enumerate(RING):
            to = moved(at, move)
            grad_out[i] = block_of(to["z"]).astype(BF16)
            send(grad_out.at[i], grad_in.at[i], GRAD, device(to))
        for move in ELEC + [{}]:
            send(wave_out.at[0], waves.at[elec], WAVE0, device(moved(at, move) | dict(c=0)))
        for move in ELEC:
            send(wave_out.at[1], waves.at[elec], WAVE1, device(moved(at, move)))
        updated = block_of(at["z"])
        came(GRAD, grad_in)
        for i in range(len(RING)):
            updated = updated + grad_in[i].astype(F32)
        updated = updated * (1.0 / (length * 32))
        fresh_out[...] = updated[:, :LANES]
        fresh[...] = updated[:, LANES:]
        gram[...] = fine_gram(updated)

    def gather_sources():
        for pair in range(8):
            pieces = [waves[2 * pair + k].astype(F32) for k in range(2)]
            for k in range(tiles):
                rows = jnp.concatenate([piece[8 * k : 8 * k + 8] for piece in pieces], 0)
                sources[16 * pair : 16 * pair + 16, k * LANES : (k + 1) * LANES] = rows.astype(BF16)

    mine = pl.ds(pl.multiple_of(row_of(at) * 16, 16), 16)

    @pl.when(core == 1)
    def _():
        for i, move in enumerate(ROW):
            to = moved(at, move)
            rows = pl.ds(pl.multiple_of(row_of(to) * 16, 16), 16)
            send(gram.at[rows], gram_row.at[i], GRAM1, device(to))
        send(fresh_out, fresh, FRESH, partner)
        came(WAVE1, waves.at[pl.ds(0, len(ELEC))])
        gather_sources()
        came(GRAM1, gram_row)
        total = gram[mine, :]
        for i in range(len(ROW)):
            total = total + gram_row[i]
        gram_sum[...] = total.astype(BF16)
        for i, move in enumerate(SHEET):
            send(gram_sum, gram_sheet.at[i], GRAM2, device(moved(at, move)))
        came(GRAM2, gram_sheet)
        total = gram_sum[...].astype(F32)
        for i in range(len(SHEET)):
            total = total + gram_sheet[i].astype(F32)
        gram_all[mine, :] = total
        for move in ROW + [{}]:
            send(gram_all.at[mine], gram_all.at[mine], GRAM3, device(moved(at, move) | dict(c=0)))
        for move in ROW:
            send(gram_all.at[mine], gram_all.at[mine], GRAM3, device(moved(at, move)))
        came(GRAM3, gram_all.at[pl.ds(0, 16 * len(ROW))])

    @pl.when(core == 0)
    def _():
        came(WAVE0, waves)
        gather_sources()
        came(FRESH, fresh)
        came(GRAM3, gram_all)

    g = gram_all[...]
    row = lax.broadcasted_iota(jnp.int32, (LANES, LANES), 0)
    column = lax.broadcasted_iota(jnp.int32, (LANES, LANES), 1)
    unit = jnp.where(row == column, 1.0, 0.0)
    squares = jnp.sum(jnp.sum(g * unit, axis=1, keepdims=True), axis=0, keepdims=True)
    scale = START * math.sqrt(LANES) * lax.rsqrt(squares + 1e-06)
    g = g * scale * scale
    current = fresh[...] * scale
    for step in range(NS_STEPS):
        factor = 1.5 * unit - 0.5 * g
        current = fine_dot(factor, current)
        if step < NS_STEPS - 1:
            g = fine_dot(fine_dot(factor, g), factor)
    unmixing[...] = current

    left(TAIL, tail_in)
    left(SPILL, spill_out)

    @pl.when(core == 0)
    def _():
        left(FAR, far_in.at[pl.ds(0, 2)])
        left(LATE, late_in.at[pl.ds(0, 2)])

    @pl.when(core == 1)
    def _():
        left(FAR, far_in.at[0])
        left(LATE, late_in.at[0])
        left(CUBE, blocks.at[pl.ds(0, 15)])
        left(CROSS, blocks.at[pl.ds(0, 16)])
        left(DERIV, derivs.at[pl.ds(0, 31)])
        left(WAVE0, waves)
        left(WAVE1, waves.at[pl.ds(0, len(ELEC))])
        left(GRAD, grad_in)
        left(FRESH, fresh)
        left(GRAM1, gram_row)
        left(GRAM2, gram_sheet)
        left(GRAM3, summed.at[pl.ds(0, 10)])


def shards(signals, vectors):
    channels, length = signals.shape
    count, columns = vectors.shape
    near, ring, row, sheet = (len(group) for group in (ELEC, RING, ROW, SHEET))
    vmem = pl.BlockSpec(memory_space=pltpu.VMEM)
    return pl.pallas_call(
        kernel,
        out_shape=(
            jax.ShapeDtypeStruct((count, length), BF16),
            jax.ShapeDtypeStruct((count, LANES), F32),
        ),
        in_specs=[pl.BlockSpec(memory_space=pltpu.HBM)] * 2,
        out_specs=(vmem, vmem),
        scratch_shapes=[
            pltpu.VMEM((channels, length), BF16),
            pltpu.VMEM((count, columns), BF16),
            pltpu.VMEM((channels // 8, LANES), F32),
            pltpu.VMEM((channels // 8, LANES), F32),
            pltpu.VMEM((columns, length + LANES), BF16),
            pltpu.VMEM((3, channels // 2, length), BF16),
            pltpu.VMEM((3, channels // 16, LANES), F32),
            pltpu.VMEM((columns // 2, 4 * length), BF16),
            pltpu.VMEM((count, length + LANES), F32),
            pltpu.VMEM((2 * near + 1, 8, length), F32),
            pltpu.VMEM((near + 1, LANES), F32),
            pltpu.VMEM((2 * near + 2, LANES), F32),
            pltpu.VMEM((2 * (near + 1), 48, LANES), BF16),
            pltpu.VMEM((8, LANES), F32),
            pltpu.VMEM((2 * (near + 1), LANES), F32),
            pltpu.VMEM((2, 32, LANES), BF16),
            pltpu.VMEM((near + 1, 32, LANES), BF16),
            pltpu.VMEM((count, 4 * length), BF16),
            pltpu.VMEM((8, count, 2 * LANES), F32),
            pltpu.VMEM((ring, count, 2 * LANES), BF16),
            pltpu.VMEM((ring, count, 2 * LANES), BF16),
            pltpu.VMEM((count, LANES), F32),
            pltpu.VMEM((count, LANES), F32),
            pltpu.VMEM((LANES, LANES), F32),
            pltpu.VMEM((row, 16, LANES), F32),
            pltpu.VMEM((16, LANES), BF16),
            pltpu.VMEM((sheet, 16, LANES), BF16),
            pltpu.VMEM((LANES, LANES), F32),
            pltpu.SemaphoreType.DMA((2,)),
            pltpu.SemaphoreType.DMA((15,)),
            pltpu.SemaphoreType.DMA((15,)),
        ],
        compiler_params=pltpu.CompilerParams(
            collective_id=0, has_side_effects=True, vmem_limit_bytes=40 * 2**20
        ),
        cost_estimate=pl.CostEstimate(flops=10**9, bytes_accessed=2 * 10**6, transcendentals=0),
        name="separate",
    )(*[pltpu.with_memory_space_constraint(a, pltpu.HBM) for a in (signals, vectors)])


def solution(mesh):
    return jax.shard_map(
        shards,
        mesh=mesh,
        in_specs=(P("elec", "tm"), P(None, "elec")),
        out_specs=(P(None, "tm"), P(None, ("elec", "tm"))),
        check_vma=False,
    )
```

```python
import functools
import itertools
import math

import jax
import jax.numpy as jnp
from jax import lax
from jax.experimental import pallas as pl
from jax.experimental.pallas import tpu as pltpu
from jax.sharding import PartitionSpec as P

LAGS = 16
NS_STEPS = 6
START = 0.15
MESH = pl.DeviceIdType.MESH
SIZE = dict(x=4, h=4, l=2, z=8, c=2)
F32, BF16 = jnp.float32, jnp.bfloat16
LANES = 128


def hops(move):
    x, y, z = move.get("x", 0), 2 * move.get("h", 0) + move.get("l", 0), move.get("z", 0)
    return min(x, 4 - x) + min(y, 8 - y) + min(z, 8 - z)


def moves(*names):
    every = itertools.product(*[range(SIZE[name]) for name in names])
    found = [dict(zip(names, move)) for move in every if any(move)]
    return sorted(found, key=lambda move: -hops(move))


ELEC, PLANE, RING = moves("x", "h"), moves("x", "h", "l"), moves("z")
ROW, SHEET = moves("x", "l"), moves("z", "h")


def place():
    elec, tm = lax.axis_index("elec"), lax.axis_index("tm")
    return dict(x=elec >> 2, h=elec & 3, l=tm >> 4, z=(tm >> 1) & 7, c=tm & 1)


def moved(at, move):
    return {k: (v + move[k]) & (SIZE[k] - 1) if move.get(k, 0) else v for k, v in at.items()}


def elec_of(at):
    return at["x"] * 4 + at["h"]


def tm_of(at):
    return (at["l"] * 8 + at["z"]) * 2 + at["c"]


def row_of(at):
    return at["x"] * 2 + at["l"]


def device(at):
    return {"elec": elec_of(at), "tm": tm_of(at)}


def remote(src, dst, sems, step, to):
    return pltpu.make_async_remote_copy(
        src_ref=src,
        dst_ref=dst,
        send_sem=sems[0].at[step],
        recv_sem=sems[1].at[step],
        device_id=to,
        device_id_type=MESH,
    )


(TAIL, FAR, LATE, SUM, SPILL, CUBE, CROSS, DERIV, WAVE0, WAVE1, GRAD, FRESH, GRAM1, GRAM2, GRAM3) = range(15)


def halves(a):
    top = a.astype(BF16)
    return top, (a - top.astype(F32)).astype(BF16)


def dot(a, b, dims=(((1,), (0,)), ((), ()))):
    return lax.dot_general(a, b, dims, preferred_element_type=F32)


def fine_dot(a, b):
    (a1, a2), (b1, b2) = halves(a), halves(b)
    return dot(jnp.concatenate([a1, a1, a2], 1), jnp.concatenate([b1, b2, b1], 0))


def fine_gram(a):
    a1, a2 = halves(a)
    both = (((1,), (1,)), ((), ()))
    return dot(jnp.concatenate([a1, a1, a2], 1), jnp.concatenate([a1, a2, a1], 1), both)


def lagged(row, shift=0):
    return pltpu.roll(jnp.broadcast_to(row, (LAGS, LANES)), shift, 1, stride=1, stride_axis=0)


def packed(tile, shift):
    return jnp.sum(pltpu.roll(tile, shift, 1, stride=LAGS, stride_axis=0), axis=0, keepdims=True)


def before_first(row, r):
    return lagged(row, (LANES - (r + 1) * LAGS) % LANES)


def kernel(
    sig_hbm, vec_hbm, sources, unmixing,
    sig, vec, tail_out, tail_in, ext, far_in, late_in, feat,
    partial, summed, spill_out, spill_in, blocks, deriv_out, derivs, wave_out, waves, cubes,
    half, grad_out, grad_in, fresh_out, fresh, gram, gram_row, gram_sum, gram_sheet, gram_all,
    load, sent, got,
):
    at = place()
    elec, tm = elec_of(at), tm_of(at)
    length = sig.shape[1]
    tiles = length // LANES
    after, before = (tm + 1) & 31, (tm + 31) & 31
    core = at["c"]

    loads = [
        pltpu.make_async_copy(sig_hbm, sig, load.at[0]),
        pltpu.make_async_copy(vec_hbm, vec, load.at[1]),
    ]
    for copy in loads:
        copy.start()
    sems = (sent, got)
    partner = device(moved(at, dict(c=1)))

    def send(src, dst, step, to):
        remote(src, dst, sems, step, to).start()

    def left(step, ref):
        remote(ref, ref, sems, step, partner).wait_send()

    def came(step, ref):
        remote(ref, ref, sems, step, partner).wait_recv()

    barrier = pltpu.get_barrier_semaphore()

    def greet(to):
        pl.semaphore_signal(barrier, inc=1, device_id=to, device_id_type=MESH)

    @pl.when(core == 1)
    def _():
        for move in ELEC + [{}]:
            to = moved(at, move)
            greet({"elec": elec_of(to), "tm": (tm + 30) & 31})
            greet(device(to | dict(c=0)))
            if move:
                greet(device(to))
        for move in PLANE:
            if move["l"]:
                greet(device(moved(at, move)))
        for move in RING:
            greet(device(moved(at, move)))
        greet(device(moved(at, dict(l=1, c=1))))

    @pl.when(core == 0)
    def _():
        greet({"elec": elec, "tm": before})

    lane = lax.broadcasted_iota(jnp.int32, (LAGS, LANES), 1)
    late = lax.broadcasted_iota(jnp.int32, (LAGS, LANES), 0)
    spill = lane < late

    loads[0].wait()

    @pl.loop(0, 8)
    def _(block):
        rows = sig[pl.ds(block * 32, 32), :].astype(F32)
        for r in range(32):
            to = pl.ds((block * 32 + r) * LAGS, LAGS)
            turned = [lagged(rows[r : r + 1, k * LANES : (k + 1) * LANES]) for k in range(tiles)]
            for k, (a, b) in enumerate(zip([0.0] + turned, turned + [0.0])):
                ext[to, k * LANES : (k + 1) * LANES] = jnp.where(spill, a, b).astype(BF16)

    loads[1].wait()
    partial[...] = dot(vec[...], ext[...])
    spill_out[...] = jnp.concatenate([packed(partial[8 * k : 8 * k + 8, length:], 0) for k in range(16)], 0)

    @pl.when(core == 1)
    def _():
        pl.semaphore_wait(barrier, len(ELEC) + 1 + len(PLANE) + len(RING) + 1)

    @pl.when(core == 0)
    def _():
        pl.semaphore_wait(barrier, len(ELEC) + 2)

    onward = (tm + 1 + core) & 31
    for i, move in enumerate(ELEC + [{}]):
        to = moved(at, move) | dict(c=1)
        rows = pl.ds(pl.multiple_of(elec_of(to) * 8, 8), 8)

        def send_sum():
            send(partial.at[rows, pl.ds(0, length)], summed.at[i + 16 * core], SUM, device(to))

        if move:
            send_sum()
        else:
            pl.when(core == 0)(send_sum)
        over = {"elec": elec_of(to), "tm": onward}
        send(spill_out.at[pl.ds(elec_of(to), 1)], spill_in.at[pl.ds(i + 16 * (1 - core), 1)], SPILL, over)
    last = lax.broadcasted_iota(jnp.int32, (8, LANES), 1) >= LANES - LAGS
    ends = sig[:, length - LANES :].astype(F32)
    tail_out[...] = jnp.concatenate(
        [packed(jnp.where(last, ends[8 * k : 8 * k + 8], 0.0), LAGS) for k in range(ends.shape[0] // 8)], 0
    )
    send(tail_out, tail_in, TAIL, {"elec": elec, "tm": after})

    other = moved(at, dict(l=1)) | dict(c=1)
    here = pl.ds(pl.multiple_of(at["l"] * 128, 128), 128)
    there = pl.ds(pl.multiple_of(other["l"] * 128, 128), 128)

    @pl.when(core == 0)
    def _():
        left(SUM, summed.at[pl.ds(0, 16)])
        send(sig.at[here], far_in.at[0], FAR, partner)

    @pl.when(core == 1)
    def _():
        left(SUM, summed.at[pl.ds(0, 15)])

    send(sig.at[there], far_in.at[2 - core], FAR, device(other))
    came(TAIL, tail_in)

    @pl.when((core == 0) & (tm == 0))
    def _():
        tail_in[...] = jnp.zeros_like(tail_in)

    here_ends = pl.ds(pl.multiple_of(at["l"] * 16, 16), 16)
    there_ends = pl.ds(pl.multiple_of(other["l"] * 16, 16), 16)

    @pl.when(core == 0)
    def _():
        send(tail_in.at[here_ends], late_in.at[0], LATE, partner)

    send(tail_in.at[there_ends], late_in.at[2 - core], LATE, device(other))

    def stacked(block):
        return jnp.concatenate([block[:, k * LANES : (k + 1) * LANES] for k in range(tiles)], 0)

    @pl.when(core == 1)
    def _():
        mine = pl.ds(pl.multiple_of(elec * 8, 8), 8)
        lane = lax.broadcasted_iota(jnp.int32, (8, LANES), 1)
        came(SUM, summed)
        came(SPILL, spill_in)
        deriv, cubed = 0.0, []
        for shard in range(2):
            total = summed[15] if shard == 0 else partial[mine, :length]
            for i in range(len(ELEC)):
                total = total + summed[i + 16 * shard]
            over = jnp.sum(spill_in[16 * shard : 16 * shard + 16], axis=0, keepdims=True)
            if shard == 0:
                over = over * jnp.where(tm > 1, 1.0, 0.0)
            over = jnp.concatenate([pltpu.roll(over, (LANES - r * LAGS) % LANES, 1) for r in range(8)], 0)
            over = jnp.where(lane < LAGS, over, 0.0)
            total = jnp.concatenate([total[:, :LANES] + over, total[:, LANES:]], 1)
            deriv = deriv + jnp.sum(3.0 * total * total, axis=1, keepdims=True)
            cubed.append(stacked(total * total * total))
            wave_out[shard] = jnp.concatenate([stacked(total), jnp.zeros((8, LANES), F32)], 0).astype(BF16)
        blocks[elec] = jnp.concatenate(cubed, 0).astype(BF16)
        for move in ELEC:
            send(blocks.at[elec], blocks.at[elec], CUBE, device(moved(at, move)))
        for move in PLANE:
            if move["l"]:
                send(blocks.at[elec], blocks.at[elec + 16], CROSS, device(moved(at, move)))
        deriv = packed(jnp.where(lane == 0, deriv, 0.0), 0)
        deriv_out[0:1] = deriv
        derivs[pl.ds(elec, 1)] = deriv
        for move in PLANE:
            row = pl.ds(elec + 16 * move["l"], 1)
            send(deriv_out.at[pl.ds(0, 1)], derivs.at[row], DERIV, device(moved(at, move)))
        waves[elec] = wave_out[1]

    both = (((1,), (1,)), ((), ()))

    def unpack(part):
        for pair in range(8):
            pieces = [blocks[16 * part + 2 * pair + k].astype(F32) for k in range(2)]
            for c, k in itertools.product(range(2), range(tiles)):
                rows = jnp.concatenate([piece[24 * c + 8 * k : 24 * c + 8 * k + 8] for piece in pieces], 0)
                begin = (2 * part + 1 - c) * length + k * LANES
                cubes[16 * pair : 16 * pair + 16, begin : begin + LANES] = rows.astype(BF16)

    @pl.when(core == 1)
    def _():
        feat[:, :length] = ext[pl.ds(pl.multiple_of(at["l"] * 2048, 2048), 2048), :length]

        @pl.loop(0, 8)
        def _(block):
            ends = tail_in[pl.ds(at["l"] * 16 + block * 2, 2), :]
            for r in range(16):
                to = pl.ds((block * 16 + r) * LAGS, LAGS)
                turned = before_first(ends[r // 8 : r // 8 + 1], r % 8)
                feat[to, :LANES] = jnp.where(spill, turned, feat[to, :LANES].astype(F32)).astype(BF16)

        came(FAR, far_in)
        came(LATE, late_in)
        for i in range(3):

            @pl.loop(0, 4)
            def _(block):
                rows = far_in[i, pl.ds(block * 32, 32), :].astype(F32)
                ends = late_in[i, pl.ds(block * 4, 4), :]
                for r in range(32):
                    to = pl.ds((block * 32 + r) * LAGS, LAGS)
                    turned = [before_first(ends[r // 8 : r // 8 + 1], r % 8)]
                    turned += [lagged(rows[r : r + 1, k * LANES : (k + 1) * LANES]) for k in range(tiles)]
                    for k in range(tiles):
                        begin = (i + 1) * length + k * LANES
                        feat[to, begin : begin + LANES] = jnp.where(spill, turned[k], turned[k + 1]).astype(BF16)

        came(CUBE, blocks.at[pl.ds(0, 15)])
        unpack(0)
        for z in range(8):
            half[z] = dot(cubes[:, : 2 * length], feat[z * 256 : z * 256 + 256, : 2 * length], both)
        came(CROSS, blocks.at[pl.ds(16, 16)])
        unpack(1)
        came(DERIV, derivs.at[pl.ds(0, 31)])
        deriv = derivs[:16] + derivs[16:]
        deriv = jnp.concatenate([jnp.broadcast_to(deriv[k : k + 1], (8, LANES)) for k in range(16)], 0)
        place_of = (lax.broadcasted_iota(jnp.int32, (LANES, LANES), 0) & 7) * LAGS
        lane = lax.broadcasted_iota(jnp.int32, (LANES, LANES), 1)
        deriv = jnp.sum(jnp.where(lane == place_of, deriv, 0.0), axis=1, keepdims=True)

        def block_of(z):
            rows = pl.ds(pl.multiple_of(z * 256, 256), 256)
            columns = pl.ds(pl.multiple_of((at["l"] * 8 + z) * 256, 256), 256)
            grad = half[z] + dot(cubes[:, 2 * length :], feat[rows, 2 * length :], both)
            return grad - deriv * vec[:, columns].astype(F32)

        for i, move in enumerate(RING):
            to = moved(at, move)
            grad_out[i] = block_of(to["z"]).astype(BF16)
            send(grad_out.at[i], grad_in.at[i], GRAD, device(to))
        for move in ELEC + [{}]:
            send(wave_out.at[0], waves.at[elec], WAVE0, device(moved(at, move) | dict(c=0)))
        for move in ELEC:
            send(wave_out.at[1], waves.at[elec], WAVE1, device(moved(at, move)))
        updated = block_of(at["z"])
        came(GRAD, grad_in)
        for i in range(len(RING)):
            updated = updated + grad_in[i].astype(F32)
        updated = updated * (1.0 / (length * 32))
        fresh_out[...] = updated[:, :LANES]
        fresh[...] = updated[:, LANES:]
        gram[...] = fine_gram(updated)

    def gather_sources():
        for pair in range(8):
            pieces = [waves[2 * pair + k].astype(F32) for k in range(2)]
            for k in range(tiles):
                rows = jnp.concatenate([piece[8 * k : 8 * k + 8] for piece in pieces], 0)
                sources[16 * pair : 16 * pair + 16, k * LANES : (k + 1) * LANES] = rows.astype(BF16)

    mine = pl.ds(pl.multiple_of(row_of(at) * 16, 16), 16)

    @pl.when(core == 1)
    def _():
        for i, move in enumerate(ROW):
            to = moved(at, move)
            rows = pl.ds(pl.multiple_of(row_of(to) * 16, 16), 16)
            send(gram.at[rows], gram_row.at[i], GRAM1, device(to))
        send(fresh_out, fresh, FRESH, partner)
        came(WAVE1, waves.at[pl.ds(0, len(ELEC))])
        gather_sources()
        came(GRAM1, gram_row)
        total = gram[mine, :]
        for i in range(len(ROW)):
            total = total + gram_row[i]
        gram_sum[...] = total.astype(BF16)
        for i, move in enumerate(SHEET):
            send(gram_sum, gram_sheet.at[i], GRAM2, device(moved(at, move)))
        came(GRAM2, gram_sheet)
        total = gram_sum[...].astype(F32)
        for i in range(len(SHEET)):
            total = total + gram_sheet[i].astype(F32)
        gram_all[mine, :] = total
        for move in ROW + [{}]:
            send(gram_all.at[mine], gram_all.at[mine], GRAM3, device(moved(at, move) | dict(c=0)))
        for move in ROW:
            send(gram_all.at[mine], gram_all.at[mine], GRAM3, device(moved(at, move)))
        came(GRAM3, gram_all.at[pl.ds(0, 16 * len(ROW))])

    @pl.when(core == 0)
    def _():
        came(WAVE0, waves)
        gather_sources()
        came(FRESH, fresh)
        came(GRAM3, gram_all)

    g = gram_all[...]
    row = lax.broadcasted_iota(jnp.int32, (LANES, LANES), 0)
    column = lax.broadcasted_iota(jnp.int32, (LANES, LANES), 1)
    unit = jnp.where(row == column, 1.0, 0.0)
    squares = jnp.sum(jnp.sum(g * unit, axis=1, keepdims=True), axis=0, keepdims=True)
    scale = START * math.sqrt(LANES) * lax.rsqrt(squares + 1e-06)
    g = g * scale * scale
    current = fresh[...] * scale
    for step in range(NS_STEPS):
        factor = 1.5 * unit - 0.5 * g
        current = fine_dot(factor, current)
        if step < NS_STEPS - 1:
            g = fine_dot(fine_dot(factor, g), factor)
    unmixing[...] = current

    left(TAIL, tail_in)
    left(SPILL, spill_out)

    @pl.when(core == 0)
    def _():
        left(FAR, far_in.at[pl.ds(0, 2)])
        left(LATE, late_in.at[pl.ds(0, 2)])

    @pl.when(core == 1)
    def _():
        left(FAR, far_in.at[0])
        left(LATE, late_in.at[0])
        left(CUBE, blocks.at[pl.ds(0, 15)])
        left(CROSS, blocks.at[pl.ds(0, 16)])
        left(DERIV, derivs.at[pl.ds(0, 31)])
        left(WAVE0, waves)
        left(WAVE1, waves.at[pl.ds(0, len(ELEC))])
        left(GRAD, grad_in)
        left(FRESH, fresh)
        left(GRAM1, gram_row)
        left(GRAM2, gram_sheet)
        left(GRAM3, summed.at[pl.ds(0, 10)])


def shards(signals, vectors):
    channels, length = signals.shape
    count, columns = vectors.shape
    near, ring, row, sheet = (len(group) for group in (ELEC, RING, ROW, SHEET))
    vmem = pl.BlockSpec(memory_space=pltpu.VMEM)
    return pl.pallas_call(
        kernel,
        out_shape=(
            jax.ShapeDtypeStruct((count, length), BF16),
            jax.ShapeDtypeStruct((count, LANES), F32),
        ),
        in_specs=[pl.BlockSpec(memory_space=pltpu.HBM)] * 2,
        out_specs=(vmem, vmem),
        scratch_shapes=[
            pltpu.VMEM((channels, length), BF16),
            pltpu.VMEM((count, columns), BF16),
            pltpu.VMEM((channels // 8, LANES), F32),
            pltpu.VMEM((channels // 8, LANES), F32),
            pltpu.VMEM((columns, length + LANES), BF16),
            pltpu.VMEM((3, channels // 2, length), BF16),
            pltpu.VMEM((3, channels // 16, LANES), F32),
            pltpu.VMEM((columns // 2, 4 * length), BF16),
            pltpu.VMEM((count, length + LANES), F32),
            pltpu.VMEM((2 * near + 1, 8, length), F32),
            pltpu.VMEM((near + 1, LANES), F32),
            pltpu.VMEM((2 * near + 2, LANES), F32),
            pltpu.VMEM((2 * (near + 1), 48, LANES), BF16),
            pltpu.VMEM((8, LANES), F32),
            pltpu.VMEM((2 * (near + 1), LANES), F32),
            pltpu.VMEM((2, 32, LANES), BF16),
            pltpu.VMEM((near + 1, 32, LANES), BF16),
            pltpu.VMEM((count, 4 * length), BF16),
            pltpu.VMEM((8, count, 2 * LANES), F32),
            pltpu.VMEM((ring, count, 2 * LANES), BF16),
            pltpu.VMEM((ring, count, 2 * LANES), BF16),
            pltpu.VMEM((count, LANES), F32),
            pltpu.VMEM((count, LANES), F32),
            pltpu.VMEM((LANES, LANES), F32),
            pltpu.VMEM((row, 16, LANES), F32),
            pltpu.VMEM((16, LANES), BF16),
            pltpu.VMEM((sheet, 16, LANES), BF16),
            pltpu.VMEM((LANES, LANES), F32),
            pltpu.SemaphoreType.DMA((2,)),
            pltpu.SemaphoreType.DMA((15,)),
            pltpu.SemaphoreType.DMA((15,)),
        ],
        compiler_params=pltpu.CompilerParams(
            collective_id=0, has_side_effects=True, vmem_limit_bytes=40 * 2**20
        ),
        cost_estimate=pl.CostEstimate(flops=10**9, bytes_accessed=2 * 10**6, transcendentals=0),
        name="separate",
    )(*[pltpu.with_memory_space_constraint(a, pltpu.HBM) for a in (signals, vectors)])


def solution(mesh):
    return jax.shard_map(
        shards,
        mesh=mesh,
        in_specs=(P("elec", "tm"), P(None, "elec")),
        out_specs=(P(None, "tm"), P(None, ("elec", "tm"))),
        check_vma=False,
    )
```
